32 devices in a mesh: section: 2 (over x), tensor: 4 (over y, core), dp: 4 (over z).
Axes of the slice: x: 2, y: 2, z: 4, core: 2. Of those that a mesh axis runs over, the one named last changes fastest.
Arguments:
- inputs: bfloat16 [8, 2048, 1024], P('dp', 'tensor'), may hold values from -6 to 6
- cotangent: bfloat16 [8, 2048, 1024], P('dp', 'tensor'), may hold values from -6 to 6
- lengths: int32 [8, 8], P('dp'), may hold values from 0 to 2048, as said below
- qkv_weight: bfloat16 [2, 1024, 3, 1024], P('section', 'dp', None, 'tensor'), may hold values from -0.1875 to 0.1875
- qkv_bias: bfloat16 [2, 3, 1024], P('section', None, ('tensor', 'dp')), may hold values from -3 to 3
- dense_weight: bfloat16 [2, 1024, 1024], P('section', 'tensor', 'dp'), may hold values from -0.5 to 0.5
- in_weight: bfloat16 [2, 1024, 4096], P('section', 'dp', 'tensor'), may hold values from -0.1875 to 0.1875
- in_bias: bfloat16 [2, 4096], P('section', ('tensor', 'dp')), may hold values from -3 to 3
- out_weight: bfloat16 [2, 4096, 1024], P('section', 'tensor', 'dp'), may hold values from -0.09375 to 0.09375
- norm_gains: bfloat16 [2, 2, 1024], P('section', None, ('tensor', 'dp')), may hold values from 0.25 to 1.75
- norm_biases: bfloat16 [2, 2, 1024], P('section', None, ('tensor', 'dp')), may hold values from -2 to 2
- out_biases: bfloat16 [2, 2, 1024], P('section', None, ('tensor', 'dp')), may hold values from -3 to 3
Outputs:
- activations: bfloat16 [2, 8, 2048, 1024], P('section', 'dp', 'tensor')
- input_grads: float32 [2, 8, 2048, 1024], P('section', 'dp', 'tensor')
- qkv_weight_grad: float32 [2, 1024, 3, 1024], P('section', 'dp', None, 'tensor')
- qkv_bias_grad: float32 [2, 3, 1024], P('section', None, ('tensor', 'dp'))
- dense_weight_grad: float32 [2, 1024, 1024], P('section', 'tensor', 'dp')
- in_weight_grad: float32 [2, 1024, 4096], P('section', 'dp', 'tensor')
- in_bias_grad: float32 [2, 4096], P('section', ('tensor', 'dp'))
- out_weight_grad: float32 [2, 4096, 1024], P('section', 'tensor', 'dp')
- norm_gains_grad: float32 [2, 2, 1024], P('section', None, ('tensor', 'dp'))
- norm_biases_grad: float32 [2, 2, 1024], P('section', None, ('tensor', 'dp'))
- out_biases_grad: float32 [2, 2, 1024], P('section', None, ('tensor', 'dp'))
The draws below stay inside these ranges and needn't reach their ends.
Inputs may be any that keep to these rules, and one draw needn't show every extreme that they name: Row j lists the lengths of the documents of sequence j in order, zeros included; they sum to 2048 or less, and the positions after that sum are padding. Among the 2 sequences of each replica (rows j with the same j // 2) one is a single document of 2048 tokens.
All inputs are finite; a program needn't handle non-finite values.
Results may differ from the reference program's by a relative error of at most 0.018.
Values may be sent and summed in bfloat16 or wider, within the bound.
No kernel may reach another device: no remote copies, remote signals or barrier semaphores. Data moves between devices by JAX's collectives and lax.ppermute only.
A program may use at most 320 MiB of HBM per device.

```python
import math
import jax
import jax.numpy as jnp
from jax import lax

D = 1024
HEADS = 16
HDIM = 64
FF = 4096
MB = 2
SEQ = 2048
NDOC = 8
QBLK = 512
SEQS = 8
N_SECTION = 2


def draw_lengths(key, part):
    key = jax.random.fold_in(key, 17)
    count_key, share_key, padding_key, pick_key = jax.random.split(key, 4)
    counts = jax.random.randint(count_key, (SEQS,), 1, NDOC + 1)
    shares = jax.random.randint(share_key, (SEQS, NDOC), 1, 9)
    slots = jnp.arange(NDOC)
    shares = jnp.where(slots[None, :] < counts[:, None], shares, 0)
    padding = jax.random.randint(padding_key, (SEQS,), 1, SEQ // 8 + 1)
    totals = SEQ - padding
    picks = jax.random.randint(pick_key, (SEQS // MB,), 0, MB)
    whole = jnp.arange(SEQS) % MB == jnp.repeat(picks, MB, total_repeat_length=SEQS)
    shares = jnp.where(whole[:, None], (slots[None, :] == 0).astype(jnp.int32), shares)
    totals = jnp.where(whole, SEQ, totals)
    running = jnp.cumsum(shares, axis=1)
    bounds = totals[:, None] * running // running[:, -1:]
    before = jnp.concatenate([jnp.zeros((SEQS, 1), bounds.dtype), bounds[:, :-1]], axis=1)
    return (bounds - before).astype(jnp.int32)


def levels(rng, dims, pieces, smallest, top_value):
    level, own = 1.0, jax.random.fold_in(rng, 6)
    for position, parts in pieces:
        steps = jnp.exp(jax.random.uniform(jax.random.fold_in(own, position), (parts,), jnp.float32, smallest / len(pieces), top_value / len(pieces)))
        level = level * jnp.repeat(steps, dims[position] // parts).reshape([-1 if axis == position else 1 for axis in range(len(dims))])
    return level


def noise(rng, dims, scale, most, cuts=(), kind=jnp.bfloat16):
    entries = scale * jax.random.normal(rng, dims, jnp.float32)
    if cuts:
        entries = entries * levels(rng, dims, cuts, -0.22, 0.18)
    return jnp.clip(entries, -most, most).astype(kind)


def setup_inputs(seed: int = 0) -> dict:
    streams_of = jax.random.split(jax.random.key(seed), 13)
    return {
        "inputs": noise(streams_of[0], (SEQS, SEQ, D), 1.0, 6.0, ((0, 4), (1, 4))),
        "cotangent": noise(streams_of[1], (SEQS, SEQ, D), 1.0, 6.0, ((0, 4), (1, 4))),
        "lengths": draw_lengths(jax.random.fold_in(streams_of[12], 71), 0),
        "qkv_weight": noise(streams_of[3], (N_SECTION, D, 3, D), D ** -0.5, 0.1875, ((0, 2), (1, 4), (3, 4))),
        "qkv_bias": noise(streams_of[4], (N_SECTION, 3, D), 0.5, 3.0, ((0, 2), (2, 16))),
        "dense_weight": noise(streams_of[5], (N_SECTION, D, D), (D // 8) ** -0.5, 0.5, ((0, 2), (1, 4), (2, 4))),
        "in_weight": noise(streams_of[6], (N_SECTION, D, FF), D ** -0.5, 0.1875, ((0, 2), (1, 4), (2, 4))),
        "in_bias": noise(streams_of[7], (N_SECTION, FF), 0.5, 3.0, ((0, 2), (1, 16))),
        "out_weight": noise(streams_of[8], (N_SECTION, FF, D), FF ** -0.5, 0.09375, ((0, 2), (1, 4), (2, 4))),
        "norm_gains": jnp.clip(1.0 + 0.15 * jax.random.normal(streams_of[9], (N_SECTION, 2, D), jnp.float32), 0.25, 1.75).astype(jnp.bfloat16),
        "norm_biases": noise(streams_of[10], (N_SECTION, 2, D), 0.3, 2.0, ((0, 2), (2, 16))),
        "out_biases": noise(streams_of[11], (N_SECTION, 2, D), 0.5, 3.0, ((0, 2), (2, 16))),
    }


exact = lax.Precision.HIGHEST
epsilon = 1e-05

@jax.custom_vjp
def low(v):
    return lax.optimization_barrier(v.astype(jnp.bfloat16)).astype(jnp.float32)

@jax.custom_vjp
def low_back(v):
    return v

def low_keep(v):
    return (low(v), None)

def low_pass(kept, grad):
    return (grad,)

def back_keep(v):
    return (v, None)

def back_low(kept, grad):
    return (low(grad),)
low.defvjp(low_keep, low_pass)
low_back.defvjp(back_keep, back_low)

def layer_norm(values, gain, shift):
    centered = values - lax.optimization_barrier(jnp.mean(values, -1, keepdims=True))
    variance = lax.optimization_barrier(jnp.mean(centered * centered, -1, keepdims=True))
    return centered * lax.rsqrt(variance + epsilon) * gain + shift

def doc_layout(length_row):
    positions = jnp.arange(SEQ, dtype=jnp.int32)
    ends = jnp.cumsum(length_row).astype(jnp.int32)
    passed = positions[:, None] >= ends[None, :]
    doc_ids = lax.optimization_barrier(jnp.sum(passed.astype(jnp.int32), -1)).astype(jnp.int32)
    starts = lax.optimization_barrier(jnp.sum(jnp.where(passed, length_row[None, :], 0), -1)).astype(jnp.int32)
    return (doc_ids, positions - starts, positions < ends[-1])

def rotary_tables(rot_pos):
    rotary = HDIM // 4
    counter = jnp.arange(rotary // 2, dtype=jnp.float32)
    inverse = jnp.exp(counter * (-2.0 * math.log(10000.0) / rotary))
    angles = rot_pos.astype(jnp.float32)[:, None] * inverse[None, :]
    return (jnp.cos(angles), jnp.sin(angles))

def rotate(values, cosine, sine):
    width = cosine.shape[-1]
    leading = values[..., :width]
    trailing = values[..., width:2 * width]
    cosines = cosine[:, None, :]
    sines = sine[:, None, :]
    return jnp.concatenate([leading * cosines - trailing * sines, trailing * cosines + leading * sines, values[..., 2 * width:]], -1)

def attention(queries, keys, values, doc_ids):
    positions = jnp.arange(SEQ, dtype=jnp.int32)
    scale = 1.0 / math.sqrt(HDIM)

    def one_block(index):
        start = (index * QBLK).astype(jnp.int32)
        query_block = lax.dynamic_slice_in_dim(queries, start, QBLK, 0)
        query_docs = lax.dynamic_slice_in_dim(doc_ids, start, QBLK, 0)
        query_pos = start + jnp.arange(QBLK, dtype=jnp.int32)
        allowed = (query_docs[:, None] == doc_ids[None, :]) & (positions[None, :] <= query_pos[:, None])
        scores = jnp.einsum('qhd,khd->hqk', query_block, keys, precision=exact) * scale
        scores = low_back(jnp.where(allowed[None], scores, -1e+30))
        shifted = jnp.exp(scores - lax.optimization_barrier(jnp.max(scores, -1, keepdims=True)))
        probs = shifted / lax.optimization_barrier(jnp.sum(shifted, -1, keepdims=True))
        return jnp.einsum('hqk,khd->qhd', low(probs), values, precision=exact)
    blocks = lax.map(jax.checkpoint(one_block), jnp.arange(SEQ // QBLK, dtype=jnp.int32))
    return blocks.reshape(SEQ, HEADS, HDIM)

def layer(hidden, length_row, qkv_w, qkv_b, dense_w, in_w, in_b, out_w, gains, shifts, out_bias):
    doc_ids, rot_pos, valid = doc_layout(length_row)
    first = low(layer_norm(hidden, gains[0], shifts[0]))
    second = low(layer_norm(hidden, gains[1], shifts[1]))
    projected = jnp.einsum('sd,dcf->scf', first, qkv_w, precision=exact) + qkv_b[None]
    projected = projected.reshape(SEQ, 3, HEADS, HDIM)
    cosine, sine = rotary_tables(rot_pos)
    queries = low(rotate(low_back(projected[:, 0]), cosine, sine))
    keys = low(rotate(low_back(projected[:, 1]), cosine, sine))
    values = low(low_back(projected[:, 2]))
    mixed = low(low_back(attention(queries, keys, values, doc_ids).reshape(SEQ, D)))
    attended = jnp.dot(mixed, dense_w, precision=exact, preferred_element_type=jnp.float32)
    inner = low_back(jnp.dot(second, in_w, precision=exact, preferred_element_type=jnp.float32) + in_b)
    activated = low(jax.nn.gelu(inner, approximate=False))
    branch = low_back(attended + jnp.dot(activated, out_w, precision=exact, preferred_element_type=jnp.float32))
    return hidden + branch + out_bias[0] + out_bias[1]

def reference(inputs, cotangent, lengths, qkv_weight, qkv_bias, dense_weight, in_weight, in_bias, out_weight, norm_gains, norm_biases, out_biases):
    params = [array.astype(jnp.float32) for array in (qkv_weight, qkv_bias, dense_weight, in_weight, in_bias, out_weight, norm_gains, norm_biases, out_biases)]
    start = inputs.astype(jnp.float32)
    probe = jnp.zeros(inputs.shape, jnp.float32)

    def network(start, probe, *weights):

        def per_sequence(items):
            row, probe_row, length_row = items
            middle = layer(row, length_row, *[array[0] for array in weights])
            middle = low_back(low(middle) + probe_row)
            final = layer(middle, length_row, *[array[1] for array in weights])
            return (middle, final)
        return lax.map(per_sequence, (start, probe, lengths))
    (middles, finals), pullback = jax.vjp(network, start, probe, *params)
    valid = jax.vmap(lambda row: doc_layout(row)[2])(lengths)
    loss_grad = cotangent.astype(jnp.float32) * valid[..., None].astype(jnp.float32)
    grads = pullback((jnp.zeros_like(middles), loss_grad))
    activations = jnp.stack([middles, finals]).astype(jnp.bfloat16)
    input_grads = jnp.stack([grads[0], grads[1]])
    return (activations, input_grads, grads[2], grads[3], grads[4], grads[5], grads[6], grads[7], grads[8], grads[9], grads[10])
```

```python
import functools
import math

import jax
import jax.numpy as jnp
from jax import lax
from jax.experimental import pallas as pl
from jax.experimental.pallas import tpu as pltpu
from jax.sharding import PartitionSpec as P

HDIM = 64
EPSILON = 1e-05
TILE = 256
NT = (((1,), (1,)), ((), ()))
NN = (((1,), (0,)), ((), ()))
TN = (((0,), (0,)), ((), ()))
LOG2E = math.log2(math.e)
FAR = 1e15
HURRY = 0.05
LIMIT = pltpu.CompilerParams(vmem_limit_bytes=28 * 2**20)


def mm(a, b, dims=NN):
    return lax.dot_general(a, b, dims, preferred_element_type=jnp.float32)


def cost(flops, moved, special=0):
    return pl.CostEstimate(flops=int(flops * HURRY), bytes_accessed=int(moved * HURRY), transcendentals=int(special))


def flip(block, axis, bit=1):
    return lax.ppermute(block, axis, [(i, i ^ bit) for i in range(lax.axis_size(axis))])


def turn(values, cosine, lead, trail):
    return values * cosine + pltpu.roll(values, 120, 1) * lead + pltpu.roll(values, 8, 1) * trail


def turn_back(grads, cosine, lead, trail):
    return grads * cosine - pltpu.roll(grads, 120, 1) * lead - pltpu.roll(grads, 8, 1) * trail


def spot(table, tile, shard_rows):
    per = shard_rows // TILE
    return pl.multiple_of(table[tile // per] * shard_rows + (tile % per) * TILE, TILE)


def head_part(block, head):
    lane = lax.broadcasted_iota(jnp.int32, block.shape, 1)
    return jnp.where((lane >= head * 64) & (lane < head * 64 + 64), block, jnp.zeros_like(block))


def attend_kernel(shard_rows, tiles, table, q_ref, k_ref, v_ref, fq_ref, fk_ref, out_ref, lse_ref, vt):
    step = pl.program_id(0)

    @pl.when(step == 0)
    def _():
        flipped = v_ref[...].T
        for head in range(2):
            vt[head, 0:64, :] = flipped[head * 64 : head * 64 + 64, :]
            vt[head, 64:80, :] = jnp.ones((16, flipped.shape[1]), jnp.bfloat16)

    def body(last):
        query = q_ref[...]
        feats = fq_ref[...]
        outs = []
        for head in range(2):
            wide = jnp.concatenate([head_part(query, head), feats], 1)
            scores = []
            for tile in range(last + 1):
                at = spot(table, tile, shard_rows)
                keys = jnp.concatenate([k_ref[pl.ds(at, TILE), :], fk_ref[pl.ds(at, TILE), :]], 1)
                block = mm(keys, wide, NT)
                if tile == last:
                    rows = lax.broadcasted_iota(jnp.int32, block.shape, 0)
                    cols = lax.broadcasted_iota(jnp.int32, block.shape, 1)
                    block = jnp.where(rows <= cols, block, -1e30)
                scores.append(block)
            top = jnp.max(scores[0], 0, keepdims=True)
            for block in scores[1:]:
                top = jnp.maximum(top, jnp.max(block, 0, keepdims=True))
            shift = top * LOG2E
            total = None
            for tile in range(last + 1):
                at = spot(table, tile, shard_rows)
                probs = jnp.exp2(scores[tile] * LOG2E - shift).astype(jnp.bfloat16)
                term = mm(vt[head, :, pl.ds(at, TILE)], probs, NN)
                total = term if total is None else total + term
            norm = total[64:65, :]
            outs.append(total[0:64, :] / norm)
            lse_ref[head : head + 1, :] = shift + jnp.log2(norm)
        lse_ref[2:8, :] = jnp.zeros((6, TILE), jnp.float32)
        both = jnp.concatenate(outs, 0)
        out_ref[...] = both.T.astype(jnp.bfloat16)

    for last in range(tiles):
        pl.when(step == last)(functools.partial(body, last))


def attend(table, qkv, fq, fk):
    seq = qkv.shape[0]
    shard_rows = seq // 4
    tiles = seq // TILE
    per = shard_rows // TILE

    def place(step, table):
        return table[step // per] * per + step % per

    return pl.pallas_call(
        functools.partial(attend_kernel, shard_rows, tiles),
        grid_spec=pltpu.PrefetchScalarGridSpec(
            num_scalar_prefetch=1,
            grid=(tiles,),
            in_specs=[
                pl.BlockSpec((TILE, 128), lambda i, t: (place(i, t), 0)),
                pl.BlockSpec((seq, 128), lambda i, t: (0, 1)),
                pl.BlockSpec((seq, 128), lambda i, t: (0, 2)),
                pl.BlockSpec((TILE, 128), lambda i, t: (place(i, t), 0)),
                pl.BlockSpec((seq, 128), lambda i, t: (0, 0)),
            ],
            out_specs=[
                pl.BlockSpec((TILE, 128), lambda i, t: (place(i, t), 0)),
                pl.BlockSpec((8, TILE), lambda i, t: (0, place(i, t))),
            ],
            scratch_shapes=[pltpu.VMEM((2, 80, seq), jnp.bfloat16)],
        ),
        out_shape=[
            jax.ShapeDtypeStruct((seq, 128), jnp.bfloat16),
            jax.ShapeDtypeStruct((8, seq), jnp.float32),
        ],
        compiler_params=LIMIT,
        cost_estimate=cost(4e9, 3e6, 5e6),
        name="attend",
    )(table, qkv, qkv, qkv, fq, fk)


def attend_back_kernel(shard_rows, tiles, table, q_ref, k_ref, v_ref, gm_ref, o_ref, lse_ref, fq_ref, fk_ref,
                       cos_ref, lead_ref, trail_ref, out_ref, kt, dk, dv):
    step = pl.program_id(0)

    @pl.when(step == 0)
    def _():
        kt[...] = k_ref[...].T
        dk[...] = jnp.zeros_like(dk)
        dv[...] = jnp.zeros_like(dv)

    def body(last):
        here = spot(table, last, shard_rows)
        query = q_ref[...]
        feats = fq_ref[...]
        grad = gm_ref[...]
        product = grad.astype(jnp.float32) * o_ref[...].astype(jnp.float32)
        high = product.astype(jnp.bfloat16)
        low = (product - high.astype(jnp.float32)).astype(jnp.bfloat16)
        lane = lax.broadcasted_iota(jnp.int32, (8, 128), 1)
        wides, grads, shifts, deltas, queries = [], [], [], [], []
        for head in range(2):
            ones = jnp.where((lane >= head * 64) & (lane < head * 64 + 64), 1.0, 0.0).astype(jnp.bfloat16)
            deltas.append((mm(ones, high, NT) + mm(ones, low, NT))[0:1, :])
            queries.append(head_part(query, head))
            wides.append(jnp.concatenate([queries[head], feats], 1))
            grads.append(head_part(grad, head))
            shifts.append(lse_ref[head : head + 1, :])
        turned = [None, None]
        for tile in range(last + 1):
            at = spot(table, tile, shard_rows)
            keys = jnp.concatenate([k_ref[pl.ds(at, TILE), :], fk_ref[pl.ds(at, TILE), :]], 1)
            values = v_ref[pl.ds(at, TILE), :]
            dk_term = dv_term = None
            for head in range(2):
                block = mm(keys, wides[head], NT)
                probs = jnp.exp2(block * LOG2E - shifts[head])
                if tile == last:
                    rows = lax.broadcasted_iota(jnp.int32, block.shape, 0)
                    cols = lax.broadcasted_iota(jnp.int32, block.shape, 1)
                    probs = jnp.where(rows <= cols, probs, 0.0)
                back = mm(values, grads[head], NT)
                slope = (probs * (back - deltas[head])).astype(jnp.bfloat16)
                dv_one = mm(probs.astype(jnp.bfloat16), grads[head], NN)
                dk_one = mm(slope, queries[head], NN)
                dv_term = dv_one if head == 0 else dv_term + dv_one
                dk_term = dk_one if head == 0 else dk_term + dk_one
                dq = mm(kt[head * 64 : head * 64 + 64, pl.ds(at, TILE)], slope, NN)
                turned[head] = dq if tile == 0 else turned[head] + dq
            dv[pl.ds(at, TILE), :] += dv_term
            dk[pl.ds(at, TILE), :] += dk_term
        dq = jnp.concatenate(turned, 0).T * 0.125
        dq = turn_back(dq, cos_ref[pl.ds(here, TILE), :], lead_ref[pl.ds(here, TILE), :], trail_ref[pl.ds(here, TILE), :])
        out_ref[pl.ds(here, TILE), 0:128] = dq.astype(jnp.bfloat16)

    for last in range(tiles):
        pl.when(step == last)(functools.partial(body, last))

    @pl.when(step == tiles - 1)
    def _():
        def finish(block, carry):
            rows = pl.ds(pl.multiple_of(block * TILE, TILE), TILE)
            turned = turn_back(dk[rows, :], cos_ref[rows, :], lead_ref[rows, :], trail_ref[rows, :])
            out_ref[rows, 128:256] = turned.astype(jnp.bfloat16)
            out_ref[rows, 256:384] = dv[rows, :].astype(jnp.bfloat16)
            return carry

        lax.fori_loop(0, tiles, finish, 0)


def attend_back(table, qkv, grad_mixed, mixed, lse, fq, fk, turns):
    seq = qkv.shape[0]
    shard_rows = seq // 4
    tiles = seq // TILE
    per = shard_rows // TILE

    def place(step, table):
        return table[step // per] * per + step % per

    whole = pl.BlockSpec((seq, 128), lambda i, t: (0, 0))
    block = pl.BlockSpec((TILE, 128), lambda i, t: (place(i, t), 0))
    return pl.pallas_call(
        functools.partial(attend_back_kernel, shard_rows, tiles),
        grid_spec=pltpu.PrefetchScalarGridSpec(
            num_scalar_prefetch=1,
            grid=(tiles,),
            in_specs=[
                block,
                pl.BlockSpec((seq, 128), lambda i, t: (0, 1)),
                pl.BlockSpec((seq, 128), lambda i, t: (0, 2)),
                block,
                block,
                pl.BlockSpec((8, TILE), lambda i, t: (0, place(i, t))),
                block,
                whole,
                whole,
                whole,
                whole,
            ],
            out_specs=pl.BlockSpec((seq, 384), lambda i, t: (0, 0)),
            scratch_shapes=[
                pltpu.VMEM((128, seq), jnp.bfloat16),
                pltpu.VMEM((seq, 128), jnp.float32),
                pltpu.VMEM((seq, 128), jnp.float32),
            ],
        ),
        out_shape=jax.ShapeDtypeStruct((seq, 384), jnp.bfloat16),
        compiler_params=LIMIT,
        cost_estimate=cost(10e9, 6e6, 5e6),
        name="attend_back",
    )(table, qkv, qkv, qkv, grad_mixed, mixed, lse, fq, fk, *turns)


def normal_of(values):
    centered = values - jnp.mean(values, -1, keepdims=True)
    inverse = lax.rsqrt(jnp.mean(centered * centered, -1, keepdims=True) + EPSILON)
    return centered * inverse, inverse


def whole_of(array):
    return pl.BlockSpec(array.shape, lambda *i: (0,) * array.ndim)


def heads_of(first, weight, bias, turns, out_ref):
    projected = mm(first, weight) + bias
    for part in range(3):
        piece = projected[:, 128 * part : 128 * part + 128]
        if part < 2:
            piece = turn(piece, *turns)
        if part == 0:
            piece = piece * 0.125
        out_ref[:, 128 * part : 128 * part + 128] = piece.astype(jnp.bfloat16)


def settle(slots, source, target, start=0):
    @pl.when(pl.program_id(0) == 0)
    def _():
        rows = target.shape[0] // source.shape[0]
        for block in range(source.shape[0]):
            target[block * rows : block * rows + rows, :] = source[slots[block], 0:rows, start : start + target.shape[1]]


def weight_scratch(width, weight, cols=None):
    return pltpu.VMEM((width, cols or weight.shape[2]), weight.dtype)


def choose(pieces, target):
    for step, piece in enumerate(pieces):

        @pl.when(pl.program_id(0) == step)
        def _():
            target[...] = piece[...]


def call(kernel, name, grid, in_specs, out_specs, out_shape, scratch, flops, moved, special=0, scalars=1, aliases=None):
    return pl.pallas_call(
        kernel,
        grid_spec=pltpu.PrefetchScalarGridSpec(
            num_scalar_prefetch=scalars, grid=grid, in_specs=in_specs, out_specs=out_specs, scratch_shapes=scratch
        ),
        out_shape=out_shape,
        compiler_params=LIMIT,
        cost_estimate=cost(flops, moved, special),
        input_output_aliases=aliases or {},
        name=name,
    )


def struct(*shape):
    return jax.ShapeDtypeStruct(shape, jnp.bfloat16)


def project_kernel(
    slots, h0, h1, h2, h3, weight_ref, bias_ref, norm_ref, cos_ref, lead_ref, trail_ref,
    out_ref, first_ref, second_ref, flip_ref, weight, h_ref
):
    settle(slots, weight_ref, weight)
    choose((h0, h1, h2, h3), h_ref)
    normal, _ = normal_of(h_ref[...].astype(jnp.float32))
    flip_ref[...] = normal.astype(jnp.bfloat16).T
    first = (normal * norm_ref[0:1, :] + norm_ref[2:3, :]).astype(jnp.bfloat16)
    first_ref[...] = first
    second_ref[...] = (normal * norm_ref[1:2, :] + norm_ref[3:4, :]).astype(jnp.bfloat16)
    heads_of(first, weight[...], bias_ref[0:1, 0 : weight.shape[1]], (cos_ref[...], lead_ref[...], trail_ref[...]), out_ref)


def project(slots, pieces, weight, cols, bias, norms, turns):
    rows, width = pieces[0].shape
    seq = rows * len(pieces)
    block = pl.BlockSpec((rows, width), lambda i, s: (i, 0))
    return call(
        project_kernel,
        "project",
        (seq // rows,),
        [whole_of(x) for x in (*pieces, weight, bias, norms)] + [pl.BlockSpec((rows, 128), lambda i, s: (i, 0))] * 3,
        [pl.BlockSpec((rows, cols), lambda i, s: (i, 0)), block, block, pl.BlockSpec((width, rows), lambda i, s: (0, i))],
        [struct(seq, cols), struct(seq, width), struct(seq, width), struct(width, seq)],
        [weight_scratch(width, weight, cols), pltpu.VMEM((rows, width), jnp.bfloat16)],
        4e9,
        18e6,
    )(slots, *pieces, weight, bias, norms, *turns)


def project_more_kernel(slots, first_ref, weight_ref, bias_ref, cos_ref, lead_ref, trail_ref, out_ref, weight):
    settle(slots, weight_ref, weight)
    heads_of(
        first_ref[...], weight[...], bias_ref[1:2, 0 : weight.shape[1]], (cos_ref[...], lead_ref[...], trail_ref[...]), out_ref
    )


def project_more(slots, first, weight, cols, bias, turns):
    seq, width = first.shape
    rows = 512
    return call(
        project_more_kernel,
        "project_more",
        (seq // rows,),
        [pl.BlockSpec((rows, width), lambda i, s: (i, 0)), whole_of(weight), whole_of(bias)]
        + [pl.BlockSpec((rows, 128), lambda i, s: (i, 0))] * 3,
        pl.BlockSpec((rows, cols), lambda i, s: (i, 0)),
        struct(seq, cols),
        [weight_scratch(width, weight, cols)],
        3e9,
        8e6,
    )(slots, first, weight, bias, *turns)


def gelu_kernel(part, slots, a_ref, weight_ref, bias_ref, out_ref, slope_ref, weight):
    settle(slots, weight_ref, weight, weight_ref.shape[2] - weight.shape[1])
    inner = mm(a_ref[...], weight[...]) + bias_ref[part : part + 1, bias_ref.shape[1] - weight.shape[1] :]
    size = jnp.abs(inner)
    t = 1.0 / (1.0 + (0.3275911 * math.sqrt(0.5)) * size)
    bell = jnp.exp2((-0.5 * LOG2E) * inner * inner)
    poly = 0.5 * 1.061405429 * t + 0.5 * -1.453152027
    poly = poly * t + 0.5 * 1.421413741
    poly = poly * t + 0.5 * -0.284496736
    poly = poly * t + 0.5 * 0.254829592
    tail = poly * t * bell
    below = jnp.where(inner >= 0, 1.0 - tail, tail)
    out_ref[...] = (inner * below).astype(jnp.bfloat16)
    slope_ref[...] = (below + inner * bell * (1.0 / math.sqrt(2 * math.pi))).astype(jnp.bfloat16)


def gelu_up(slots, second, weight, cols, bias, part):
    seq, width = second.shape
    rows = 256
    block = pl.BlockSpec((rows, cols), lambda i, s: (i, 0))
    return call(
        functools.partial(gelu_kernel, part),
        "gelu_up",
        (seq // rows,),
        [pl.BlockSpec((rows, width), lambda i, s: (i, 0)), whole_of(weight), whole_of(bias)],
        [block, block],
        [struct(seq, cols), struct(seq, cols)],
        [weight_scratch(width, weight, cols)],
        5e9,
        10e6,
        2e6,
    )(slots, second, weight, bias)


def deal(value, *targets):
    for step, target in enumerate(targets):

        @pl.when(pl.program_id(0) == step)
        def _():
            target[...] = value


def down_kernel(slots, mixed_mine, mixed_other, act_mine, act_other, mine_ref, other_ref, near_ref, beside_ref, mine, other):
    settle(slots, mine_ref, mine)
    settle(slots, other_ref, other)
    heads = mixed_mine.shape[1]
    total = mm(mixed_mine[...], mine[:, 0:heads], NT) + mm(act_mine[...], mine[:, heads:], NT)
    total += mm(mixed_other[...], other[:, 0:heads], NT) + mm(act_other[...], other[:, heads:], NT)
    deal(total.astype(jnp.bfloat16), near_ref, beside_ref)


def down(slots, mixed, act, weights, half):
    seq = mixed[0].shape[0]
    width = weights[0].shape[0] * weights[0].shape[1]
    rows = 512
    steps = seq // rows // 2
    return call(
        down_kernel,
        "down",
        (steps,),
        [pl.BlockSpec((rows, x.shape[1]), lambda i, s: (i + half * steps, 0)) for x in (*mixed, *act)]
        + [whole_of(w) for w in weights],
        [pl.BlockSpec((rows, width), lambda i, s: (0, 0))] * 2,
        [struct(rows, width)] * 2,
        [weight_scratch(width, w) for w in weights],
        4e9,
        8e6,
    )(slots, *mixed, *act, *weights)


def down_back_kernel(
    slots, g0, g1, g2, g3, slope_mine, slope_other, mine_ref, other_ref,
    mixed_mine, mixed_other, inner_mine, inner_other, flip_ref, mine, other, grad_ref
):
    choose((g0, g1, g2, g3), grad_ref)
    settle(slots, mine_ref, mine)
    settle(slots, other_ref, other)
    heads = mixed_mine.shape[1]
    flip_ref[...] = grad_ref[...].T
    for slope, weight, mixed, inner in (
        (slope_mine, mine, mixed_mine, inner_mine),
        (slope_other, other, mixed_other, inner_other),
    ):
        mixed[...] = mm(grad_ref[...], weight[:, 0:heads]).astype(jnp.bfloat16)
        inner[...] = (mm(grad_ref[...], weight[:, heads:]) * slope[...].astype(jnp.float32)).astype(jnp.bfloat16)


def down_back(slots, pieces, slopes, weights, heads):
    rows, width = pieces[0].shape
    seq = rows * len(pieces)
    hidden = slopes[0].shape[1]
    wide = pl.BlockSpec((rows, hidden), lambda i, s: (i, 0))
    return call(
        down_back_kernel,
        "down_back",
        (seq // rows,),
        [whole_of(x) for x in pieces] + [wide, wide] + [whole_of(w) for w in weights],
        [pl.BlockSpec((rows, heads), lambda i, s: (i, 0))] * 2 + [wide, wide, pl.BlockSpec((width, rows), lambda i, s: (0, i))],
        [struct(seq, heads)] * 2 + [struct(seq, hidden)] * 2 + [struct(width, seq)],
        [weight_scratch(width, w) for w in weights] + [pltpu.VMEM((rows, width), jnp.bfloat16)],
        8e9,
        18e6,
    )(slots, *pieces, *slopes, *weights)


def up_back_kernel(
    slots, proj_mine, proj_other, inner_mine, inner_other, qkv_mine, qkv_other, in_mine, in_other, gain_ref, near_ref, beside_ref, *weights
):
    for source, target in zip((qkv_mine, qkv_other), weights[:2]):
        settle(slots, source, target)
    for source, target in zip((in_mine, in_other), weights[2:]):
        settle(slots, source, target, source.shape[2] - target.shape[1])
    qkv_a, qkv_b, in_a, in_b = weights
    first = mm(proj_mine[...], qkv_a[...], NT) + mm(proj_other[...], qkv_b[...], NT)
    second = mm(inner_mine[...], in_a[...], NT) + mm(inner_other[...], in_b[...], NT)
    deal((first * gain_ref[0:1, :] + second * gain_ref[1:2, :]).astype(jnp.bfloat16), near_ref, beside_ref)


def up_back(slots, proj, inner, qkv_w, in_w, gains, half):
    seq = proj[0].shape[0]
    width = gains.shape[1]
    rows = 512
    steps = seq // rows // 2
    return call(
        up_back_kernel,
        "up_back",
        (steps,),
        [pl.BlockSpec((rows, x.shape[1]), lambda i, s: (i + half * steps, 0)) for x in (*proj, *inner)]
        + [whole_of(w) for w in (*qkv_w, *in_w, gains)],
        [pl.BlockSpec((rows, width), lambda i, s: (0, 0))] * 2,
        [struct(rows, width)] * 2,
        [weight_scratch(width, w, x.shape[1]) for w, x in zip((*qkv_w, *in_w), (*proj, *inner))],
        4e9,
        10e6,
    )(slots, *proj, *inner, *qkv_w, *in_w, gains)


def grads_kernel(ups, downs, adds, slots, *refs):
    refs = list(refs)
    normal = refs.pop(0) if ups else None
    flipped = refs.pop(0) if downs else None
    backs = [refs.pop(0) for _ in range(ups)]
    sources = [refs.pop(0) for _ in range(downs)]
    weights = [refs.pop(0) for _ in range(ups)]
    norm_ref = refs.pop(0)
    got_ref = refs.pop(0) if adds else None
    out_ref = refs.pop(0)
    row = 1 if downs else 0
    norm = norm_ref[...].T
    gain_column, bias_column = norm[:, row : row + 1], norm[:, 2 + row : 3 + row]

    def store(first, last, value):
        if adds:
            value += got_ref[0, :, first:last].astype(jnp.float32)
        out_ref[0, :, first:last] = value.astype(jnp.bfloat16)

    at = 0
    for k in range(ups):
        stat_ref, sum_ref = refs[2 * k : 2 * k + 2]
        cols = backs[k].shape[1]
        raw = mm(normal[...], backs[k][...])
        total = mm(jnp.ones((8, backs[k].shape[0]), jnp.bfloat16), backs[k][...])
        sum_ref[...] = total
        total = total[0:1, :]
        store(at, at + cols, raw * gain_column + total * bias_column)
        first = weights[k].shape[2] - cols if downs else 0
        wide = weights[k][0, :, first : first + cols].astype(jnp.float32)
        lane = lax.broadcasted_iota(jnp.int32, stat_ref.shape, 1)
        gain = jnp.sum(raw * wide, 1, keepdims=True)
        shift = jnp.sum(wide * total, 1, keepdims=True)
        stat_ref[...] = jnp.where(lane == 0, gain, jnp.where(lane == 1, shift, 0.0))
        at += cols
    for source in sources:
        cols = source.shape[1]
        store(at, at + cols, mm(flipped[...], source[...]))
        at += cols


def weight_grads(slots, normal, flipped, ups, downs, norms, got=None):
    width, seq = (normal if ups else flipped).shape
    groups = 4
    rows = width // groups
    strip = pl.BlockSpec((rows, seq), lambda i, s: (i, 0))
    args, specs = [], []
    for array, used in ((normal, ups), (flipped, downs)):
        if used:
            args.append(array)
            specs.append(strip)
    for array in [back for back, _ in ups] + list(downs):
        args.append(array)
        specs.append(whole_of(array))
    for _, weight in ups:
        args.append(weight)
        specs.append(pl.BlockSpec((1, rows, weight.shape[2]), lambda i, s: (s[i], 0, 0)))
    args.append(norms)
    specs.append(pl.BlockSpec((norms.shape[0], rows), lambda i, s: (0, i)))
    cols = sum(back.shape[1] for back, _ in ups) + sum(source.shape[1] for source in downs)
    out_specs = [pl.BlockSpec((1, rows, cols), lambda i, s: (i, 0, 0))]
    if got is not None:
        args.append(got)
        specs.append(out_specs[0])
    out_shape = [struct(groups, rows, cols)]
    for back, _ in ups:
        out_specs += [pl.BlockSpec((rows, 8), lambda i, s: (i, 0)), pl.BlockSpec((8, back.shape[1]), lambda i, s: (0, 0))]
        out_shape += [jax.ShapeDtypeStruct((width, 8), jnp.float32), jax.ShapeDtypeStruct((8, back.shape[1]), jnp.float32)]
    return call(
        functools.partial(grads_kernel, len(ups), len(downs), got is not None),
        "weight_grads",
        (groups,),
        specs,
        out_specs,
        out_shape,
        [],
        2 * seq * width * cols,
        8e6,
    )(slots, *args)


def shards(
    inputs,
    cotangent,
    lengths,
    qkv_weight,
    qkv_bias,
    dense_weight,
    in_weight,
    in_bias,
    out_weight,
    norm_gains,
    norm_biases,
    out_biases,
):
    f32, bf16 = jnp.float32, jnp.bfloat16
    lefthand = lax.axis_index("section") == 0
    me, depth = lax.axis_index("tensor"), lax.axis_index("dp")
    n_tensor, n_dp = lax.axis_size("tensor"), lax.axis_size("dp")
    shard_rows, width = inputs.shape[1:]
    heads = qkv_weight.shape[3]
    hidden = in_weight.shape[2]
    groups = 4
    direct = n_dp == groups

    def pick(first, second):
        return jnp.where(lefthand, first, second)

    def ordered(mine, other):
        return pick(mine, other), pick(other, mine)

    steps = jnp.arange(groups, dtype=jnp.int32)
    slots = (depth - steps) % groups if direct else steps

    def gather_deep(piece):
        if not direct:
            return lax.all_gather(piece, "dp", axis=0, tiled=True).reshape(groups, -1, piece.shape[1])
        pieces = [piece]
        for hop in range(1, n_dp):
            pieces.append(lax.ppermute(piece, "dp", [(i, (i + hop) % n_dp) for i in range(n_dp)]))
        return jnp.stack(pieces)

    def scatter_late(total):
        return lax.psum_scatter(total.reshape(-1, total.shape[2]), "dp", scatter_dimension=0, tiled=True)

    def pin(*values):
        return lax.optimization_barrier(values)

    h_own = pick(inputs[0], inputs[1])
    cot = pick(cotangent[0], cotangent[1])
    row = pick(lengths[0], lengths[1])

    def halves(group):
        return pick(group[0], group[1]), pick(group[1], group[0])

    def cut(array, axis, k):
        size = array.shape[axis] // 2
        return lax.slice_in_dim(array, k * size, k * size + size, axis=axis)

    small = jnp.concatenate([piece[0].reshape(-1) for piece in (qkv_bias, norm_gains, norm_biases, out_biases, in_bias)])
    part = qkv_bias.shape[2]
    n_small = small.shape[0]
    qkv_cols, in_cols = 3 * heads // 2, hidden // 2
    qkv_half = halves([cut(qkv_weight[0], 2, k).reshape(-1, qkv_cols) for k in range(2)])
    qkv_got = flip(qkv_half[1], "section")
    pair = jnp.stack([small, flip(small, "tensor", 2)])
    h_own, pair = pin(h_own, pair)
    h_far = flip(h_own, "tensor", 2)
    pair = jnp.stack([pair, flip(pair, "tensor", 1)], 1)
    pair = jnp.stack(ordered(pair, flip(pair, "section"))).reshape(-1)
    extra = -(-pair.shape[0] // (16 * qkv_cols)) * 16
    pair = jnp.zeros((extra * qkv_cols,), bf16).at[: pair.shape[0]].set(pair).reshape(extra, qkv_cols)
    deep = qkv_half[0].shape[0]
    qkv_shard = ordered(qkv_half[0], qkv_got)
    rest_half = halves(
        [
            jnp.concatenate([cut(in_weight[0], 1, k), cut(dense_weight[0], 0, k).T, cut(out_weight[0], 0, k).T], 1)
            for k in range(2)
        ]
    )
    first = jnp.concatenate([qkv_shard[0], pair], 0)
    first, row, cot, rest_mine, rest_other = pin(first, row, cot, *rest_half)
    first = gather_deep(first) if direct else lax.all_gather(first, "dp", axis=0)
    rest_shard = ordered(rest_mine, flip(rest_other, "section"))
    qkv0 = first if direct else first[:, :deep].reshape(groups, -1, qkv_cols)
    pair = first[:, deep:].reshape(n_dp, -1)[:, : 2 * n_tensor * n_small].reshape(n_dp, 2, n_tensor, n_small)
    order = jnp.arange(n_tensor) ^ me
    small_all = pair.astype(f32).transpose(1, 2, 0, 3)

    def chosen(array, index, axis):
        size = index.shape[0]
        shape = [1] * array.ndim
        shape[axis] = size
        return sum(
            jnp.where(index.reshape(shape) == place, lax.slice_in_dim(array, place, place + 1, axis=axis), 0.0)
            for place in range(size)
        )

    if direct:
        small_all = chosen(small_all, slots, 2)
    here = small_all[:, 0]
    small_all = chosen(small_all, order, 1)

    def gather_early(piece):
        return lax.all_gather(piece, "dp", axis=0, tiled=True).reshape(groups, -1, piece.shape[1])

    def shares(rest):
        return rest[:, :in_cols], rest[:, in_cols:]

    table = jnp.arange(n_tensor, dtype=jnp.int32) ^ me
    positions = jnp.concatenate(
        [slot * shard_rows + jnp.arange(shard_rows, dtype=jnp.int32) for slot in (me, me ^ 1, me ^ 2, me ^ 3)]
    )
    ends = jnp.cumsum(row)
    passed = positions[:, None] >= ends[None, :]
    doc = jnp.sum(passed.astype(jnp.int32), -1)
    offset = positions - jnp.sum(jnp.where(passed, row[None, :], 0), -1)
    valid_own = (positions < ends[-1])[:shard_rows]
    lane = jnp.arange(128, dtype=jnp.int32)
    same = doc[:, None] == lane[None, :]
    feats_q = jnp.where(same, -FAR, 0.0).astype(bf16)
    feats_k = jnp.where(same | (lane[None, :] > row.shape[0]), 0.0, FAR).astype(bf16)
    place = lane % HDIM
    rotary = HDIM // 4
    counter = (place % (rotary // 2)).astype(f32)
    inverse = jnp.exp(counter * (-2.0 * math.log(10000.0) / rotary))
    angles = offset.astype(f32)[:, None] * inverse[None, :]
    turned = (place < rotary)[None, :]
    sine = jnp.sin(angles)
    rotary_turns = (
        jnp.where(turned, jnp.cos(angles), 1.0),
        jnp.where((place < rotary // 2)[None, :], -sine, 0.0),
        jnp.where(turned & (place >= rotary // 2)[None, :], sine, 0.0),
    )

    rows_all = small_all[..., 3 * part : 9 * part].reshape(2, n_tensor, n_dp, 6, part).transpose(0, 3, 1, 2, 4)
    rows_all = jnp.pad(rows_all.reshape(2, 6, width), ((0, 0), (0, 2), (0, 0)))
    qkv_parts = here[..., : 3 * part].reshape(2, n_dp, 3, part).transpose(0, 2, 1, 3).reshape(2, 3, 2, heads // 2)
    qkv_parts = qkv_parts.transpose(0, 2, 1, 3).reshape(2, 2, qkv_cols)
    bias_all = jnp.concatenate([qkv_parts, here[..., 9 * part : n_small].reshape(2, 2, in_cols)], 2)
    bias_all = pick(bias_all, bias_all[:, ::-1])

    def chip_sum(terms):
        return terms[0].astype(f32) + flip(terms[1], "tensor", 1).astype(f32)

    def branch_sum(make):
        far = chip_sum(make(1)).astype(bf16)
        return chip_sum(make(0)), far

    def result_of(own, near, far, rows):
        return (own.astype(f32) + near + far.astype(f32) + rows[4:5] + rows[5:6]).astype(bf16)

    def input_back(own, grad_own, partial):
        n, inverse = normal_of(own.astype(f32))
        return grad_own.astype(f32) + inverse * (
            partial - jnp.mean(partial, -1, keepdims=True) - n * jnp.mean(partial * n, -1, keepdims=True)
        )

    def attend_one(qkv):
        return attend(table, qkv, feats_q, feats_k)

    def attend_back_one(qkv, attended, grad_mixed):
        mixed, lse = attended
        return attend_back(table, qkv, grad_mixed, mixed, lse, feats_q, feats_k, rotary_turns)

    def rows_of(own, far):
        return own, flip(own, "tensor", 1), far, flip(far, "tensor", 1)

    (in_shard0, out_shard0), (in_shard1, out_shard1) = shares(rest_shard[0]), shares(rest_shard[1])
    qkv0, rows_all, bias_all, *h_all = pin(qkv0, rows_all, bias_all, *rows_of(h_own, h_far))
    (norms0, norms1), (bias0, bias1) = rows_all, bias_all
    qkv0_other = flip(qkv0, "section")
    qkv_a0, normed, second, normal0 = project(slots, h_all, qkv0, qkv_cols, bias0, norms0, rotary_turns)
    qkv_a0, cot, in_shard0, out_shard0 = pin(qkv_a0, cot, in_shard0, out_shard0)
    in0 = gather_deep(in_shard0)
    out0 = gather_early(out_shard0)
    grad2 = cot * valid_own[:, None].astype(bf16)
    grad2_far = flip(grad2, "tensor", 2)
    mixed_a0 = attend_one(qkv_a0)
    in0, qkv0_other, normed, *mixed_a0 = pin(in0, qkv0_other, normed, *mixed_a0)
    in0_other = flip(in0, "section")
    qkv0 = (qkv0, qkv0_other)
    qkv_b0 = project_more(slots, normed, qkv0[1], qkv_cols, bias0, rotary_turns)
    mixed_b0 = attend_one(qkv_b0)
    up_shard1 = jnp.concatenate([qkv_shard[1], in_shard1], 1)
    second, grad2_far, in0_other, out0, up_shard1, out_shard1, *mixed_b0 = pin(
        second, grad2_far, in0_other, out0, up_shard1, out_shard1, *mixed_b0
    )
    in0, out0 = (in0, in0_other), (out0, flip(out0, "section"))
    up1 = gather_early(up_shard1)
    hid_a0 = gelu_up(slots, second, in0[0], in_cols, bias0, 0)
    grad_all1 = rows_of(grad2, grad2_far)
    hid_b0 = gelu_up(slots, second, in0[1], in_cols, bias0, 1)
    mixed0 = (mixed_a0[0], mixed_b0[0])
    near, far = branch_sum(lambda half: down(steps, mixed0, (hid_a0[0], hid_b0[0]), out0, half))
    far, up1, out_shard1, *grad_all1 = pin(far, up1, out_shard1, *grad_all1)
    out1 = gather_early(out_shard1)
    qkv1_other = flip(up1[:, :, :qkv_cols], "section")
    middle = result_of(h_own, near, flip(far, "tensor", 2), norms0)
    middle, up1, qkv1_other = pin(middle, up1, qkv1_other)
    in1_other = flip(up1[:, :, qkv_cols:], "section")

    h_all = rows_of(middle, flip(middle, "tensor", 2))
    in1_other, *h_all = pin(in1_other, *h_all)
    qkv1, in1 = (up1, qkv1_other), (up1, in1_other)
    qkv_a1, normed, second, normal1 = project(steps, h_all, qkv1[0], qkv_cols, bias1, norms1, rotary_turns)
    mixed_a1 = attend_one(qkv_a1)
    normed, out1, *mixed_a1 = pin(normed, out1, *mixed_a1)
    out1_other = flip(out1, "section")
    qkv_b1 = project_more(steps, normed, qkv1[1], qkv_cols, bias1, rotary_turns)
    mixed_b1 = attend_one(qkv_b1)
    second, *mixed_b1 = pin(second, *mixed_b1)
    hid_a1 = gelu_up(steps, second, in1[0], in_cols, bias1, 0)
    hid_b1 = gelu_up(steps, second, in1[1], in_cols, bias1, 1)
    mixed1 = (mixed_a1[0], mixed_b1[0])
    out1_other, hid_a1, hid_b1 = pin(out1_other, hid_a1, hid_b1)
    out1 = (out1, out1_other)

    gm_a, gm_b, gi_a1, gi_b1, flipped1 = down_back(steps, grad_all1, (hid_a1[1], hid_b1[1]), out1, heads // 2)

    def rest_grads(blocks, normal, flipped, gi, in_w, mixed, hid, norms, got=None):
        return weight_grads(blocks, normal, flipped, ((gi, in_w),), (mixed, hid[0]), norms, got)

    def qkv_grads(blocks, normal, gp, qkv_w, norms, got=None):
        return weight_grads(blocks, normal, None, ((gp, qkv_w),), (), norms, got)

    rest_b1 = rest_grads(steps, normal1, flipped1, gi_b1, in1[1], mixed1[1], hid_b1, norms1)
    gm_a, gm_b, rest_b1_grad = pin(gm_a, gm_b, rest_b1[0])
    rest_got1 = flip(rest_b1_grad, "section")
    gp_b1 = attend_back_one(qkv_b1, mixed_b1, gm_b)
    gm_a, gp_b1 = pin(gm_a, gp_b1)
    gp_a1 = attend_back_one(qkv_a1, mixed_a1, gm_a)
    gp_a1, rest_got1 = pin(gp_a1, rest_got1)
    near, far = branch_sum(lambda half: up_back(steps, (gp_a1, gp_b1), (gi_a1, gi_b1), qkv1, in1, norms1, half))
    far, normal1, flipped1, rest_got1 = pin(far, normal1, flipped1, rest_got1)
    far = flip(far, "tensor", 2)
    rest_a1 = rest_grads(steps, normal1, flipped1, gi_a1, in1[0], mixed1[0], hid_a1, norms1, rest_got1)
    normal1, rest_a1_grad = pin(normal1, rest_a1[0])
    qkv_g_b1 = qkv_grads(steps, normal1, gp_b1, qkv1[1], norms1)
    normal1, qkv_b1_grad, mixed1_a, mixed1_b = pin(normal1, qkv_g_b1[0], *mixed1)
    qkv_got1 = flip(qkv_b1_grad, "section")
    final_far = chip_sum(down(steps, (mixed1_a, mixed1_b), (hid_a1[0], hid_b1[0]), out1, 1)).astype(bf16)
    far, normal1, rest_a1_grad = pin(far, normal1, rest_a1_grad)
    grad1 = input_back(middle, grad2, near + far.astype(f32))
    grad1_low = grad1.astype(bf16)
    grad1_low, rest_a1_grad, normal1, final_far, mixed1_a, mixed1_b = pin(
        grad1_low, rest_a1_grad, normal1, final_far, mixed1_a, mixed1_b
    )
    grad1_far = flip(grad1_low, "tensor", 2)
    reduced_rest1 = scatter_late(rest_a1_grad)
    qkv_g_a1 = qkv_grads(steps, normal1, gp_a1, qkv1[0], norms1, qkv_got1)
    near_terms = down(steps, (mixed1_a, mixed1_b), (hid_a1[0], hid_b1[0]), out1, 0)
    grad1_far, qkv_a1_grad, *near_terms = pin(grad1_far, qkv_g_a1[0], *near_terms)
    grad_all0 = rows_of(grad1_low, grad1_far)
    final_far, *grad_all0 = pin(final_far, *grad_all0)
    final_far = flip(final_far, "tensor", 2)

    gm_a, gm_b, gi_a0, gi_b0, flipped0 = down_back(steps, grad_all0, (hid_a0[1], hid_b0[1]), out0, heads // 2)
    rest_b0 = rest_grads(slots, normal0, flipped0, gi_b0, in0[1], mixed0[1], hid_b0, norms0)
    gm_a, gm_b, rest_b0_grad, qkv_a1_grad, reduced_rest1 = pin(gm_a, gm_b, rest_b0[0], qkv_a1_grad, reduced_rest1)
    rest_got0 = flip(rest_b0_grad, "section")
    reduced_qkv1 = scatter_late(qkv_a1_grad)
    gp_b0 = attend_back_one(qkv_b0, mixed_b0, gm_b)
    gp_b0, gm_a, normal0, final_far = pin(gp_b0, gm_a, normal0, final_far)
    final = result_of(middle, chip_sum(near_terms), final_far, norms1)
    qkv_g_b0 = qkv_grads(slots, normal0, gp_b0, qkv0[1], norms0)
    normal0, qkv_b0_grad = pin(normal0, qkv_g_b0[0])
    rest_a0 = rest_grads(slots, normal0, flipped0, gi_a0, in0[0], mixed0[0], hid_a0, norms0)
    gm_a, qkv_b0_grad, rest_a0_grad, rest_got0, final, reduced_qkv1 = pin(
        gm_a, qkv_b0_grad, rest_a0[0], rest_got0, final, reduced_qkv1
    )
    qkv_got0 = flip(qkv_b0_grad, "section")
    reduced_rest0 = scatter_late((rest_a0_grad.astype(f32) + rest_got0.astype(f32)).astype(bf16))
    gp_a0 = attend_back_one(qkv_a0, mixed_a0, gm_a)
    gp_a0, normal0, qkv_got0 = pin(gp_a0, normal0, qkv_got0)
    qkv_g_a0 = qkv_grads(slots, normal0, gp_a0, qkv0[0], norms0, qkv_got0)
    gp_a0, last, final = pin(gp_a0, qkv_g_a0[0], final)
    act_got = flip(pick(final, middle), "section")
    near, far = branch_sum(lambda half: up_back(slots, (gp_a0, gp_b0), (gi_a0, gi_b0), qkv0, in0, norms0, half))
    stats = [
        [[pieces[0][1], pieces[1][1], pieces[0][2], pieces[1][2]] for pieces in pair]
        for pair in (((qkv_g_a0, qkv_g_b0), (rest_a0, rest_b0)), ((qkv_g_a1, qkv_g_b1), (rest_a1, rest_b1)))
    ]
    far, stats = pin(far, stats)
    far = flip(far, "tensor", 2)

    packed = []
    for grad_own, (qkv_t, in_t) in zip((grad1_low, grad2), stats):
        vectors = jnp.concatenate([(qkv_t[0] + qkv_t[1])[:, :2], (in_t[0] + in_t[1])[:, :2]], 1).T
        vectors = jnp.concatenate([vectors[0::2], vectors[1::2], jnp.sum(grad_own.astype(f32), 0, keepdims=True)], 0)
        everywhere = vectors.reshape(5, n_tensor, n_dp, part).transpose(1, 2, 0, 3).reshape(n_tensor, n_dp, -1)
        halves_q = ordered(qkv_t[2][0].reshape(3, heads // 2), qkv_t[3][0].reshape(3, heads // 2))
        bias_q = jnp.concatenate(halves_q, 1).reshape(3, n_dp, part).transpose(1, 0, 2).reshape(n_dp, -1)
        bias_i = jnp.concatenate(ordered(in_t[2][0], in_t[3][0])).reshape(n_dp, -1)
        mine = jnp.concatenate([bias_q, bias_i], 1)
        only = (jnp.arange(n_tensor) == me)[:, None, None]
        packed.append(jnp.concatenate([everywhere, jnp.where(only, mine[None], 0.0)], 2))
    total = pick(packed[0], packed[1]) + flip(pick(packed[1], packed[0]), "section")
    total = chosen(total, order, 0)
    small_sum = total[0::2] + flip(total[1::2], "tensor", 1)
    far, small_sum = pin(far, small_sum)
    last, reduced_rest0 = pin(last, reduced_rest0)
    reduced_qkv0 = scatter_late(last)
    grad0 = input_back(h_own, grad1_low, near + far.astype(f32))
    grad_got = flip(pick(grad1_low, grad0.astype(bf16)), "section")

    activations = jnp.stack(ordered(pick(middle, final), act_got))
    input_grads = jnp.stack(ordered(pick(grad0, grad1_low.astype(f32)), grad_got.astype(f32)))

    def settled(one, two):
        got = flip(pick(two, one), "section")
        return [piece.astype(f32) for piece in ordered(pick(one, two), got)]

    rest_g = settled(reduced_rest0, reduced_rest1)
    qkv_g = settled(reduced_qkv0, reduced_qkv1)
    qkv_grad = jnp.concatenate([piece.reshape(-1, 3, heads // 2) for piece in qkv_g], 2)
    in_grad = jnp.concatenate([piece[:, :in_cols] for piece in rest_g], 1)
    dense_grad = jnp.concatenate([piece[:, in_cols : in_cols + heads // 2].T for piece in rest_g], 0)
    out_grad = jnp.concatenate([piece[:, in_cols + heads // 2 :].T for piece in rest_g], 0)

    total = small_sum
    total = total[0] + flip(total[1], "tensor", 2)
    sums = lax.psum_scatter(total, "dp", scatter_dimension=0) if not direct else None
    if direct:
        total = chosen(total, slots, 0)
        got = [lax.ppermute(total[hop], "dp", [(i, (i - hop) % n_dp) for i in range(n_dp)]) for hop in range(1, n_dp)]
        sums = sum(got, total[0])
    return (
        activations[None],
        input_grads[None],
        qkv_grad[None],
        sums[5 * part : 8 * part].reshape(1, 3, part),
        dense_grad[None],
        in_grad[None],
        sums[8 * part :].reshape(1, -1),
        out_grad[None],
        sums[: 2 * part].reshape(1, 2, part),
        sums[2 * part : 4 * part].reshape(1, 2, part),
        jnp.stack([sums[4 * part : 5 * part]] * 2)[None],
    )


def solution(mesh):
    placed = (
        P("dp", "tensor", None),
        P("dp", "tensor", None),
        P("dp", None),
        P("section", "dp", None, "tensor"),
        P("section", None, ("tensor", "dp")),
        P("section", "tensor", "dp"),
        P("section", "dp", "tensor"),
        P("section", ("tensor", "dp")),
        P("section", "tensor", "dp"),
        P("section", None, ("tensor", "dp")),
        P("section", None, ("tensor", "dp")),
        P("section", None, ("tensor", "dp")),
    )
    return jax.shard_map(
        shards,
        mesh=mesh,
        in_specs=placed,
        out_specs=(
            P("section", "dp", "tensor", None),
            P("section", "dp", "tensor", None),
            P("section", "dp", None, "tensor"),
            P("section", None, ("tensor", "dp")),
            P("section", "tensor", "dp"),
            P("section", "dp", "tensor"),
            P("section", ("tensor", "dp")),
            P("section", "tensor", "dp"),
            P("section", None, ("tensor", "dp")),
            P("section", None, ("tensor", "dp")),
            P("section", None, ("tensor", "dp")),
        ),
        check_vma=False,
    )
```

```python
import functools
import math

import jax
import jax.numpy as jnp
from jax import lax
from jax.experimental import pallas as pl
from jax.experimental.pallas import tpu as pltpu
from jax.sharding import PartitionSpec as P

HDIM = 64
EPSILON = 1e-05
TILE = 512
KEYS = 512
NT = (((1,), (1,)), ((), ()))
NN = (((1,), (0,)), ((), ()))
TN = (((0,), (0,)), ((), ()))
LOG2E = math.log2(math.e)
FAR = 1e15
HURRY = 0.05
LIMIT = pltpu.CompilerParams(vmem_limit_bytes=20 * 2**20)


def mm(a, b, dims=NN):
    return lax.dot_general(a, b, dims, preferred_element_type=jnp.float32)


def cost(flops, moved, special=0):
    return pl.CostEstimate(flops=int(flops * HURRY), bytes_accessed=int(moved * HURRY), transcendentals=int(special))


def flip(block, axis, bit=1):
    return lax.ppermute(block, axis, [(i, i ^ bit) for i in range(lax.axis_size(axis))])


def turn(values, cosine, lead, trail):
    return values * cosine + pltpu.roll(values, 120, 1) * lead + pltpu.roll(values, 8, 1) * trail


def turn_back(grads, cosine, lead, trail):
    return grads * cosine - pltpu.roll(grads, 120, 1) * lead - pltpu.roll(grads, 8, 1) * trail


def head_part(block, head):
    lane = lax.broadcasted_iota(jnp.int32, block.shape, 1)
    return jnp.where((lane >= head * 64) & (lane < head * 64 + 64), block, jnp.zeros_like(block))


def tile_at(table, tile, size, shard_rows):
    per = shard_rows // size
    return pl.multiple_of(table[tile // per] * shard_rows + tile % per * size, size)


def below(query_tile, key_tile, keys, queries):
    rows = lax.broadcasted_iota(jnp.int32, (keys, queries), 0) + key_tile * keys
    cols = lax.broadcasted_iota(jnp.int32, (keys, queries), 1) + query_tile * queries
    return rows <= cols


def attend_kernel(shard_rows, table, q_ref, k_ref, v_ref, fq_ref, fk_ref, out_ref, lse_ref, vt, wides, tops, totals):
    step = pl.program_id(0)

    @pl.when(step == 0)
    def _():
        flipped = v_ref[...].T
        for head in range(2):
            vt[head, 0:64, :] = flipped[head * 64 : head * 64 + 64, :]
            vt[head, 64:80, :] = jnp.ones((16, flipped.shape[1]), jnp.bfloat16)

    for head in range(2):
        wides[head, :, 0:128] = head_part(q_ref[...], head)
        wides[head, :, 128:256] = fq_ref[...]
    tops[...] = jnp.full(tops.shape, -3e38, jnp.float32)
    totals[...] = jnp.zeros_like(totals)

    def tile(index, masked):
        at = tile_at(table, index, KEYS, shard_rows)
        keys = jnp.concatenate([k_ref[pl.ds(at, KEYS), :], fk_ref[pl.ds(at, KEYS), :]], 1)
        blocks = [mm(keys, wides[head], NT) for head in range(2)]
        blocks = [block * LOG2E for block in blocks]
        if masked:
            seen = below(step, index, KEYS, TILE)
            blocks = [jnp.where(seen, block, -1e30) for block in blocks]
        news = [jnp.maximum(tops[head], jnp.max(blocks[head], 0, keepdims=True)) for head in range(2)]
        probs = [jnp.exp2(blocks[head] - news[head]).astype(jnp.bfloat16) for head in range(2)]
        terms = [mm(vt[head, :, pl.ds(at, KEYS)], probs[head], NN) for head in range(2)]
        for head in range(2):
            totals[head] = totals[head] * jnp.exp2(tops[head] - news[head]) + terms[head]
            tops[head] = news[head]

    def loop(index, carry):
        tile(index, False)
        return carry

    whole = step * TILE // KEYS
    lax.fori_loop(0, whole, loop, 0)
    tile(whole, True)
    outs = []
    for head in range(2):
        norm = totals[head, 64:65, :]
        outs.append(totals[head, 0:64, :] / norm)
        lse_ref[head : head + 1, :] = tops[head] + jnp.log2(norm)
    lse_ref[2:8, :] = jnp.zeros((6, TILE), jnp.float32)
    out_ref[...] = jnp.concatenate(outs, 0).T.astype(jnp.bfloat16)


def attend(table, qkv, fq, fk):
    seq = qkv.shape[0]
    shard_rows = seq // 4
    per = shard_rows // TILE

    def place(step, table):
        return table[step // per] * per + step % per

    return pl.pallas_call(
        functools.partial(attend_kernel, shard_rows),
        grid_spec=pltpu.PrefetchScalarGridSpec(
            num_scalar_prefetch=1,
            grid=(seq // TILE,),
            in_specs=[
                pl.BlockSpec((TILE, 128), lambda i, t: (place(i, t), 0)),
                pl.BlockSpec((seq, 128), lambda i, t: (0, 1)),
                pl.BlockSpec((seq, 128), lambda i, t: (0, 2)),
                pl.BlockSpec((TILE, 128), lambda i, t: (place(i, t), 0)),
                pl.BlockSpec((seq, 128), lambda i, t: (0, 0)),
            ],
            out_specs=[
                pl.BlockSpec((TILE, 128), lambda i, t: (place(i, t), 0)),
                pl.BlockSpec((8, TILE), lambda i, t: (0, place(i, t))),
            ],
            scratch_shapes=[
                pltpu.VMEM((2, 80, seq), jnp.bfloat16),
                pltpu.VMEM((2, TILE, 256), jnp.bfloat16),
                pltpu.VMEM((2, 1, TILE), jnp.float32),
                pltpu.VMEM((2, 80, TILE), jnp.float32),
            ],
        ),
        out_shape=[
            jax.ShapeDtypeStruct((seq, 128), jnp.bfloat16),
            jax.ShapeDtypeStruct((8, seq), jnp.float32),
        ],
        compiler_params=LIMIT,
        cost_estimate=cost(4e9, 3e6, 5e6),
        name="attend",
    )(table, qkv, qkv, qkv, fq, fk)


def attend_back_kernel(shard_rows, table, q_ref, k_ref, v_ref, gm_ref, o_ref, lse_ref, fq_ref, fk_ref,
                       cos_ref, lead_ref, trail_ref, out_ref, kt, dk, dv, wides, grads, deltas, dq):
    step = pl.program_id(0)
    last = pl.num_programs(0) - 1 - step

    @pl.when(step == 0)
    def _():
        kt[...] = k_ref[...].T
        dk[...] = jnp.zeros_like(dk)
        dv[...] = jnp.zeros_like(dv)

    grad = gm_ref[...]
    product = grad.astype(jnp.float32) * o_ref[...].astype(jnp.float32)
    high = product.astype(jnp.bfloat16)
    low = (product - high.astype(jnp.float32)).astype(jnp.bfloat16)
    lane = lax.broadcasted_iota(jnp.int32, (8, 128), 1)
    for head in range(2):
        ones = jnp.where((lane >= head * 64) & (lane < head * 64 + 64), 1.0, 0.0).astype(jnp.bfloat16)
        deltas[head] = (mm(ones, high, NT) + mm(ones, low, NT))[0:1, :]
        wides[head, :, 0:128] = head_part(q_ref[...], head)
        wides[head, :, 128:256] = fq_ref[...]
        grads[head] = head_part(grad, head)
    dq[...] = jnp.zeros_like(dq)

    def tile(index, masked):
        at = tile_at(table, index, KEYS, shard_rows)
        rows = pl.ds(at, KEYS)
        keys = jnp.concatenate([k_ref[rows, :], fk_ref[rows, :]], 1)
        values = v_ref[rows, :]
        blocks = [mm(keys, wides[head], NT) for head in range(2)]
        backs = [mm(values, grads[head], NT) for head in range(2)]
        probs = [jnp.exp2(blocks[head] * LOG2E - lse_ref[head : head + 1, :]) for head in range(2)]
        if masked:
            seen = below(last, index, KEYS, TILE)
            probs = [jnp.where(seen, one, 0.0) for one in probs]
        slopes = [(probs[head] * (backs[head] - deltas[head])).astype(jnp.bfloat16) for head in range(2)]
        probs = [one.astype(jnp.bfloat16) for one in probs]
        dv[rows, :] += mm(jnp.concatenate(probs, 1), grads[...].reshape(2 * TILE, 128), NN)
        dk[rows, :] += mm(jnp.concatenate(slopes, 1), wides[:, :, 0:128].reshape(2 * TILE, 128), NN)
        for head in range(2):
            dq[head * 64 : head * 64 + 64, :] += mm(kt[head * 64 : head * 64 + 64, rows], slopes[head], NN)

    def loop(index, carry):
        tile(index, False)
        return carry

    whole = last * TILE // KEYS
    lax.fori_loop(0, whole, loop, 0)
    tile(whole, True)
    here = pl.ds(tile_at(table, last, TILE, shard_rows), TILE)
    turns = (cos_ref[...], lead_ref[...], trail_ref[...])
    out_ref[:, 0:128] = turn_back(dq[...].T * 0.125, *turns).astype(jnp.bfloat16)
    out_ref[:, 128:256] = turn_back(dk[here, :], *turns).astype(jnp.bfloat16)
    out_ref[:, 256:384] = dv[here, :].astype(jnp.bfloat16)


def attend_back(table, qkv, grad_mixed, mixed, lse, fq, fk, turns):
    seq = qkv.shape[0]
    shard_rows = seq // 4
    tiles = seq // TILE
    per = shard_rows // TILE

    def place(step, table):
        tile = tiles - 1 - step
        return table[tile // per] * per + tile % per

    block = pl.BlockSpec((TILE, 128), lambda i, t: (place(i, t), 0))
    return pl.pallas_call(
        functools.partial(attend_back_kernel, shard_rows),
        grid_spec=pltpu.PrefetchScalarGridSpec(
            num_scalar_prefetch=1,
            grid=(tiles,),
            in_specs=[
                block,
                pl.BlockSpec((seq, 128), lambda i, t: (0, 1)),
                pl.BlockSpec((seq, 128), lambda i, t: (0, 2)),
                block,
                block,
                pl.BlockSpec((8, TILE), lambda i, t: (0, place(i, t))),
                block,
                pl.BlockSpec((seq, 128), lambda i, t: (0, 0)),
                block,
                block,
                block,
            ],
            out_specs=pl.BlockSpec((TILE, 384), lambda i, t: (place(i, t), 0)),
            scratch_shapes=[
                pltpu.VMEM((128, seq), jnp.bfloat16),
                pltpu.VMEM((seq, 128), jnp.float32),
                pltpu.VMEM((seq, 128), jnp.float32),
                pltpu.VMEM((2, TILE, 256), jnp.bfloat16),
                pltpu.VMEM((2, TILE, 128), jnp.bfloat16),
                pltpu.VMEM((2, 1, TILE), jnp.float32),
                pltpu.VMEM((128, TILE), jnp.float32),
            ],
        ),
        out_shape=pltpu.HBM((seq, 384), jnp.bfloat16),
        compiler_params=LIMIT,
        cost_estimate=cost(10e9, 6e6, 5e6),
        name="attend_back",
    )(table, qkv, qkv, qkv, grad_mixed, mixed, lse, fq, fk, *turns)


def normal_of(values):
    centered = values - jnp.mean(values, -1, keepdims=True)
    inverse = lax.rsqrt(jnp.mean(centered * centered, -1, keepdims=True) + EPSILON)
    return centered * inverse, inverse


def whole_of(array):
    return pl.BlockSpec(array.shape, lambda *i: (0,) * array.ndim)


def heads_of(first, weight, bias, turns, out_ref):
    projected = mm(first, weight) + bias
    for part in range(3):
        piece = projected[:, 128 * part : 128 * part + 128]
        if part < 2:
            piece = turn(piece, *turns)
        if part == 0:
            piece = piece * 0.125
        out_ref[:, 128 * part : 128 * part + 128] = piece.astype(jnp.bfloat16)


def settle(slots, source, target, start=0):
    @pl.when(pl.program_id(0) == 0)
    def _():
        rows = target.shape[0] // source.shape[0]
        for block in range(source.shape[0]):
            target[block * rows : block * rows + rows, :] = source[slots[block], 0:rows, start : start + target.shape[1]]


def weight_scratch(width, weight, cols=None):
    return pltpu.VMEM((width, cols or weight.shape[2]), weight.dtype)


def choose(pieces, target):
    for step, piece in enumerate(pieces):

        @pl.when(pl.program_id(0) == step)
        def _():
            target[...] = piece[...]


def call(kernel, name, grid, in_specs, out_specs, out_shape, scratch, flops, moved, special=0, scalars=1, aliases=None):
    return pl.pallas_call(
        kernel,
        grid_spec=pltpu.PrefetchScalarGridSpec(
            num_scalar_prefetch=scalars, grid=grid, in_specs=in_specs, out_specs=out_specs, scratch_shapes=scratch
        ),
        out_shape=out_shape,
        compiler_params=LIMIT,
        cost_estimate=cost(flops, moved, special),
        input_output_aliases=aliases or {},
        name=name,
    )


def struct(*shape, far=False):
    return pltpu.HBM(shape, jnp.bfloat16) if far else jax.ShapeDtypeStruct(shape, jnp.bfloat16)


def stay(*arrays):
    return [pltpu.with_memory_space_constraint(array, pltpu.HBM) for array in arrays]


def project_kernel(
    slots, h0, h1, h2, h3, weight_ref, bias_ref, norm_ref, cos_ref, lead_ref, trail_ref,
    out_ref, first_ref, second_ref, flip_ref, weight, h_ref
):
    settle(slots, weight_ref, weight)
    choose((h0, h1, h2, h3), h_ref)
    normal, _ = normal_of(h_ref[...].astype(jnp.float32))
    flip_ref[...] = normal.astype(jnp.bfloat16).T
    first = (normal * norm_ref[0:1, :] + norm_ref[2:3, :]).astype(jnp.bfloat16)
    first_ref[...] = first
    second_ref[...] = (normal * norm_ref[1:2, :] + norm_ref[3:4, :]).astype(jnp.bfloat16)
    heads_of(first, weight[...], bias_ref[0:1, 0 : weight.shape[1]], (cos_ref[...], lead_ref[...], trail_ref[...]), out_ref)


def project(slots, pieces, weight, cols, bias, norms, turns, far=False):
    rows, width = pieces[0].shape
    seq = rows * len(pieces)
    block = pl.BlockSpec((rows, width), lambda i, s: (i, 0))
    return call(
        project_kernel,
        "project",
        (seq // rows,),
        [whole_of(x) for x in (*pieces, weight, bias, norms)] + [pl.BlockSpec((rows, 128), lambda i, s: (i, 0))] * 3,
        [pl.BlockSpec((rows, cols), lambda i, s: (i, 0)), block, block, pl.BlockSpec((width, rows), lambda i, s: (0, i))],
        [struct(seq, cols)] + [struct(*shape, far=far) for shape in ((seq, width), (seq, width), (width, seq))],
        [weight_scratch(width, weight, cols), pltpu.VMEM((rows, width), jnp.bfloat16)],
        4e9,
        18e6,
    )(slots, *pieces, weight, bias, norms, *turns)


def project_more_kernel(slots, first_ref, weight_ref, bias_ref, cos_ref, lead_ref, trail_ref, out_ref, weight):
    settle(slots, weight_ref, weight)
    heads_of(
        first_ref[...], weight[...], bias_ref[1:2, 0 : weight.shape[1]], (cos_ref[...], lead_ref[...], trail_ref[...]), out_ref
    )


def project_more(slots, first, weight, cols, bias, turns):
    seq, width = first.shape
    rows = 512
    return call(
        project_more_kernel,
        "project_more",
        (seq // rows,),
        [pl.BlockSpec((rows, width), lambda i, s: (i, 0)), whole_of(weight), whole_of(bias)]
        + [pl.BlockSpec((rows, 128), lambda i, s: (i, 0))] * 3,
        pl.BlockSpec((rows, cols), lambda i, s: (i, 0)),
        struct(seq, cols),
        [weight_scratch(width, weight, cols)],
        3e9,
        8e6,
    )(slots, first, weight, bias, *turns)


def gelu_kernel(part, slots, a_ref, weight_ref, bias_ref, out_ref, slope_ref, weight):
    settle(slots, weight_ref, weight, weight_ref.shape[2] - weight.shape[1])
    inner = mm(a_ref[...], weight[...]) + bias_ref[part : part + 1, bias_ref.shape[1] - weight.shape[1] :]
    size = jnp.abs(inner)
    t = 1.0 / (1.0 + (0.3275911 * math.sqrt(0.5)) * size)
    bell = jnp.exp2((-0.5 * LOG2E) * inner * inner)
    poly = 0.5 * 1.061405429 * t + 0.5 * -1.453152027
    poly = poly * t + 0.5 * 1.421413741
    poly = poly * t + 0.5 * -0.284496736
    poly = poly * t + 0.5 * 0.254829592
    tail = poly * t * bell
    below = jnp.where(inner >= 0, 1.0 - tail, tail)
    out_ref[...] = (inner * below).astype(jnp.bfloat16)
    slope_ref[...] = (below + inner * bell * (1.0 / math.sqrt(2 * math.pi))).astype(jnp.bfloat16)


def gelu_up(slots, second, weight, cols, bias, part, far=False):
    seq, width = second.shape
    rows = 256
    block = pl.BlockSpec((rows, cols), lambda i, s: (i, 0))
    return call(
        functools.partial(gelu_kernel, part),
        "gelu_up",
        (seq // rows,),
        [pl.BlockSpec((rows, width), lambda i, s: (i, 0)), whole_of(weight), whole_of(bias)],
        [block, block],
        [struct(seq, cols), struct(seq, cols, far=far)],
        [weight_scratch(width, weight, cols)],
        5e9,
        10e6,
        2e6,
    )(slots, second, weight, bias)


def deal(value, *targets):
    for step, target in enumerate(targets):

        @pl.when(pl.program_id(0) == step)
        def _():
            target[...] = value


def down_kernel(slots, mixed_mine, mixed_other, act_mine, act_other, mine_ref, other_ref, near_ref, beside_ref, mine, other):
    settle(slots, mine_ref, mine)
    settle(slots, other_ref, other)
    heads = mixed_mine.shape[1]
    total = mm(mixed_mine[...], mine[:, 0:heads], NT) + mm(act_mine[...], mine[:, heads:], NT)
    total += mm(mixed_other[...], other[:, 0:heads], NT) + mm(act_other[...], other[:, heads:], NT)
    deal(total.astype(jnp.bfloat16), near_ref, beside_ref)


def down(slots, mixed, act, weights, half):
    seq = mixed[0].shape[0]
    width = weights[0].shape[0] * weights[0].shape[1]
    rows = 512
    steps = seq // rows // 2
    return call(
        down_kernel,
        "down",
        (steps,),
        [pl.BlockSpec((rows, x.shape[1]), lambda i, s: (i + half * steps, 0)) for x in (*mixed, *act)]
        + [whole_of(w) for w in weights],
        [pl.BlockSpec((rows, width), lambda i, s: (0, 0))] * 2,
        [struct(rows, width)] * 2,
        [weight_scratch(width, w) for w in weights],
        4e9,
        8e6,
    )(slots, *mixed, *act, *weights)


def down_back_kernel(
    slots, g0, g1, g2, g3, slope_mine, slope_other, mine_ref, other_ref,
    mixed_mine, mixed_other, inner_mine, inner_other, flip_ref, mine, other, grad_ref
):
    choose((g0, g1, g2, g3), grad_ref)
    settle(slots, mine_ref, mine)
    settle(slots, other_ref, other)
    heads = mixed_mine.shape[1]
    flip_ref[...] = grad_ref[...].T
    for slope, weight, mixed, inner in (
        (slope_mine, mine, mixed_mine, inner_mine),
        (slope_other, other, mixed_other, inner_other),
    ):
        mixed[...] = mm(grad_ref[...], weight[:, 0:heads]).astype(jnp.bfloat16)
        inner[...] = (mm(grad_ref[...], weight[:, heads:]) * slope[...].astype(jnp.float32)).astype(jnp.bfloat16)


def down_back(slots, pieces, slopes, weights, heads, far=False):
    rows, width = pieces[0].shape
    seq = rows * len(pieces)
    hidden = slopes[0].shape[1]
    wide = pl.BlockSpec((rows, hidden), lambda i, s: (i, 0))
    return call(
        down_back_kernel,
        "down_back",
        (seq // rows,),
        [whole_of(x) for x in pieces] + [wide, wide] + [whole_of(w) for w in weights],
        [pl.BlockSpec((rows, heads), lambda i, s: (i, 0))] * 2 + [wide, wide, pl.BlockSpec((width, rows), lambda i, s: (0, i))],
        [struct(seq, heads)] * 2 + [struct(seq, hidden, far=far)] * 2 + [struct(width, seq, far=far)],
        [weight_scratch(width, w) for w in weights] + [pltpu.VMEM((rows, width), jnp.bfloat16)],
        8e9,
        18e6,
    )(slots, *pieces, *slopes, *weights)


def up_back_kernel(
    slots, in_slots, proj_mine, proj_other, inner_mine, inner_other, qkv_mine, qkv_other, in_mine, in_other, gain_ref, near_ref, beside_ref, *weights
):
    for source, target in zip((qkv_mine, qkv_other), weights[:2]):
        settle(slots, source, target)
    for source, target in zip((in_mine, in_other), weights[2:]):
        settle(in_slots, source, target, source.shape[2] - target.shape[1])
    qkv_a, qkv_b, in_a, in_b = weights
    first = mm(proj_mine[...], qkv_a[...], NT) + mm(proj_other[...], qkv_b[...], NT)
    second = mm(inner_mine[...], in_a[...], NT) + mm(inner_other[...], in_b[...], NT)
    deal((first * gain_ref[0:1, :] + second * gain_ref[1:2, :]).astype(jnp.bfloat16), near_ref, beside_ref)


def up_back(slots, proj, inner, qkv_w, in_w, gains, half):
    seq = proj[0].shape[0]
    width = gains.shape[1]
    rows = 512
    steps = seq // rows // 2
    return call(
        up_back_kernel,
        "up_back",
        (steps,),
        [pl.BlockSpec((rows, x.shape[1]), lambda i, *s: (i + half * steps, 0)) for x in (*proj, *inner)]
        + [whole_of(w) for w in (*qkv_w, *in_w, gains)],
        [pl.BlockSpec((rows, width), lambda i, *s: (0, 0))] * 2,
        [struct(rows, width)] * 2,
        [weight_scratch(width, w, x.shape[1]) for w, x in zip((*qkv_w, *in_w), (*proj, *inner))],
        4e9,
        10e6,
        scalars=2,
    )(*slots, *proj, *inner, *qkv_w, *in_w, gains)


def grads_kernel(ups, downs, adds, slots, *refs):
    refs = list(refs)
    normal = refs.pop(0) if ups else None
    flipped = refs.pop(0) if downs else None
    backs = [refs.pop(0) for _ in range(ups)]
    sources = [refs.pop(0) for _ in range(downs)]
    weights = [refs.pop(0) for _ in range(ups)]
    norm_ref = refs.pop(0)
    got_ref = refs.pop(0) if adds else None
    out_ref = refs.pop(0)
    row = 1 if downs else 0
    norm = norm_ref[...].T
    gain_column, bias_column = norm[:, row : row + 1], norm[:, 2 + row : 3 + row]

    def store(first, last, value):
        if adds:
            value += got_ref[0, :, first:last].astype(jnp.float32)
        out_ref[0, :, first:last] = value.astype(jnp.bfloat16)

    at = 0
    for k in range(ups):
        stat_ref, sum_ref = refs[2 * k : 2 * k + 2]
        cols = backs[k].shape[1]
        raw = mm(normal[...], backs[k][...])
        total = mm(jnp.ones((8, backs[k].shape[0]), jnp.bfloat16), backs[k][...])
        sum_ref[...] = total
        total = total[0:1, :]
        store(at, at + cols, raw * gain_column + total * bias_column)
        first = weights[k].shape[2] - cols if downs else 0
        wide = weights[k][0, :, first : first + cols].astype(jnp.float32)
        gain = jnp.sum(raw * wide, 1, keepdims=True)
        shift = jnp.sum(wide * total, 1, keepdims=True)
        lane = lax.broadcasted_iota(jnp.int32, (raw.shape[0], 128), 1)
        stat_ref[...] = jnp.where(lane == 0, gain, jnp.where(lane == 1, shift, 0.0)).T[0:8, :]
        at += cols
    for source in sources:
        cols = source.shape[1]
        store(at, at + cols, mm(flipped[...], source[...]))
        at += cols


def weight_grads(slots, normal, flipped, ups, downs, norms, got=None):
    width, seq = (normal if ups else flipped).shape
    groups = 4
    rows = width // groups
    strip = pl.BlockSpec((rows, seq), lambda i, s: (i, 0))
    args, specs = [], []
    for array, used in ((normal, ups), (flipped, downs)):
        if used:
            args.append(array)
            specs.append(strip)
    for array in [back for back, _ in ups] + list(downs):
        args.append(array)
        specs.append(whole_of(array))
    for _, weight in ups:
        args.append(weight)
        specs.append(pl.BlockSpec((1, rows, weight.shape[2]), lambda i, s: (s[i], 0, 0)))
    args.append(norms)
    specs.append(pl.BlockSpec((norms.shape[0], rows), lambda i, s: (0, i)))
    cols = sum(back.shape[1] for back, _ in ups) + sum(source.shape[1] for source in downs)
    out_specs = [pl.BlockSpec((1, rows, cols), lambda i, s: (i, 0, 0))]
    if got is not None:
        args.append(got)
        specs.append(out_specs[0])
    out_shape = [struct(groups, rows, cols, far=True)]
    for back, _ in ups:
        out_specs += [pl.BlockSpec((8, rows), lambda i, s: (0, i)), pl.BlockSpec((8, back.shape[1]), lambda i, s: (0, 0))]
        out_shape += [pltpu.HBM((8, width), jnp.float32), pltpu.HBM((8, back.shape[1]), jnp.float32)]
    return call(
        functools.partial(grads_kernel, len(ups), len(downs), got is not None),
        "weight_grads",
        (groups,),
        specs,
        out_specs,
        out_shape,
        [],
        2 * seq * width * cols,
        8e6,
    )(slots, *args)


def shards(
    inputs,
    cotangent,
    lengths,
    qkv_weight,
    qkv_bias,
    dense_weight,
    in_weight,
    in_bias,
    out_weight,
    norm_gains,
    norm_biases,
    out_biases,
):
    f32, bf16 = jnp.float32, jnp.bfloat16
    lefthand = lax.axis_index("section") == 0
    me, depth = lax.axis_index("tensor"), lax.axis_index("dp")
    n_tensor, n_dp = lax.axis_size("tensor"), lax.axis_size("dp")
    shard_rows, width = inputs.shape[1:]
    heads = qkv_weight.shape[3]
    hidden = in_weight.shape[2]
    groups = 4
    direct = n_dp == groups

    def pick(first, second):
        return jnp.where(lefthand, first, second)

    def ordered(mine, other):
        return pick(mine, other), pick(other, mine)

    def gather_deep(piece):
        if not direct:
            return lax.all_gather(piece, "dp", axis=0, tiled=True).reshape(groups, -1, piece.shape[1])
        pieces = [piece]
        for hop in range(1, n_dp):
            pieces.append(lax.ppermute(piece, "dp", [(i, (i + hop) % n_dp) for i in range(n_dp)]))
        return jnp.stack(pieces)

    def scatter_late(total):
        return lax.psum_scatter(total.reshape(-1, total.shape[2]), "dp", scatter_dimension=0, tiled=True)

    def pin(*values):
        return lax.optimization_barrier(values)

    h_own = pick(inputs[0], inputs[1])
    cot = pick(cotangent[0], cotangent[1])
    row = pick(lengths[0], lengths[1])

    def halves(group):
        return pick(group[0], group[1]), pick(group[1], group[0])

    def cut(array, axis, k):
        size = array.shape[axis] // 2
        return lax.slice_in_dim(array, k * size, k * size + size, axis=axis)

    small = jnp.concatenate([piece[0].reshape(-1) for piece in (qkv_bias, norm_gains, norm_biases, out_biases, in_bias)])
    part = qkv_bias.shape[2]
    n_small = small.shape[0]
    qkv_cols, in_cols = 3 * heads // 2, hidden // 2
    qkv_half = halves([cut(qkv_weight[0], 2, k).reshape(-1, qkv_cols) for k in range(2)])
    qkv_got = flip(qkv_half[1], "section")
    pair = jnp.stack([small, flip(small, "tensor", 2)])
    h_own, pair = pin(h_own, pair)
    h_far = flip(h_own, "tensor", 2)
    pair = jnp.stack([pair, flip(pair, "tensor", 1)], 1)
    pair = jnp.stack(ordered(pair, flip(pair, "section"))).reshape(-1)
    extra = -(-pair.shape[0] // (16 * qkv_cols)) * 16
    pair = jnp.zeros((extra * qkv_cols,), bf16).at[: pair.shape[0]].set(pair).reshape(extra, qkv_cols)
    deep = qkv_half[0].shape[0]
    qkv_shard = ordered(qkv_half[0], qkv_got)
    first = jnp.concatenate([qkv_shard[0], pair], 0)
    zero = jnp.zeros((), jnp.int32)
    first, row, zero, cot, in_weight, dense_weight, out_weight = pin(
        first, row, zero, cot, in_weight, dense_weight, out_weight
    )
    rest_half = halves(
        [
            jnp.concatenate([cut(in_weight[0], 1, k), cut(dense_weight[0], 0, k).T, cut(out_weight[0], 0, k).T], 1)
            for k in range(2)
        ]
    )
    first = gather_deep(first) if direct else lax.all_gather(first, "dp", axis=0)

    steps = zero + jnp.arange(groups, dtype=jnp.int32)
    slots = (depth - steps) % groups if direct else steps
    rest_mine, rest_got = rest_half[0], flip(rest_half[1], "section")
    qkv0 = first if direct else first[:, :deep].reshape(groups, -1, qkv_cols)
    pair = first[:, deep:].reshape(n_dp, -1)[:, : 2 * n_tensor * n_small].reshape(n_dp, 2, n_tensor, n_small)
    order = (zero + jnp.arange(n_tensor)) ^ me
    small_all = pair.astype(f32).transpose(1, 2, 0, 3)

    def chosen(array, index, axis):
        size = index.shape[0]
        shape = [1] * array.ndim
        shape[axis] = size
        return sum(
            jnp.where(index.reshape(shape) == place, lax.slice_in_dim(array, place, place + 1, axis=axis), 0.0)
            for place in range(size)
        )

    if direct:
        small_all = chosen(small_all, slots, 2)
    here = small_all[:, 0]
    small_all = chosen(small_all, order, 1)

    def gather_early(piece):
        return lax.all_gather(piece, "dp", axis=0, tiled=True).reshape(groups, -1, piece.shape[1])

    def shares(rest):
        return rest[:, :in_cols], rest[:, in_cols:]

    table = jnp.arange(n_tensor, dtype=jnp.int32) ^ me
    positions = jnp.concatenate(
        [slot * shard_rows + zero + jnp.arange(shard_rows, dtype=jnp.int32) for slot in (me, me ^ 1, me ^ 2, me ^ 3)]
    )
    ends = jnp.cumsum(row)
    passed = positions[:, None] >= ends[None, :]
    doc = jnp.sum(passed.astype(jnp.int32), -1)
    offset = positions - jnp.sum(jnp.where(passed, row[None, :], 0), -1)
    valid_own = (positions < ends[-1])[:shard_rows]
    lane = jnp.arange(128, dtype=jnp.int32) + zero
    same = doc[:, None] == lane[None, :]
    feats_q = jnp.where(same, -FAR, 0.0).astype(bf16)
    feats_k = jnp.where(same | (lane[None, :] > row.shape[0]), 0.0, FAR).astype(bf16)
    place = lane % HDIM
    rotary = HDIM // 4
    counter = (place % (rotary // 2)).astype(f32)
    inverse = jnp.exp(counter * (-2.0 * math.log(10000.0) / rotary))
    angles = offset.astype(f32)[:, None] * inverse[None, :]
    turned = (place < rotary)[None, :]
    sine = jnp.sin(angles)
    rotary_turns = (
        jnp.where(turned, jnp.cos(angles), 1.0),
        jnp.where((place < rotary // 2)[None, :], -sine, 0.0),
        jnp.where(turned & (place >= rotary // 2)[None, :], sine, 0.0),
    )

    rows_all = small_all[..., 3 * part : 9 * part].reshape(2, n_tensor, n_dp, 6, part).transpose(0, 3, 1, 2, 4)
    rows_all = jnp.pad(rows_all.reshape(2, 6, width), ((0, 0), (0, 2), (0, 0)))
    qkv_parts = here[..., : 3 * part].reshape(2, n_dp, 3, part).transpose(0, 2, 1, 3).reshape(2, 3, 2, heads // 2)
    qkv_parts = qkv_parts.transpose(0, 2, 1, 3).reshape(2, 2, qkv_cols)
    bias_all = jnp.concatenate([qkv_parts, here[..., 9 * part : n_small].reshape(2, 2, in_cols)], 2)
    bias_all = jnp.stack(ordered(bias_all[:, 0], bias_all[:, 1]), 1)

    def chip_sum(terms):
        return terms[0].astype(f32) + flip(terms[1], "tensor", 1).astype(f32)

    def branch_sum(make):
        far = chip_sum(make(1)).astype(bf16)
        return chip_sum(make(0)), far

    def result_of(own, near, far, rows):
        return (own.astype(f32) + near + far.astype(f32) + rows[4:5] + rows[5:6]).astype(bf16)

    def input_back(own, grad_own, partial):
        n, inverse = normal_of(own.astype(f32))
        return grad_own.astype(f32) + inverse * (
            partial - jnp.mean(partial, -1, keepdims=True) - n * jnp.mean(partial * n, -1, keepdims=True)
        )

    def attend_one(qkv):
        return attend(table, qkv, feats_q, feats_k)

    def attend_back_one(qkv, attended, grad_mixed):
        mixed, lse = attended
        return attend_back(table, qkv, grad_mixed, mixed, lse, feats_q, feats_k, stay(*rotary_turns))

    def rows_of(own, far):
        return own, flip(own, "tensor", 1), far, flip(far, "tensor", 1)

    in_shard0 = pick(rest_mine[:, :in_cols], rest_got[:, :in_cols])
    qkv0, rows_all, bias_all, in_shard0, *h_all = pin(qkv0, rows_all, bias_all, in_shard0, *rows_of(h_own, h_far))
    in0 = gather_deep(in_shard0)
    (norms0, norms1), (bias0, bias1) = rows_all, bias_all
    qkv0_other = flip(qkv0, "section")
    qkv_a0, normed, second, normal0 = project(slots, h_all, qkv0, qkv_cols, bias0, norms0, rotary_turns, True)
    qkv_a0, cot, rest_mine, rest_got = pin(qkv_a0, cot, rest_mine, rest_got)
    rest0, rest1 = ordered(rest_mine, rest_got)
    (_, out_shard0), (in_shard1, out_shard1) = shares(rest0), shares(rest1)
    grad2 = cot * valid_own[:, None].astype(bf16)
    grad2_far = flip(grad2, "tensor", 2)
    mixed_a0 = attend_one(qkv_a0)
    in0, qkv0_other, normed, out_shard0, *mixed_a0 = pin(in0, qkv0_other, normed, out_shard0, *mixed_a0)
    out0 = gather_early(out_shard0)
    in0_other = flip(in0, "section")
    qkv0 = stay(qkv0, qkv0_other)
    qkv_b0 = project_more(slots, *stay(normed), qkv0[1], qkv_cols, bias0, rotary_turns)
    mixed_b0 = attend_one(qkv_b0)
    second, grad2_far, in0_other, *mixed_b0 = pin(second, grad2_far, in0_other, *mixed_b0)
    in0 = stay(in0, in0_other)
    hid_a0 = gelu_up(slots, *stay(second), in0[0], in_cols, bias0, 0, True)
    grad_all1 = rows_of(grad2, grad2_far)
    second, out0, hid_a0, qkv_shard1 = pin(second, out0, hid_a0, qkv_shard[1])
    qkv1 = gather_deep(qkv_shard1)
    out0 = stay(out0, flip(out0, "section"))
    hid_b0 = gelu_up(slots, *stay(second), in0[1], in_cols, bias0, 1, True)
    mixed0 = (mixed_a0[0], mixed_b0[0])
    hid_b0, qkv1, in_shard1 = pin(hid_b0, qkv1, in_shard1)
    in1 = gather_early(in_shard1)
    far = chip_sum(down(steps, stay(*mixed0), stay(hid_a0[0], hid_b0[0]), out0, 1)).astype(bf16)
    far, mixed0, qkv1, *grad_all1 = pin(far, mixed0, qkv1, *grad_all1)
    qkv1_other = flip(qkv1, "section")
    near = chip_sum(down(steps, stay(*mixed0), stay(hid_a0[0], hid_b0[0]), out0, 0))
    middle = result_of(h_own, near, flip(far, "tensor", 2), norms0)
    middle, qkv1_other, out_shard1 = pin(middle, qkv1_other, out_shard1)
    out1 = gather_early(out_shard1)

    h_all = rows_of(middle, flip(middle, "tensor", 2))
    in1, *h_all = pin(in1, *h_all)
    in1_other = flip(in1, "section")
    qkv1 = (qkv1, qkv1_other)
    qkv_a1, normed, second, normal1 = project(slots, h_all, qkv1[0], qkv_cols, bias1, norms1, rotary_turns)
    mixed_a1 = attend_one(qkv_a1)
    normed, out1, in1_other, *mixed_a1 = pin(normed, out1, in1_other, *mixed_a1)
    in1 = (in1, in1_other)
    out1_other = flip(out1, "section")
    qkv_b1 = project_more(slots, normed, qkv1[1], qkv_cols, bias1, rotary_turns)
    mixed_b1 = attend_one(qkv_b1)
    second, *mixed_b1 = pin(second, *mixed_b1)
    hid_a1 = gelu_up(steps, second, in1[0], in_cols, bias1, 0)
    hid_b1 = gelu_up(steps, second, in1[1], in_cols, bias1, 1)
    mixed1 = (mixed_a1[0], mixed_b1[0])
    out1_other, hid_a1, hid_b1 = pin(out1_other, hid_a1, hid_b1)
    out1 = (out1, out1_other)

    gm_a, gm_b, gi_a1, gi_b1, flipped1 = down_back(steps, grad_all1, (hid_a1[1], hid_b1[1]), out1, heads // 2)

    def rest_grads(blocks, normal, flipped, gi, in_w, mixed, hid, norms, got=None):
        return weight_grads(blocks, normal, flipped, ((gi, in_w),), (mixed, hid[0]), norms, got)

    def qkv_grads(blocks, normal, gp, qkv_w, norms, got=None):
        return weight_grads(blocks, normal, None, ((*stay(gp), qkv_w),), (), norms, got)

    rest_b1 = rest_grads(steps, normal1, flipped1, gi_b1, in1[1], mixed1[1], hid_b1, norms1)
    gm_a, gm_b, rest_b1_grad = pin(gm_a, gm_b, rest_b1[0])
    rest_got1 = flip(rest_b1_grad, "section")
    gp_b1 = attend_back_one(qkv_b1, mixed_b1, gm_b)
    gm_a, gp_b1 = pin(gm_a, gp_b1)
    gp_a1 = attend_back_one(qkv_a1, mixed_a1, gm_a)
    gp_a1, rest_got1 = pin(gp_a1, rest_got1)
    near, far = branch_sum(lambda half: up_back((slots, steps), stay(gp_a1, gp_b1), stay(gi_a1, gi_b1), qkv1, in1, norms1, half))
    far, normal1, flipped1, rest_got1 = pin(far, normal1, flipped1, rest_got1)
    far = flip(far, "tensor", 2)
    rest_a1 = rest_grads(steps, normal1, flipped1, gi_a1, in1[0], mixed1[0], hid_a1, norms1, rest_got1)
    normal1, rest_a1_grad = pin(normal1, rest_a1[0])
    qkv_g_b1 = qkv_grads(slots, normal1, gp_b1, qkv1[1], norms1)
    normal1, qkv_b1_grad, mixed1_a, mixed1_b = pin(normal1, qkv_g_b1[0], *mixed1)
    qkv_got1 = flip(qkv_b1_grad, "section")
    final_far = chip_sum(down(steps, stay(mixed1_a, mixed1_b), stay(hid_a1[0], hid_b1[0]), stay(*out1), 1)).astype(bf16)
    far, normal1, rest_a1_grad = pin(far, normal1, rest_a1_grad)
    grad1 = input_back(middle, grad2, near + far.astype(f32))
    grad1_low = grad1.astype(bf16)
    grad1_low, rest_a1_grad, normal1, final_far, mixed1_a, mixed1_b = pin(
        grad1_low, rest_a1_grad, normal1, final_far, mixed1_a, mixed1_b
    )
    grad1_far = flip(grad1_low, "tensor", 2)
    reduced_rest1 = scatter_late(rest_a1_grad)
    near_terms = down(steps, stay(mixed1_a, mixed1_b), stay(hid_a1[0], hid_b1[0]), stay(*out1), 0)
    qkv_got1, normal1, *near_terms = pin(qkv_got1, normal1, *near_terms)
    qkv_g_a1 = qkv_grads(slots, normal1, gp_a1, qkv1[0], norms1, qkv_got1)
    grad1_far, qkv_a1_grad = pin(grad1_far, qkv_g_a1[0])
    grad_all0 = rows_of(grad1_low, grad1_far)
    final_far, *grad_all0 = pin(final_far, *grad_all0)
    final_far = flip(final_far, "tensor", 2)

    (normal0,) = stay(normal0)
    gm_a, gm_b, gi_a0, gi_b0, flipped0 = down_back(steps, grad_all0, stay(hid_a0[1], hid_b0[1]), out0, heads // 2, True)
    rest_b0 = rest_grads(slots, normal0, flipped0, gi_b0, in0[1], mixed0[1], hid_b0, norms0)
    gm_a, gm_b, rest_b0_grad, qkv_a1_grad, reduced_rest1 = pin(gm_a, gm_b, rest_b0[0], qkv_a1_grad, reduced_rest1)
    rest_got0 = flip(rest_b0_grad, "section")
    reduced_qkv1 = scatter_late(qkv_a1_grad)
    gp_b0 = attend_back_one(*stay(qkv_b0), stay(*mixed_b0), gm_b)
    gp_b0, gm_a, normal0, final_far = pin(gp_b0, gm_a, normal0, final_far)
    final = result_of(middle, chip_sum(near_terms), final_far, norms1)
    qkv_g_b0 = qkv_grads(slots, normal0, gp_b0, qkv0[1], norms0)
    normal0, qkv_b0_grad = pin(normal0, qkv_g_b0[0])
    rest_a0 = rest_grads(slots, normal0, flipped0, gi_a0, in0[0], mixed0[0], hid_a0, norms0)
    gm_a, qkv_b0_grad, rest_a0_grad, rest_got0, final, reduced_qkv1 = pin(
        gm_a, qkv_b0_grad, rest_a0[0], rest_got0, final, reduced_qkv1
    )
    qkv_got0 = flip(qkv_b0_grad, "section")
    rest_total0 = (rest_a0_grad.astype(f32) + rest_got0.astype(f32)).astype(bf16)
    gm_a, rest_total0 = pin(gm_a, rest_total0)
    reduced_in0 = scatter_late(rest_total0[:, :, :in_cols])
    gp_a0 = attend_back_one(*stay(qkv_a0), stay(*mixed_a0), gm_a)
    gp_a0, normal0, qkv_got0 = pin(gp_a0, normal0, qkv_got0)
    qkv_g_a0 = qkv_grads(slots, normal0, gp_a0, qkv0[0], norms0, qkv_got0)
    gp_a0, last, final, reduced_in0, rest_total0 = pin(gp_a0, qkv_g_a0[0], final, reduced_in0, rest_total0)
    act_got = flip(pick(final, middle), "section")
    reduced_out0 = scatter_late(rest_total0[:, :, in_cols:])
    reduced_qkv0 = scatter_late(last)
    stats = [
        [[pieces[0][1], pieces[1][1], pieces[0][2], pieces[1][2]] for pieces in pair]
        for pair in (((qkv_g_a0, qkv_g_b0), (rest_a0, rest_b0)), ((qkv_g_a1, qkv_g_b1), (rest_a1, rest_b1)))
    ]
    packed = []
    for grad_own, (qkv_t, in_t) in zip((grad1_low, grad2), stats):
        qkv_sum, in_sum = qkv_t[0] + qkv_t[1], in_t[0] + in_t[1]
        bias_sum = jnp.sum(grad_own.astype(f32), 0, keepdims=True)
        vectors = jnp.concatenate([qkv_sum[0:1], in_sum[0:1], qkv_sum[1:2], in_sum[1:2], bias_sum], 0)
        everywhere = vectors.reshape(5, n_tensor, n_dp, part).transpose(1, 2, 0, 3).reshape(n_tensor, n_dp, -1)
        halves_q = ordered(qkv_t[2][0].reshape(3, heads // 2), qkv_t[3][0].reshape(3, heads // 2))
        bias_q = jnp.concatenate(halves_q, 1).reshape(3, n_dp, part).transpose(1, 0, 2).reshape(n_dp, -1)
        bias_i = jnp.concatenate(ordered(in_t[2][0], in_t[3][0])).reshape(n_dp, -1)
        mine = jnp.concatenate([bias_q, bias_i], 1)
        only = (jnp.arange(n_tensor) == me)[:, None, None]
        packed.append(jnp.concatenate([everywhere, jnp.where(only, mine[None], 0.0)], 2))
    gp_a0, gp_b0, *packed = pin(gp_a0, gp_b0, *packed)

    def last_terms(half):
        return up_back((slots, slots), stay(gp_a0, gp_b0), stay(gi_a0, gi_b0), qkv0, in0, norms0, half)

    far = chip_sum(last_terms(1)).astype(bf16)
    far, gp_a0, gp_b0 = pin(far, gp_a0, gp_b0)
    near, beside = last_terms(0)
    near = (near, flip(beside, "tensor", 1))
    far = flip(far, "tensor", 2)
    total = pick(packed[0], packed[1]) + flip(pick(packed[1], packed[0]), "section")
    total = chosen(total, order, 0)
    small_sum = total[0::2] + flip(total[1::2], "tensor", 1)
    far, small_sum, reduced_qkv0, reduced_out0, *near = pin(far, small_sum, reduced_qkv0, reduced_out0, *near)
    near = near[0].astype(f32) + near[1].astype(f32)
    grad0 = input_back(h_own, grad1_low, near + far.astype(f32))
    grad_got = flip(pick(grad1_low, grad0.astype(bf16)), "section")

    total = small_sum
    total = total[0] + flip(total[1], "tensor", 2)
    sums = lax.psum_scatter(total, "dp", scatter_dimension=0) if not direct else None
    if direct:
        total = chosen(total, slots, 0)
        got = [lax.ppermute(total[hop], "dp", [(i, (i - hop) % n_dp) for i in range(n_dp)]) for hop in range(1, n_dp)]
        sums = sum(got, total[0])
    grad_got, sums = pin(grad_got, sums)

    activations = jnp.stack(ordered(pick(middle, final), act_got))
    input_grads = jnp.stack(ordered(pick(grad0, grad1_low.astype(f32)), grad_got.astype(f32)))

    def settled(one, two):
        got = flip(pick(two, one), "section")
        return [piece.astype(f32) for piece in ordered(pick(one, two), got)]

    rest_g = settled(jnp.concatenate([reduced_in0, reduced_out0], 1), reduced_rest1)
    qkv_g = settled(reduced_qkv0, reduced_qkv1)
    qkv_grad = jnp.concatenate([piece.reshape(-1, 3, heads // 2) for piece in qkv_g], 2)
    in_grad = jnp.concatenate([piece[:, :in_cols] for piece in rest_g], 1)
    dense_grad = jnp.concatenate([piece[:, in_cols : in_cols + heads // 2].T for piece in rest_g], 0)
    out_grad = jnp.concatenate([piece[:, in_cols + heads // 2 :].T for piece in rest_g], 0)

    return (
        activations[None],
        input_grads[None],
        qkv_grad[None],
        sums[5 * part : 8 * part].reshape(1, 3, part),
        dense_grad[None],
        in_grad[None],
        sums[8 * part :].reshape(1, -1),
        out_grad[None],
        sums[: 2 * part].reshape(1, 2, part),
        sums[2 * part : 4 * part].reshape(1, 2, part),
        jnp.stack([sums[4 * part : 5 * part]] * 2)[None],
    )


def solution(mesh):
    placed = (
        P("dp", "tensor", None),
        P("dp", "tensor", None),
        P("dp", None),
        P("section", "dp", None, "tensor"),
        P("section", None, ("tensor", "dp")),
        P("section", "tensor", "dp"),
        P("section", "dp", "tensor"),
        P("section", ("tensor", "dp")),
        P("section", "tensor", "dp"),
        P("section", None, ("tensor", "dp")),
        P("section", None, ("tensor", "dp")),
        P("section", None, ("tensor", "dp")),
    )
    return jax.shard_map(
        shards,
        mesh=mesh,
        in_specs=placed,
        out_specs=(
            P("section", "dp", "tensor", None),
            P("section", "dp", "tensor", None),
            P("section", "dp", None, "tensor"),
            P("section", None, ("tensor", "dp")),
            P("section", "tensor", "dp"),
            P("section", "dp", "tensor"),
            P("section", ("tensor", "dp")),
            P("section", "tensor", "dp"),
            P("section", None, ("tensor", "dp")),
            P("section", None, ("tensor", "dp")),
            P("section", None, ("tensor", "dp")),
        ),
        check_vma=False,
    )
```

```python
import functools
import math

import jax
import jax.numpy as jnp
from jax import lax
from jax.experimental import pallas as pl
from jax.experimental.pallas import tpu as pltpu
from jax.sharding import PartitionSpec as P

HDIM = 64
EPSILON = 1e-05
TILE = 512
KEYS = 512
NT = (((1,), (1,)), ((), ()))
NN = (((1,), (0,)), ((), ()))
TN = (((0,), (0,)), ((), ()))
LOG2E = math.log2(math.e)
FAR = 1e15
HURRY = 0.05
LIMIT = pltpu.CompilerParams(vmem_limit_bytes=20 * 2**20)


def mm(a, b, dims=NN):
    return lax.dot_general(a, b, dims, preferred_element_type=jnp.float32)


def cost(flops, moved, special=0):
    return pl.CostEstimate(flops=int(flops * HURRY), bytes_accessed=int(moved * HURRY), transcendentals=int(special))


def flip(block, axis, bit=1):
    return lax.ppermute(block, axis, [(i, i ^ bit) for i in range(lax.axis_size(axis))])


def turn(values, cosine, lead, trail):
    return values * cosine + pltpu.roll(values, 120, 1) * lead + pltpu.roll(values, 8, 1) * trail


def turn_back(grads, cosine, lead, trail):
    return grads * cosine - pltpu.roll(grads, 120, 1) * lead - pltpu.roll(grads, 8, 1) * trail


def head_part(block, head):
    lane = lax.broadcasted_iota(jnp.int32, block.shape, 1)
    return jnp.where((lane >= head * 64) & (lane < head * 64 + 64), block, jnp.zeros_like(block))


def tile_at(table, tile, size, shard_rows):
    per = shard_rows // size
    return pl.multiple_of(table[tile // per] * shard_rows + tile % per * size, size)


def below(query_tile, key_tile, keys, queries):
    rows = lax.broadcasted_iota(jnp.int32, (keys, queries), 0) + key_tile * keys
    cols = lax.broadcasted_iota(jnp.int32, (keys, queries), 1) + query_tile * queries
    return rows <= cols


def attend_kernel(shard_rows, table, q_ref, k_ref, v_ref, fq_ref, fk_ref, out_ref, lse_ref, vt, wides, tops, totals):
    step = pl.program_id(0)

    @pl.when(step == 0)
    def _():
        flipped = v_ref[...].T
        for head in range(2):
            vt[head, 0:64, :] = flipped[head * 64 : head * 64 + 64, :]
            vt[head, 64:80, :] = jnp.ones((16, flipped.shape[1]), jnp.bfloat16)

    for head in range(2):
        wides[head, :, 0:128] = head_part(q_ref[...], head)
        wides[head, :, 128:256] = fq_ref[...]
    tops[...] = jnp.full(tops.shape, -3e38, jnp.float32)
    totals[...] = jnp.zeros_like(totals)

    def tile(index, masked):
        at = tile_at(table, index, KEYS, shard_rows)
        keys = jnp.concatenate([k_ref[pl.ds(at, KEYS), :], fk_ref[pl.ds(at, KEYS), :]], 1)
        blocks = [mm(keys, wides[head], NT) for head in range(2)]
        blocks = [block * LOG2E for block in blocks]
        if masked:
            seen = below(step, index, KEYS, TILE)
            blocks = [jnp.where(seen, block, -1e30) for block in blocks]
        news = [jnp.maximum(tops[head], jnp.max(blocks[head], 0, keepdims=True)) for head in range(2)]
        probs = [jnp.exp2(blocks[head] - news[head]).astype(jnp.bfloat16) for head in range(2)]
        terms = [mm(vt[head, :, pl.ds(at, KEYS)], probs[head], NN) for head in range(2)]
        for head in range(2):
            totals[head] = totals[head] * jnp.exp2(tops[head] - news[head]) + terms[head]
            tops[head] = news[head]

    def loop(index, carry):
        tile(index, False)
        return carry

    whole = step * TILE // KEYS
    lax.fori_loop(0, whole, loop, 0)
    tile(whole, True)
    outs = []
    for head in range(2):
        norm = totals[head, 64:65, :]
        outs.append(totals[head, 0:64, :] / norm)
        lse_ref[head : head + 1, :] = tops[head] + jnp.log2(norm)
    lse_ref[2:8, :] = jnp.zeros((6, TILE), jnp.float32)
    out_ref[...] = jnp.concatenate(outs, 0).T.astype(jnp.bfloat16)


def attend(table, qkv, fq, fk):
    seq = qkv.shape[0]
    shard_rows = seq // 4
    per = shard_rows // TILE

    def place(step, table):
        return table[step // per] * per + step % per

    return pl.pallas_call(
        functools.partial(attend_kernel, shard_rows),
        grid_spec=pltpu.PrefetchScalarGridSpec(
            num_scalar_prefetch=1,
            grid=(seq // TILE,),
            in_specs=[
                pl.BlockSpec((TILE, 128), lambda i, t: (place(i, t), 0)),
                pl.BlockSpec((seq, 128), lambda i, t: (0, 1)),
                pl.BlockSpec((seq, 128), lambda i, t: (0, 2)),
                pl.BlockSpec((TILE, 128), lambda i, t: (place(i, t), 0)),
                pl.BlockSpec((seq, 128), lambda i, t: (0, 0)),
            ],
            out_specs=[
                pl.BlockSpec((TILE, 128), lambda i, t: (place(i, t), 0)),
                pl.BlockSpec((8, TILE), lambda i, t: (0, place(i, t))),
            ],
            scratch_shapes=[
                pltpu.VMEM((2, 80, seq), jnp.bfloat16),
                pltpu.VMEM((2, TILE, 256), jnp.bfloat16),
                pltpu.VMEM((2, 1, TILE), jnp.float32),
                pltpu.VMEM((2, 80, TILE), jnp.float32),
            ],
        ),
        out_shape=[
            jax.ShapeDtypeStruct((seq, 128), jnp.bfloat16),
            jax.ShapeDtypeStruct((8, seq), jnp.float32),
        ],
        compiler_params=LIMIT,
        cost_estimate=cost(4e9, 3e6, 5e6),
        name="attend",
    )(table, qkv, qkv, qkv, fq, fk)


def attend_back_kernel(shard_rows, table, q_ref, k_ref, v_ref, gm_ref, o_ref, lse_ref, fq_ref, fk_ref,
                       cos_ref, lead_ref, trail_ref, out_ref, kt, dk, dv, wides, grads, deltas, dq):
    step = pl.program_id(0)
    last = pl.num_programs(0) - 1 - step

    @pl.when(step == 0)
    def _():
        kt[...] = k_ref[...].T
        dk[...] = jnp.zeros_like(dk)
        dv[...] = jnp.zeros_like(dv)

    grad = gm_ref[...]
    product = grad.astype(jnp.float32) * o_ref[...].astype(jnp.float32)
    high = product.astype(jnp.bfloat16)
    low = (product - high.astype(jnp.float32)).astype(jnp.bfloat16)
    lane = lax.broadcasted_iota(jnp.int32, (8, 128), 1)
    for head in range(2):
        ones = jnp.where((lane >= head * 64) & (lane < head * 64 + 64), 1.0, 0.0).astype(jnp.bfloat16)
        deltas[head] = (mm(ones, high, NT) + mm(ones, low, NT))[0:1, :]
        wides[head, :, 0:128] = head_part(q_ref[...], head)
        wides[head, :, 128:256] = fq_ref[...]
        grads[head] = head_part(grad, head)
    dq[...] = jnp.zeros_like(dq)

    def tile(index, masked):
        at = tile_at(table, index, KEYS, shard_rows)
        rows = pl.ds(at, KEYS)
        keys = jnp.concatenate([k_ref[rows, :], fk_ref[rows, :]], 1)
        values = v_ref[rows, :]
        blocks = [mm(keys, wides[head], NT) for head in range(2)]
        backs = [mm(values, grads[head], NT) for head in range(2)]
        probs = [jnp.exp2(blocks[head] * LOG2E - lse_ref[head : head + 1, :]) for head in range(2)]
        if masked:
            seen = below(last, index, KEYS, TILE)
            probs = [jnp.where(seen, one, 0.0) for one in probs]
        slopes = [(probs[head] * (backs[head] - deltas[head])).astype(jnp.bfloat16) for head in range(2)]
        probs = [one.astype(jnp.bfloat16) for one in probs]
        dv[rows, :] += mm(jnp.concatenate(probs, 1), grads[...].reshape(2 * TILE, 128), NN)
        dk[rows, :] += mm(jnp.concatenate(slopes, 1), wides[:, :, 0:128].reshape(2 * TILE, 128), NN)
        for head in range(2):
            dq[head * 64 : head * 64 + 64, :] += mm(kt[head * 64 : head * 64 + 64, rows], slopes[head], NN)

    def loop(index, carry):
        tile(index, False)
        return carry

    whole = last * TILE // KEYS
    lax.fori_loop(0, whole, loop, 0)
    tile(whole, True)
    here = pl.ds(tile_at(table, last, TILE, shard_rows), TILE)
    turns = (cos_ref[...], lead_ref[...], trail_ref[...])
    out_ref[:, 0:128] = turn_back(dq[...].T * 0.125, *turns).astype(jnp.bfloat16)
    out_ref[:, 128:256] = turn_back(dk[here, :], *turns).astype(jnp.bfloat16)
    out_ref[:, 256:384] = dv[here, :].astype(jnp.bfloat16)


def attend_back(table, qkv, grad_mixed, mixed, lse, fq, fk, turns):
    seq = qkv.shape[0]
    shard_rows = seq // 4
    tiles = seq // TILE
    per = shard_rows // TILE

    def place(step, table):
        tile = tiles - 1 - step
        return table[tile // per] * per + tile % per

    block = pl.BlockSpec((TILE, 128), lambda i, t: (place(i, t), 0))
    return pl.pallas_call(
        functools.partial(attend_back_kernel, shard_rows),
        grid_spec=pltpu.PrefetchScalarGridSpec(
            num_scalar_prefetch=1,
            grid=(tiles,),
            in_specs=[
                block,
                pl.BlockSpec((seq, 128), lambda i, t: (0, 1)),
                pl.BlockSpec((seq, 128), lambda i, t: (0, 2)),
                block,
                block,
                pl.BlockSpec((8, TILE), lambda i, t: (0, place(i, t))),
                block,
                pl.BlockSpec((seq, 128), lambda i, t: (0, 0)),
                block,
                block,
                block,
            ],
            out_specs=pl.BlockSpec((TILE, 384), lambda i, t: (place(i, t), 0)),
            scratch_shapes=[
                pltpu.VMEM((128, seq), jnp.bfloat16),
                pltpu.VMEM((seq, 128), jnp.float32),
                pltpu.VMEM((seq, 128), jnp.float32),
                pltpu.VMEM((2, TILE, 256), jnp.bfloat16),
                pltpu.VMEM((2, TILE, 128), jnp.bfloat16),
                pltpu.VMEM((2, 1, TILE), jnp.float32),
                pltpu.VMEM((128, TILE), jnp.float32),
            ],
        ),
        out_shape=pltpu.HBM((seq, 384), jnp.bfloat16),
        compiler_params=LIMIT,
        cost_estimate=cost(10e9, 6e6, 5e6),
        name="attend_back",
    )(table, qkv, qkv, qkv, grad_mixed, mixed, lse, fq, fk, *turns)


def normal_of(values):
    centered = values - jnp.mean(values, -1, keepdims=True)
    inverse = lax.rsqrt(jnp.mean(centered * centered, -1, keepdims=True) + EPSILON)
    return centered * inverse, inverse


def whole_of(array):
    return pl.BlockSpec(array.shape, lambda *i: (0,) * array.ndim)


def heads_of(first, weight, bias, turns, out_ref):
    projected = mm(first, weight) + bias
    for part in range(3):
        piece = projected[:, 128 * part : 128 * part + 128]
        if part < 2:
            piece = turn(piece, *turns)
        if part == 0:
            piece = piece * 0.125
        out_ref[:, 128 * part : 128 * part + 128] = piece.astype(jnp.bfloat16)


def settle(slots, source, target, start=0):
    @pl.when(pl.program_id(0) == 0)
    def _():
        rows = target.shape[0] // source.shape[0]
        for block in range(source.shape[0]):
            target[block * rows : block * rows + rows, :] = source[slots[block], 0:rows, start : start + target.shape[1]]


def weight_scratch(width, weight, cols=None):
    return pltpu.VMEM((width, cols or weight.shape[2]), weight.dtype)


def choose(pieces, target):
    for step, piece in enumerate(pieces):

        @pl.when(pl.program_id(0) == step)
        def _():
            target[...] = piece[...]


def call(kernel, name, grid, in_specs, out_specs, out_shape, scratch, flops, moved, special=0, scalars=1, aliases=None):
    return pl.pallas_call(
        kernel,
        grid_spec=pltpu.PrefetchScalarGridSpec(
            num_scalar_prefetch=scalars, grid=grid, in_specs=in_specs, out_specs=out_specs, scratch_shapes=scratch
        ),
        out_shape=out_shape,
        compiler_params=LIMIT,
        cost_estimate=cost(flops, moved, special),
        input_output_aliases=aliases or {},
        name=name,
    )


def struct(*shape, far=False):
    return pltpu.HBM(shape, jnp.bfloat16) if far else jax.ShapeDtypeStruct(shape, jnp.bfloat16)


def stay(*arrays):
    return [pltpu.with_memory_space_constraint(array, pltpu.HBM) for array in arrays]


def project_kernel(
    slots, h0, h1, h2, h3, weight_ref, bias_ref, norm_ref, cos_ref, lead_ref, trail_ref,
    out_ref, first_ref, second_ref, flip_ref, weight, h_ref
):
    settle(slots, weight_ref, weight)
    choose((h0, h1, h2, h3), h_ref)
    normal, _ = normal_of(h_ref[...].astype(jnp.float32))
    flip_ref[...] = normal.astype(jnp.bfloat16).T
    first = (normal * norm_ref[0:1, :] + norm_ref[2:3, :]).astype(jnp.bfloat16)
    first_ref[...] = first
    second_ref[...] = (normal * norm_ref[1:2, :] + norm_ref[3:4, :]).astype(jnp.bfloat16)
    heads_of(first, weight[...], bias_ref[0:1, 0 : weight.shape[1]], (cos_ref[...], lead_ref[...], trail_ref[...]), out_ref)


def project(slots, pieces, weight, cols, bias, norms, turns, far=False):
    rows, width = pieces[0].shape
    seq = rows * len(pieces)
    block = pl.BlockSpec((rows, width), lambda i, s: (i, 0))
    return call(
        project_kernel,
        "project",
        (seq // rows,),
        [whole_of(x) for x in (*pieces, weight, bias, norms)] + [pl.BlockSpec((rows, 128), lambda i, s: (i, 0))] * 3,
        [pl.BlockSpec((rows, cols), lambda i, s: (i, 0)), block, block, pl.BlockSpec((width, rows), lambda i, s: (0, i))],
        [struct(seq, cols)] + [struct(*shape, far=far) for shape in ((seq, width), (seq, width), (width, seq))],
        [weight_scratch(width, weight, cols), pltpu.VMEM((rows, width), jnp.bfloat16)],
        4e9,
        18e6,
    )(slots, *pieces, weight, bias, norms, *turns)


def project_more_kernel(slots, first_ref, weight_ref, bias_ref, cos_ref, lead_ref, trail_ref, out_ref, weight):
    settle(slots, weight_ref, weight)
    heads_of(
        first_ref[...], weight[...], bias_ref[1:2, 0 : weight.shape[1]], (cos_ref[...], lead_ref[...], trail_ref[...]), out_ref
    )


def project_more(slots, first, weight, cols, bias, turns):
    seq, width = first.shape
    rows = 512
    return call(
        project_more_kernel,
        "project_more",
        (seq // rows,),
        [pl.BlockSpec((rows, width), lambda i, s: (i, 0)), whole_of(weight), whole_of(bias)]
        + [pl.BlockSpec((rows, 128), lambda i, s: (i, 0))] * 3,
        pl.BlockSpec((rows, cols), lambda i, s: (i, 0)),
        struct(seq, cols),
        [weight_scratch(width, weight, cols)],
        3e9,
        8e6,
    )(slots, first, weight, bias, *turns)


def gelu_kernel(part, slots, a_ref, weight_ref, bias_ref, out_ref, slope_ref, weight):
    settle(slots, weight_ref, weight, weight_ref.shape[2] - weight.shape[1])
    inner = mm(a_ref[...], weight[...]) + bias_ref[part : part + 1, bias_ref.shape[1] - weight.shape[1] :]
    size = jnp.abs(inner)
    t = 1.0 / (1.0 + (0.3275911 * math.sqrt(0.5)) * size)
    bell = jnp.exp2((-0.5 * LOG2E) * inner * inner)
    poly = 0.5 * 1.061405429 * t + 0.5 * -1.453152027
    poly = poly * t + 0.5 * 1.421413741
    poly = poly * t + 0.5 * -0.284496736
    poly = poly * t + 0.5 * 0.254829592
    tail = poly * t * bell
    below = jnp.where(inner >= 0, 1.0 - tail, tail)
    out_ref[...] = (inner * below).astype(jnp.bfloat16)
    slope_ref[...] = (below + inner * bell * (1.0 / math.sqrt(2 * math.pi))).astype(jnp.bfloat16)


def gelu_up(slots, second, weight, cols, bias, part, far=False):
    seq, width = second.shape
    rows = 256
    block = pl.BlockSpec((rows, cols), lambda i, s: (i, 0))
    return call(
        functools.partial(gelu_kernel, part),
        "gelu_up",
        (seq // rows,),
        [pl.BlockSpec((rows, width), lambda i, s: (i, 0)), whole_of(weight), whole_of(bias)],
        [block, block],
        [struct(seq, cols), struct(seq, cols, far=far)],
        [weight_scratch(width, weight, cols)],
        5e9,
        10e6,
        2e6,
    )(slots, second, weight, bias)


def deal(value, *targets):
    for step, target in enumerate(targets):

        @pl.when(pl.program_id(0) == step)
        def _():
            target[...] = value


def down_kernel(slots, mixed_mine, mixed_other, act_mine, act_other, mine_ref, other_ref, near_ref, beside_ref, mine, other):
    settle(slots, mine_ref, mine)
    settle(slots, other_ref, other)
    heads = mixed_mine.shape[1]
    total = mm(mixed_mine[...], mine[:, 0:heads], NT) + mm(act_mine[...], mine[:, heads:], NT)
    total += mm(mixed_other[...], other[:, 0:heads], NT) + mm(act_other[...], other[:, heads:], NT)
    deal(total.astype(jnp.bfloat16), near_ref, beside_ref)


def down(slots, mixed, act, weights, half):
    seq = mixed[0].shape[0]
    width = weights[0].shape[0] * weights[0].shape[1]
    rows = 512
    steps = seq // rows // 2
    return call(
        down_kernel,
        "down",
        (steps,),
        [pl.BlockSpec((rows, x.shape[1]), lambda i, s: (i + half * steps, 0)) for x in (*mixed, *act)]
        + [whole_of(w) for w in weights],
        [pl.BlockSpec((rows, width), lambda i, s: (0, 0))] * 2,
        [struct(rows, width)] * 2,
        [weight_scratch(width, w) for w in weights],
        4e9,
        8e6,
    )(slots, *mixed, *act, *weights)


def down_back_kernel(
    slots, g0, g1, g2, g3, slope_mine, slope_other, mine_ref, other_ref,
    mixed_mine, mixed_other, inner_mine, inner_other, flip_ref, mine, other, grad_ref
):
    choose((g0, g1, g2, g3), grad_ref)
    settle(slots, mine_ref, mine)
    settle(slots, other_ref, other)
    heads = mixed_mine.shape[1]
    flip_ref[...] = grad_ref[...].T
    for slope, weight, mixed, inner in (
        (slope_mine, mine, mixed_mine, inner_mine),
        (slope_other, other, mixed_other, inner_other),
    ):
        mixed[...] = mm(grad_ref[...], weight[:, 0:heads]).astype(jnp.bfloat16)
        inner[...] = (mm(grad_ref[...], weight[:, heads:]) * slope[...].astype(jnp.float32)).astype(jnp.bfloat16)


def down_back(slots, pieces, slopes, weights, heads, far=False):
    rows, width = pieces[0].shape
    seq = rows * len(pieces)
    hidden = slopes[0].shape[1]
    wide = pl.BlockSpec((rows, hidden), lambda i, s: (i, 0))
    return call(
        down_back_kernel,
        "down_back",
        (seq // rows,),
        [whole_of(x) for x in pieces] + [wide, wide] + [whole_of(w) for w in weights],
        [pl.BlockSpec((rows, heads), lambda i, s: (i, 0))] * 2 + [wide, wide, pl.BlockSpec((width, rows), lambda i, s: (0, i))],
        [struct(seq, heads)] * 2 + [struct(seq, hidden, far=far)] * 2 + [struct(width, seq, far=far)],
        [weight_scratch(width, w) for w in weights] + [pltpu.VMEM((rows, width), jnp.bfloat16)],
        8e9,
        18e6,
    )(slots, *pieces, *slopes, *weights)


def up_back_kernel(
    slots, in_slots, proj_mine, proj_other, inner_mine, inner_other, qkv_mine, qkv_other, in_mine, in_other, gain_ref, near_ref, beside_ref, *weights
):
    for source, target in zip((qkv_mine, qkv_other), weights[:2]):
        settle(slots, source, target)
    for source, target in zip((in_mine, in_other), weights[2:]):
        settle(in_slots, source, target, source.shape[2] - target.shape[1])
    qkv_a, qkv_b, in_a, in_b = weights
    first = mm(proj_mine[...], qkv_a[...], NT) + mm(proj_other[...], qkv_b[...], NT)
    second = mm(inner_mine[...], in_a[...], NT) + mm(inner_other[...], in_b[...], NT)
    deal((first * gain_ref[0:1, :] + second * gain_ref[1:2, :]).astype(jnp.bfloat16), near_ref, beside_ref)


def up_back(slots, proj, inner, qkv_w, in_w, gains, half):
    seq = proj[0].shape[0]
    width = gains.shape[1]
    rows = 512
    steps = seq // rows // 2
    return call(
        up_back_kernel,
        "up_back",
        (steps,),
        [pl.BlockSpec((rows, x.shape[1]), lambda i, *s: (i + half * steps, 0)) for x in (*proj, *inner)]
        + [whole_of(w) for w in (*qkv_w, *in_w, gains)],
        [pl.BlockSpec((rows, width), lambda i, *s: (0, 0))] * 2,
        [struct(rows, width)] * 2,
        [weight_scratch(width, w, x.shape[1]) for w, x in zip((*qkv_w, *in_w), (*proj, *inner))],
        4e9,
        10e6,
        scalars=2,
    )(*slots, *proj, *inner, *qkv_w, *in_w, gains)


def grads_kernel(ups, downs, adds, slots, *refs):
    refs = list(refs)
    normal = refs.pop(0) if ups else None
    flipped = refs.pop(0) if downs else None
    backs = [refs.pop(0) for _ in range(ups)]
    sources = [refs.pop(0) for _ in range(downs)]
    weights = [refs.pop(0) for _ in range(ups)]
    norm_ref = refs.pop(0)
    got_ref = refs.pop(0) if adds else None
    out_ref = refs.pop(0)
    row = 1 if downs else 0
    norm = norm_ref[...].T
    gain_column, bias_column = norm[:, row : row + 1], norm[:, 2 + row : 3 + row]

    def store(first, last, value):
        if adds:
            value += got_ref[0, :, first:last].astype(jnp.float32)
        out_ref[0, :, first:last] = value.astype(jnp.bfloat16)

    at = 0
    for k in range(ups):
        stat_ref, sum_ref = refs[2 * k : 2 * k + 2]
        cols = backs[k].shape[1]
        raw = mm(normal[...], backs[k][...])
        total = mm(jnp.ones((8, backs[k].shape[0]), jnp.bfloat16), backs[k][...])
        sum_ref[...] = total
        total = total[0:1, :]
        store(at, at + cols, raw * gain_column + total * bias_column)
        first = weights[k].shape[2] - cols if downs else 0
        wide = weights[k][0, :, first : first + cols].astype(jnp.float32)
        gain = jnp.sum(raw * wide, 1, keepdims=True)
        shift = jnp.sum(wide * total, 1, keepdims=True)
        lane = lax.broadcasted_iota(jnp.int32, (raw.shape[0], 128), 1)
        stat_ref[...] = jnp.where(lane == 0, gain, jnp.where(lane == 1, shift, 0.0)).T[0:8, :]
        at += cols
    for source in sources:
        cols = source.shape[1]
        store(at, at + cols, mm(flipped[...], source[...]))
        at += cols


def weight_grads(slots, normal, flipped, ups, downs, norms, got=None):
    width, seq = (normal if ups else flipped).shape
    groups = 4
    rows = width // groups
    strip = pl.BlockSpec((rows, seq), lambda i, s: (i, 0))
    args, specs = [], []
    for array, used in ((normal, ups), (flipped, downs)):
        if used:
            args.append(array)
            specs.append(strip)
    for array in [back for back, _ in ups] + list(downs):
        args.append(array)
        specs.append(whole_of(array))
    for _, weight in ups:
        args.append(weight)
        specs.append(pl.BlockSpec((1, rows, weight.shape[2]), lambda i, s: (s[i], 0, 0)))
    args.append(norms)
    specs.append(pl.BlockSpec((norms.shape[0], rows), lambda i, s: (0, i)))
    cols = sum(back.shape[1] for back, _ in ups) + sum(source.shape[1] for source in downs)
    out_specs = [pl.BlockSpec((1, rows, cols), lambda i, s: (i, 0, 0))]
    if got is not None:
        args.append(got)
        specs.append(out_specs[0])
    out_shape = [struct(groups, rows, cols, far=True)]
    for back, _ in ups:
        out_specs += [pl.BlockSpec((8, rows), lambda i, s: (0, i)), pl.BlockSpec((8, back.shape[1]), lambda i, s: (0, 0))]
        out_shape += [pltpu.HBM((8, width), jnp.float32), pltpu.HBM((8, back.shape[1]), jnp.float32)]
    return call(
        functools.partial(grads_kernel, len(ups), len(downs), got is not None),
        "weight_grads",
        (groups,),
        specs,
        out_specs,
        out_shape,
        [],
        2 * seq * width * cols,
        8e6,
    )(slots, *args)


def shards(
    inputs,
    cotangent,
    lengths,
    qkv_weight,
    qkv_bias,
    dense_weight,
    in_weight,
    in_bias,
    out_weight,
    norm_gains,
    norm_biases,
    out_biases,
):
    f32, bf16 = jnp.float32, jnp.bfloat16
    lefthand = lax.axis_index("section") == 0
    me, depth = lax.axis_index("tensor"), lax.axis_index("dp")
    n_tensor, n_dp = lax.axis_size("tensor"), lax.axis_size("dp")
    shard_rows, width = inputs.shape[1:]
    heads = qkv_weight.shape[3]
    hidden = in_weight.shape[2]
    groups = 4
    direct = n_dp == groups

    def pick(first, second):
        return jnp.where(lefthand, first, second)

    def ordered(mine, other):
        return pick(mine, other), pick(other, mine)

    def gather_deep(piece):
        if not direct:
            return lax.all_gather(piece, "dp", axis=0, tiled=True).reshape(groups, -1, piece.shape[1])
        pieces = [piece]
        for hop in range(1, n_dp):
            pieces.append(lax.ppermute(piece, "dp", [(i, (i + hop) % n_dp) for i in range(n_dp)]))
        return jnp.stack(pieces)

    def scatter_late(total):
        return lax.psum_scatter(total.reshape(-1, total.shape[2]), "dp", scatter_dimension=0, tiled=True)

    def pin(*values):
        return lax.optimization_barrier(values)

    h_own = pick(inputs[0], inputs[1])
    cot = pick(cotangent[0], cotangent[1])
    row = pick(lengths[0], lengths[1])

    def halves(group):
        return pick(group[0], group[1]), pick(group[1], group[0])

    def cut(array, axis, k):
        size = array.shape[axis] // 2
        return lax.slice_in_dim(array, k * size, k * size + size, axis=axis)

    small = jnp.concatenate([piece[0].reshape(-1) for piece in (qkv_bias, norm_gains, norm_biases, out_biases, in_bias)])
    part = qkv_bias.shape[2]
    n_small = small.shape[0]
    qkv_cols, in_cols = 3 * heads // 2, hidden // 2
    qkv_half = halves([cut(qkv_weight[0], 2, k).reshape(-1, qkv_cols) for k in range(2)])
    qkv_got = flip(qkv_half[1], "section")
    pair = jnp.stack([small, flip(small, "tensor", 2)])
    h_own, pair = pin(h_own, pair)
    h_far = flip(h_own, "tensor", 2)
    pair = jnp.stack([pair, flip(pair, "tensor", 1)], 1)
    pair = jnp.stack(ordered(pair, flip(pair, "section"))).reshape(-1)
    extra = -(-pair.shape[0] // (16 * qkv_cols)) * 16
    pair = jnp.zeros((extra * qkv_cols,), bf16).at[: pair.shape[0]].set(pair).reshape(extra, qkv_cols)
    deep = qkv_half[0].shape[0]
    qkv_shard = ordered(qkv_half[0], qkv_got)
    first = jnp.concatenate([qkv_shard[0], pair], 0)
    zero = jnp.zeros((), jnp.int32)
    first, row, zero, cot, in_weight, dense_weight, out_weight = pin(
        first, row, zero, cot, in_weight, dense_weight, out_weight
    )
    rest_half = halves(
        [
            jnp.concatenate([cut(in_weight[0], 1, k), cut(dense_weight[0], 0, k).T, cut(out_weight[0], 0, k).T], 1)
            for k in range(2)
        ]
    )
    first = gather_deep(first) if direct else lax.all_gather(first, "dp", axis=0)

    steps = zero + jnp.arange(groups, dtype=jnp.int32)
    slots = (depth - steps) % groups if direct else steps
    rest_mine, rest_got = rest_half[0], flip(rest_half[1], "section")
    qkv0 = first if direct else first[:, :deep].reshape(groups, -1, qkv_cols)
    pair = first[:, deep:].reshape(n_dp, -1)[:, : 2 * n_tensor * n_small].reshape(n_dp, 2, n_tensor, n_small)
    order = (zero + jnp.arange(n_tensor)) ^ me
    small_all = pair.astype(f32).transpose(1, 2, 0, 3)

    def chosen(array, index, axis):
        size = index.shape[0]
        shape = [1] * array.ndim
        shape[axis] = size
        return sum(
            jnp.where(index.reshape(shape) == place, lax.slice_in_dim(array, place, place + 1, axis=axis), 0.0)
            for place in range(size)
        )

    if direct:
        small_all = chosen(small_all, slots, 2)
    here = small_all[:, 0]
    small_all = chosen(small_all, order, 1)

    def gather_early(piece):
        return lax.all_gather(piece, "dp", axis=0, tiled=True).reshape(groups, -1, piece.shape[1])

    def shares(rest):
        return rest[:, :in_cols], rest[:, in_cols:]

    table = jnp.arange(n_tensor, dtype=jnp.int32) ^ me
    positions = jnp.concatenate(
        [slot * shard_rows + zero + jnp.arange(shard_rows, dtype=jnp.int32) for slot in (me, me ^ 1, me ^ 2, me ^ 3)]
    )
    ends = jnp.cumsum(row)
    passed = positions[:, None] >= ends[None, :]
    doc = jnp.sum(passed.astype(jnp.int32), -1)
    offset = positions - jnp.sum(jnp.where(passed, row[None, :], 0), -1)
    valid_own = (positions < ends[-1])[:shard_rows]
    lane = jnp.arange(128, dtype=jnp.int32) + zero
    same = doc[:, None] == lane[None, :]
    feats_q = jnp.where(same, -FAR, 0.0).astype(bf16)
    feats_k = jnp.where(same | (lane[None, :] > row.shape[0]), 0.0, FAR).astype(bf16)
    place = lane % HDIM
    rotary = HDIM // 4
    counter = (place % (rotary // 2)).astype(f32)
    inverse = jnp.exp(counter * (-2.0 * math.log(10000.0) / rotary))
    angles = offset.astype(f32)[:, None] * inverse[None, :]
    turned = (place < rotary)[None, :]
    sine = jnp.sin(angles)
    rotary_turns = (
        jnp.where(turned, jnp.cos(angles), 1.0),
        jnp.where((place < rotary // 2)[None, :], -sine, 0.0),
        jnp.where(turned & (place >= rotary // 2)[None, :], sine, 0.0),
    )

    rows_all = small_all[..., 3 * part : 9 * part].reshape(2, n_tensor, n_dp, 6, part).transpose(0, 3, 1, 2, 4)
    rows_all = jnp.pad(rows_all.reshape(2, 6, width), ((0, 0), (0, 2), (0, 0)))
    qkv_parts = here[..., : 3 * part].reshape(2, n_dp, 3, part).transpose(0, 2, 1, 3).reshape(2, 3, 2, heads // 2)
    qkv_parts = qkv_parts.transpose(0, 2, 1, 3).reshape(2, 2, qkv_cols)
    bias_all = jnp.concatenate([qkv_parts, here[..., 9 * part : n_small].reshape(2, 2, in_cols)], 2)
    bias_all = jnp.stack(ordered(bias_all[:, 0], bias_all[:, 1]), 1)

    def chip_sum(terms):
        return terms[0].astype(f32) + flip(terms[1], "tensor", 1).astype(f32)

    def branch_sum(make):
        far = chip_sum(make(1)).astype(bf16)
        return chip_sum(make(0)), far

    def result_of(own, near, far, rows):
        return (own.astype(f32) + near + far.astype(f32) + rows[4:5] + rows[5:6]).astype(bf16)

    def input_back(own, grad_own, partial):
        n, inverse = normal_of(own.astype(f32))
        return grad_own.astype(f32) + inverse * (
            partial - jnp.mean(partial, -1, keepdims=True) - n * jnp.mean(partial * n, -1, keepdims=True)
        )

    def attend_one(qkv):
        return attend(table, qkv, feats_q, feats_k)

    def attend_back_one(qkv, attended, grad_mixed):
        mixed, lse = attended
        return attend_back(table, qkv, grad_mixed, mixed, lse, feats_q, feats_k, stay(*rotary_turns))

    def rows_of(own, far):
        return own, flip(own, "tensor", 1), far, flip(far, "tensor", 1)

    in_shard0 = pick(rest_mine[:, :in_cols], rest_got[:, :in_cols])
    qkv0, rows_all, bias_all, in_shard0, *h_all = pin(qkv0, rows_all, bias_all, in_shard0, *rows_of(h_own, h_far))
    in0 = gather_deep(in_shard0)
    (norms0, norms1), (bias0, bias1) = rows_all, bias_all
    qkv0_other = flip(qkv0, "section")
    qkv_a0, normed, second, normal0 = project(slots, h_all, qkv0, qkv_cols, bias0, norms0, rotary_turns, True)
    qkv_a0, cot, rest_mine, rest_got = pin(qkv_a0, cot, rest_mine, rest_got)
    rest0, rest1 = ordered(rest_mine, rest_got)
    (_, out_shard0), (in_shard1, out_shard1) = shares(rest0), shares(rest1)
    grad2 = cot * valid_own[:, None].astype(bf16)
    grad2_far = flip(grad2, "tensor", 2)
    mixed_a0 = attend_one(qkv_a0)
    in0, qkv0_other, normed, out_shard0, *mixed_a0 = pin(in0, qkv0_other, normed, out_shard0, *mixed_a0)
    out0 = gather_early(out_shard0)
    in0_other = flip(in0, "section")
    qkv0 = stay(qkv0, qkv0_other)
    qkv_b0 = project_more(slots, *stay(normed), qkv0[1], qkv_cols, bias0, rotary_turns)
    mixed_b0 = attend_one(qkv_b0)
    second, grad2_far, in0_other, *mixed_b0 = pin(second, grad2_far, in0_other, *mixed_b0)
    in0 = stay(in0, in0_other)
    hid_a0 = gelu_up(slots, *stay(second), in0[0], in_cols, bias0, 0, True)
    grad_all1 = rows_of(grad2, grad2_far)
    second, out0, hid_a0, qkv_shard1 = pin(second, out0, hid_a0, qkv_shard[1])
    qkv1 = gather_deep(qkv_shard1)
    out0 = stay(out0, flip(out0, "section"))
    hid_b0 = gelu_up(slots, *stay(second), in0[1], in_cols, bias0, 1, True)
    mixed0 = (mixed_a0[0], mixed_b0[0])
    hid_b0, qkv1, in_shard1 = pin(hid_b0, qkv1, in_shard1)
    in1 = gather_early(in_shard1)
    far = chip_sum(down(steps, stay(*mixed0), stay(hid_a0[0], hid_b0[0]), out0, 1)).astype(bf16)
    far, mixed0, qkv1, *grad_all1 = pin(far, mixed0, qkv1, *grad_all1)
    qkv1_other = flip(qkv1, "section")
    near = chip_sum(down(steps, stay(*mixed0), stay(hid_a0[0], hid_b0[0]), out0, 0))
    middle = result_of(h_own, near, flip(far, "tensor", 2), norms0)
    middle, qkv1_other, out_shard1 = pin(middle, qkv1_other, out_shard1)
    out1 = gather_early(out_shard1)

    h_all = rows_of(middle, flip(middle, "tensor", 2))
    in1, *h_all = pin(in1, *h_all)
    in1_other = flip(in1, "section")
    qkv1 = (qkv1, qkv1_other)
    qkv_a1, normed, second, normal1 = project(slots, h_all, qkv1[0], qkv_cols, bias1, norms1, rotary_turns)
    mixed_a1 = attend_one(qkv_a1)
    normed, out1, in1_other, *mixed_a1 = pin(normed, out1, in1_other, *mixed_a1)
    in1 = (in1, in1_other)
    out1_other = flip(out1, "section")
    qkv_b1 = project_more(slots, normed, qkv1[1], qkv_cols, bias1, rotary_turns)
    mixed_b1 = attend_one(qkv_b1)
    second, *mixed_b1 = pin(second, *mixed_b1)
    hid_a1 = gelu_up(steps, second, in1[0], in_cols, bias1, 0)
    hid_b1 = gelu_up(steps, second, in1[1], in_cols, bias1, 1)
    mixed1 = (mixed_a1[0], mixed_b1[0])
    out1_other, hid_a1, hid_b1 = pin(out1_other, hid_a1, hid_b1)
    out1 = (out1, out1_other)

    gm_a, gm_b, gi_a1, gi_b1, flipped1 = down_back(steps, grad_all1, (hid_a1[1], hid_b1[1]), out1, heads // 2)

    def rest_grads(blocks, normal, flipped, gi, in_w, mixed, hid, norms, got=None):
        return weight_grads(blocks, normal, flipped, ((gi, in_w),), (mixed, hid[0]), norms, got)

    def qkv_grads(blocks, normal, gp, qkv_w, norms, got=None):
        return weight_grads(blocks, normal, None, ((*stay(gp), qkv_w),), (), norms, got)

    rest_b1 = rest_grads(steps, normal1, flipped1, gi_b1, in1[1], mixed1[1], hid_b1, norms1)
    gm_a, gm_b, rest_b1_grad = pin(gm_a, gm_b, rest_b1[0])
    rest_got1 = flip(rest_b1_grad, "section")
    gp_b1 = attend_back_one(qkv_b1, mixed_b1, gm_b)
    gm_a, gp_b1, normal1 = pin(gm_a, gp_b1, normal1)
    qkv_g_b1 = qkv_grads(slots, normal1, gp_b1, qkv1[1], norms1)
    gm_a, gp_b1, qkv_b1_grad = pin(gm_a, gp_b1, qkv_g_b1[0])
    gp_a1 = attend_back_one(qkv_a1, mixed_a1, gm_a)
    gp_a1, rest_got1 = pin(gp_a1, rest_got1)
    near, far = branch_sum(lambda half: up_back((slots, steps), stay(gp_a1, gp_b1), stay(gi_a1, gi_b1), qkv1, in1, norms1, half))
    far, normal1, flipped1, rest_got1 = pin(far, normal1, flipped1, rest_got1)
    far = flip(far, "tensor", 2)
    rest_a1 = rest_grads(steps, normal1, flipped1, gi_a1, in1[0], mixed1[0], hid_a1, norms1, rest_got1)
    normal1, rest_a1_grad, qkv_b1_grad, mixed1_a, mixed1_b = pin(normal1, rest_a1[0], qkv_b1_grad, *mixed1)
    qkv_got1 = flip(qkv_b1_grad, "section")
    final_far = chip_sum(down(steps, stay(mixed1_a, mixed1_b), stay(hid_a1[0], hid_b1[0]), stay(*out1), 1)).astype(bf16)
    far, normal1, rest_a1_grad = pin(far, normal1, rest_a1_grad)
    grad1 = input_back(middle, grad2, near + far.astype(f32))
    grad1_low = grad1.astype(bf16)
    grad1_low, rest_a1_grad, normal1, final_far, mixed1_a, mixed1_b = pin(
        grad1_low, rest_a1_grad, normal1, final_far, mixed1_a, mixed1_b
    )
    grad1_far = flip(grad1_low, "tensor", 2)
    reduced_rest1 = scatter_late(rest_a1_grad)
    near_terms = down(steps, stay(mixed1_a, mixed1_b), stay(hid_a1[0], hid_b1[0]), stay(*out1), 0)
    qkv_got1, normal1, *near_terms = pin(qkv_got1, normal1, *near_terms)
    qkv_g_a1 = qkv_grads(slots, normal1, gp_a1, qkv1[0], norms1, qkv_got1)
    grad1_far, qkv_a1_grad = pin(grad1_far, qkv_g_a1[0])
    grad_all0 = rows_of(grad1_low, grad1_far)
    final_far, *grad_all0 = pin(final_far, *grad_all0)
    final_far = flip(final_far, "tensor", 2)

    (normal0,) = stay(normal0)
    gm_a, gm_b, gi_a0, gi_b0, flipped0 = down_back(steps, grad_all0, stay(hid_a0[1], hid_b0[1]), out0, heads // 2, True)
    rest_b0 = rest_grads(slots, normal0, flipped0, gi_b0, in0[1], mixed0[1], hid_b0, norms0)
    gm_a, gm_b, rest_b0_grad, qkv_a1_grad, reduced_rest1 = pin(gm_a, gm_b, rest_b0[0], qkv_a1_grad, reduced_rest1)
    rest_got0 = flip(rest_b0_grad, "section")
    reduced_qkv1 = scatter_late(qkv_a1_grad)
    gp_b0 = attend_back_one(*stay(qkv_b0), stay(*mixed_b0), gm_b)
    gp_b0, gm_a, normal0, final_far = pin(gp_b0, gm_a, normal0, final_far)
    final = result_of(middle, chip_sum(near_terms), final_far, norms1)
    qkv_g_b0 = qkv_grads(slots, normal0, gp_b0, qkv0[1], norms0)
    normal0, qkv_b0_grad = pin(normal0, qkv_g_b0[0])
    rest_a0 = rest_grads(slots, normal0, flipped0, gi_a0, in0[0], mixed0[0], hid_a0, norms0)
    gm_a, qkv_b0_grad, rest_a0_grad, rest_got0, final, reduced_qkv1 = pin(
        gm_a, qkv_b0_grad, rest_a0[0], rest_got0, final, reduced_qkv1
    )
    qkv_got0 = flip(qkv_b0_grad, "section")
    rest_total0 = (rest_a0_grad.astype(f32) + rest_got0.astype(f32)).astype(bf16)
    gm_a, rest_total0 = pin(gm_a, rest_total0)
    reduced_in0 = scatter_late(rest_total0[:, :, :in_cols])
    gp_a0 = attend_back_one(*stay(qkv_a0), stay(*mixed_a0), gm_a)
    gp_a0, normal0, qkv_got0 = pin(gp_a0, normal0, qkv_got0)
    qkv_g_a0 = qkv_grads(slots, normal0, gp_a0, qkv0[0], norms0, qkv_got0)
    gp_a0, last, final, reduced_in0, rest_total0 = pin(gp_a0, qkv_g_a0[0], final, reduced_in0, rest_total0)
    act_got = flip(pick(final, middle), "section")
    reduced_out0 = scatter_late(rest_total0[:, :, in_cols:])
    reduced_qkv0 = scatter_late(last)
    stats = [
        [[pieces[0][1], pieces[1][1], pieces[0][2], pieces[1][2]] for pieces in pair]
        for pair in (((qkv_g_a0, qkv_g_b0), (rest_a0, rest_b0)), ((qkv_g_a1, qkv_g_b1), (rest_a1, rest_b1)))
    ]
    packed = []
    for grad_own, (qkv_t, in_t) in zip((grad1_low, grad2), stats):
        qkv_sum, in_sum = qkv_t[0] + qkv_t[1], in_t[0] + in_t[1]
        bias_sum = jnp.sum(grad_own.astype(f32), 0, keepdims=True)
        vectors = jnp.concatenate([qkv_sum[0:1], in_sum[0:1], qkv_sum[1:2], in_sum[1:2], bias_sum], 0)
        everywhere = vectors.reshape(5, n_tensor, n_dp, part).transpose(1, 2, 0, 3).reshape(n_tensor, n_dp, -1)
        halves_q = ordered(qkv_t[2][0].reshape(3, heads // 2), qkv_t[3][0].reshape(3, heads // 2))
        bias_q = jnp.concatenate(halves_q, 1).reshape(3, n_dp, part).transpose(1, 0, 2).reshape(n_dp, -1)
        bias_i = jnp.concatenate(ordered(in_t[2][0], in_t[3][0])).reshape(n_dp, -1)
        mine = jnp.concatenate([bias_q, bias_i], 1)
        only = (jnp.arange(n_tensor) == me)[:, None, None]
        packed.append(jnp.concatenate([everywhere, jnp.where(only, mine[None], 0.0)], 2))
    gp_a0, gp_b0, *packed = pin(gp_a0, gp_b0, *packed)

    def last_terms(half):
        return up_back((slots, slots), stay(gp_a0, gp_b0), stay(gi_a0, gi_b0), qkv0, in0, norms0, half)

    far = chip_sum(last_terms(1)).astype(bf16)
    far, gp_a0, gp_b0 = pin(far, gp_a0, gp_b0)
    near, beside = last_terms(0)
    near = (near, flip(beside, "tensor", 1))
    far = flip(far, "tensor", 2)
    total = pick(packed[0], packed[1]) + flip(pick(packed[1], packed[0]), "section")
    total = chosen(total, order, 0)
    small_sum = total[0::2] + flip(total[1::2], "tensor", 1)
    far, small_sum, reduced_qkv0, reduced_out0, *near = pin(far, small_sum, reduced_qkv0, reduced_out0, *near)
    near = near[0].astype(f32) + near[1].astype(f32)
    grad0 = input_back(h_own, grad1_low, near + far.astype(f32))
    grad_got = flip(pick(grad1_low, grad0.astype(bf16)), "section")

    total = small_sum
    total = total[0] + flip(total[1], "tensor", 2)
    sums = lax.psum_scatter(total, "dp", scatter_dimension=0) if not direct else None
    if direct:
        total = chosen(total, slots, 0)
        got = [lax.ppermute(total[hop], "dp", [(i, (i - hop) % n_dp) for i in range(n_dp)]) for hop in range(1, n_dp)]
        sums = sum(got, total[0])
    grad_got, sums = pin(grad_got, sums)

    activations = jnp.stack(ordered(pick(middle, final), act_got))
    input_grads = jnp.stack(ordered(pick(grad0, grad1_low.astype(f32)), grad_got.astype(f32)))

    def settled(one, two):
        got = flip(pick(two, one), "section")
        return [piece.astype(f32) for piece in ordered(pick(one, two), got)]

    rest_g = settled(jnp.concatenate([reduced_in0, reduced_out0], 1), reduced_rest1)
    qkv_g = settled(reduced_qkv0, reduced_qkv1)
    qkv_grad = jnp.concatenate([piece.reshape(-1, 3, heads // 2) for piece in qkv_g], 2)
    in_grad = jnp.concatenate([piece[:, :in_cols] for piece in rest_g], 1)
    dense_grad = jnp.concatenate([piece[:, in_cols : in_cols + heads // 2].T for piece in rest_g], 0)
    out_grad = jnp.concatenate([piece[:, in_cols + heads // 2 :].T for piece in rest_g], 0)

    return (
        activations[None],
        input_grads[None],
        qkv_grad[None],
        sums[5 * part : 8 * part].reshape(1, 3, part),
        dense_grad[None],
        in_grad[None],
        sums[8 * part :].reshape(1, -1),
        out_grad[None],
        sums[: 2 * part].reshape(1, 2, part),
        sums[2 * part : 4 * part].reshape(1, 2, part),
        jnp.stack([sums[4 * part : 5 * part]] * 2)[None],
    )


def solution(mesh):
    placed = (
        P("dp", "tensor", None),
        P("dp", "tensor", None),
        P("dp", None),
        P("section", "dp", None, "tensor"),
        P("section", None, ("tensor", "dp")),
        P("section", "tensor", "dp"),
        P("section", "dp", "tensor"),
        P("section", ("tensor", "dp")),
        P("section", "tensor", "dp"),
        P("section", None, ("tensor", "dp")),
        P("section", None, ("tensor", "dp")),
        P("section", None, ("tensor", "dp")),
    )
    return jax.shard_map(
        shards,
        mesh=mesh,
        in_specs=placed,
        out_specs=(
            P("section", "dp", "tensor", None),
            P("section", "dp", "tensor", None),
            P("section", "dp", None, "tensor"),
            P("section", None, ("tensor", "dp")),
            P("section", "tensor", "dp"),
            P("section", "dp", "tensor"),
            P("section", ("tensor", "dp")),
            P("section", "tensor", "dp"),
            P("section", None, ("tensor", "dp")),
            P("section", None, ("tensor", "dp")),
            P("section", None, ("tensor", "dp")),
        ),
        check_vma=False,
    )
```

```python
import functools
import math

import jax
import jax.numpy as jnp
from jax import lax
from jax.experimental import pallas as pl
from jax.experimental.pallas import tpu as pltpu
from jax.sharding import PartitionSpec as P

HDIM = 64
EPSILON = 1e-05
TILE = 512
KEYS = 512
NT = (((1,), (1,)), ((), ()))
NN = (((1,), (0,)), ((), ()))
TN = (((0,), (0,)), ((), ()))
LOG2E = math.log2(math.e)
FAR = 1e15
HURRY = 0.05
LIMIT = pltpu.CompilerParams(vmem_limit_bytes=20 * 2**20)


def mm(a, b, dims=NN):
    return lax.dot_general(a, b, dims, preferred_element_type=jnp.float32)


def cost(flops, moved, special=0):
    return pl.CostEstimate(flops=int(flops * HURRY), bytes_accessed=int(moved * HURRY), transcendentals=int(special))


def flip(block, axis, bit=1):
    return lax.ppermute(block, axis, [(i, i ^ bit) for i in range(lax.axis_size(axis))])


def turn(values, cosine, lead, trail):
    return values * cosine + pltpu.roll(values, 120, 1) * lead + pltpu.roll(values, 8, 1) * trail


def turn_back(grads, cosine, lead, trail):
    return grads * cosine - pltpu.roll(grads, 120, 1) * lead - pltpu.roll(grads, 8, 1) * trail


def head_part(block, head):
    lane = lax.broadcasted_iota(jnp.int32, block.shape, 1)
    return jnp.where((lane >= head * 64) & (lane < head * 64 + 64), block, jnp.zeros_like(block))


def tile_at(table, tile, size, shard_rows):
    per = shard_rows // size
    return pl.multiple_of(table[tile // per] * shard_rows + tile % per * size, size)


def below(query_tile, key_tile, keys, queries):
    rows = lax.broadcasted_iota(jnp.int32, (keys, queries), 0) + key_tile * keys
    cols = lax.broadcasted_iota(jnp.int32, (keys, queries), 1) + query_tile * queries
    return rows <= cols


def attend_kernel(shard_rows, table, q_ref, k_ref, v_ref, fq_ref, fk_ref, out_ref, lse_ref, vt, wides, tops, totals):
    step = pl.program_id(0)

    @pl.when(step == 0)
    def _():
        flipped = v_ref[...].T
        for head in range(2):
            vt[head, 0:64, :] = flipped[head * 64 : head * 64 + 64, :]
            vt[head, 64:80, :] = jnp.ones((16, flipped.shape[1]), jnp.bfloat16)

    for head in range(2):
        wides[head, :, 0:128] = head_part(q_ref[...], head)
        wides[head, :, 128:256] = fq_ref[...]
    tops[...] = jnp.full(tops.shape, -3e38, jnp.float32)
    totals[...] = jnp.zeros_like(totals)

    def tile(index, masked):
        at = tile_at(table, index, KEYS, shard_rows)
        keys = jnp.concatenate([k_ref[pl.ds(at, KEYS), :], fk_ref[pl.ds(at, KEYS), :]], 1)
        blocks = [mm(keys, wides[head], NT) for head in range(2)]
        blocks = [block * LOG2E for block in blocks]
        if masked:
            seen = below(step, index, KEYS, TILE)
            blocks = [jnp.where(seen, block, -1e30) for block in blocks]
        news = [jnp.maximum(tops[head], jnp.max(blocks[head], 0, keepdims=True)) for head in range(2)]
        probs = [jnp.exp2(blocks[head] - news[head]).astype(jnp.bfloat16) for head in range(2)]
        terms = [mm(vt[head, :, pl.ds(at, KEYS)], probs[head], NN) for head in range(2)]
        for head in range(2):
            totals[head] = totals[head] * jnp.exp2(tops[head] - news[head]) + terms[head]
            tops[head] = news[head]

    def loop(index, carry):
        tile(index, False)
        return carry

    whole = step * TILE // KEYS
    lax.fori_loop(0, whole, loop, 0)
    tile(whole, True)
    outs = []
    for head in range(2):
        norm = totals[head, 64:65, :]
        outs.append(totals[head, 0:64, :] / norm)
        lse_ref[head : head + 1, :] = tops[head] + jnp.log2(norm)
    lse_ref[2:8, :] = jnp.zeros((6, TILE), jnp.float32)
    out_ref[...] = jnp.concatenate(outs, 0).T.astype(jnp.bfloat16)


def attend(table, qkv, fq, fk):
    seq = qkv.shape[0]
    shard_rows = seq // 4
    per = shard_rows // TILE

    def place(step, table):
        return table[step // per] * per + step % per

    return pl.pallas_call(
        functools.partial(attend_kernel, shard_rows),
        grid_spec=pltpu.PrefetchScalarGridSpec(
            num_scalar_prefetch=1,
            grid=(seq // TILE,),
            in_specs=[
                pl.BlockSpec((TILE, 128), lambda i, t: (place(i, t), 0)),
                pl.BlockSpec((seq, 128), lambda i, t: (0, 1)),
                pl.BlockSpec((seq, 128), lambda i, t: (0, 2)),
                pl.BlockSpec((TILE, 128), lambda i, t: (place(i, t), 0)),
                pl.BlockSpec((seq, 128), lambda i, t: (0, 0)),
            ],
            out_specs=[
                pl.BlockSpec((TILE, 128), lambda i, t: (place(i, t), 0)),
                pl.BlockSpec((8, TILE), lambda i, t: (0, place(i, t))),
            ],
            scratch_shapes=[
                pltpu.VMEM((2, 80, seq), jnp.bfloat16),
                pltpu.VMEM((2, TILE, 256), jnp.bfloat16),
                pltpu.VMEM((2, 1, TILE), jnp.float32),
                pltpu.VMEM((2, 80, TILE), jnp.float32),
            ],
        ),
        out_shape=[
            jax.ShapeDtypeStruct((seq, 128), jnp.bfloat16),
            jax.ShapeDtypeStruct((8, seq), jnp.float32),
        ],
        compiler_params=LIMIT,
        cost_estimate=cost(4e9, 3e6, 5e6),
        name="attend",
    )(table, qkv, qkv, qkv, fq, fk)


def attend_back_kernel(shard_rows, table, q_ref, k_ref, v_ref, gm_ref, o_ref, lse_ref, fq_ref, fk_ref,
                       cos_ref, lead_ref, trail_ref, out_ref, kt, dk, dv, wides, grads, deltas, dq):
    step = pl.program_id(0)
    last = pl.num_programs(0) - 1 - step

    @pl.when(step == 0)
    def _():
        kt[...] = k_ref[...].T
        dk[...] = jnp.zeros_like(dk)
        dv[...] = jnp.zeros_like(dv)

    grad = gm_ref[...]
    product = grad.astype(jnp.float32) * o_ref[...].astype(jnp.float32)
    high = product.astype(jnp.bfloat16)
    low = (product - high.astype(jnp.float32)).astype(jnp.bfloat16)
    lane = lax.broadcasted_iota(jnp.int32, (8, 128), 1)
    for head in range(2):
        ones = jnp.where((lane >= head * 64) & (lane < head * 64 + 64), 1.0, 0.0).astype(jnp.bfloat16)
        deltas[head] = (mm(ones, high, NT) + mm(ones, low, NT))[0:1, :]
        wides[head, :, 0:128] = head_part(q_ref[...], head)
        wides[head, :, 128:256] = fq_ref[...]
        grads[head] = head_part(grad, head)
    dq[...] = jnp.zeros_like(dq)

    def tile(index, masked):
        at = tile_at(table, index, KEYS, shard_rows)
        rows = pl.ds(at, KEYS)
        keys = jnp.concatenate([k_ref[rows, :], fk_ref[rows, :]], 1)
        values = v_ref[rows, :]
        blocks = [mm(keys, wides[head], NT) for head in range(2)]
        backs = [mm(values, grads[head], NT) for head in range(2)]
        probs = [jnp.exp2(blocks[head] * LOG2E - lse_ref[head : head + 1, :]) for head in range(2)]
        if masked:
            seen = below(last, index, KEYS, TILE)
            probs = [jnp.where(seen, one, 0.0) for one in probs]
        slopes = [(probs[head] * (backs[head] - deltas[head])).astype(jnp.bfloat16) for head in range(2)]
        probs = [one.astype(jnp.bfloat16) for one in probs]
        dv[rows, :] += mm(jnp.concatenate(probs, 1), grads[...].reshape(2 * TILE, 128), NN)
        dk[rows, :] += mm(jnp.concatenate(slopes, 1), wides[:, :, 0:128].reshape(2 * TILE, 128), NN)
        for head in range(2):
            dq[head * 64 : head * 64 + 64, :] += mm(kt[head * 64 : head * 64 + 64, rows], slopes[head], NN)

    def loop(index, carry):
        tile(index, False)
        return carry

    whole = last * TILE // KEYS
    lax.fori_loop(0, whole, loop, 0)
    tile(whole, True)
    here = pl.ds(tile_at(table, last, TILE, shard_rows), TILE)
    turns = (cos_ref[...], lead_ref[...], trail_ref[...])
    out_ref[:, 0:128] = turn_back(dq[...].T * 0.125, *turns).astype(jnp.bfloat16)
    out_ref[:, 128:256] = turn_back(dk[here, :], *turns).astype(jnp.bfloat16)
    out_ref[:, 256:384] = dv[here, :].astype(jnp.bfloat16)


def attend_back(table, qkv, grad_mixed, mixed, lse, fq, fk, turns):
    seq = qkv.shape[0]
    shard_rows = seq // 4
    tiles = seq // TILE
    per = shard_rows // TILE

    def place(step, table):
        tile = tiles - 1 - step
        return table[tile // per] * per + tile % per

    block = pl.BlockSpec((TILE, 128), lambda i, t: (place(i, t), 0))
    return pl.pallas_call(
        functools.partial(attend_back_kernel, shard_rows),
        grid_spec=pltpu.PrefetchScalarGridSpec(
            num_scalar_prefetch=1,
            grid=(tiles,),
            in_specs=[
                block,
                pl.BlockSpec((seq, 128), lambda i, t: (0, 1)),
                pl.BlockSpec((seq, 128), lambda i, t: (0, 2)),
                block,
                block,
                pl.BlockSpec((8, TILE), lambda i, t: (0, place(i, t))),
                block,
                pl.BlockSpec((seq, 128), lambda i, t: (0, 0)),
                block,
                block,
                block,
            ],
            out_specs=pl.BlockSpec((TILE, 384), lambda i, t: (place(i, t), 0)),
            scratch_shapes=[
                pltpu.VMEM((128, seq), jnp.bfloat16),
                pltpu.VMEM((seq, 128), jnp.float32),
                pltpu.VMEM((seq, 128), jnp.float32),
                pltpu.VMEM((2, TILE, 256), jnp.bfloat16),
                pltpu.VMEM((2, TILE, 128), jnp.bfloat16),
                pltpu.VMEM((2, 1, TILE), jnp.float32),
                pltpu.VMEM((128, TILE), jnp.float32),
            ],
        ),
        out_shape=pltpu.HBM((seq, 384), jnp.bfloat16),
        compiler_params=LIMIT,
        cost_estimate=cost(10e9, 6e6, 5e6),
        name="attend_back",
    )(table, qkv, qkv, qkv, grad_mixed, mixed, lse, fq, fk, *turns)


def normal_of(values):
    centered = values - jnp.mean(values, -1, keepdims=True)
    inverse = lax.rsqrt(jnp.mean(centered * centered, -1, keepdims=True) + EPSILON)
    return centered * inverse, inverse


def whole_of(array):
    return pl.BlockSpec(array.shape, lambda *i: (0,) * array.ndim)


def heads_of(first, weight, bias, turns, out_ref):
    projected = mm(first, weight) + bias
    for part in range(3):
        piece = projected[:, 128 * part : 128 * part + 128]
        if part < 2:
            piece = turn(piece, *turns)
        if part == 0:
            piece = piece * 0.125
        out_ref[:, 128 * part : 128 * part + 128] = piece.astype(jnp.bfloat16)


def settle(slots, source, target, start=0):
    @pl.when(pl.program_id(0) == 0)
    def _():
        rows = target.shape[0] // source.shape[0]
        for block in range(source.shape[0]):
            target[block * rows : block * rows + rows, :] = source[slots[block], 0:rows, start : start + target.shape[1]]


def weight_scratch(width, weight, cols=None):
    return pltpu.VMEM((width, cols or weight.shape[2]), weight.dtype)


def choose(pieces, target):
    for step, piece in enumerate(pieces):

        @pl.when(pl.program_id(0) == step)
        def _():
            target[...] = piece[...]


def call(kernel, name, grid, in_specs, out_specs, out_shape, scratch, flops, moved, special=0, scalars=1, aliases=None):
    return pl.pallas_call(
        kernel,
        grid_spec=pltpu.PrefetchScalarGridSpec(
            num_scalar_prefetch=scalars, grid=grid, in_specs=in_specs, out_specs=out_specs, scratch_shapes=scratch
        ),
        out_shape=out_shape,
        compiler_params=LIMIT,
        cost_estimate=cost(flops, moved, special),
        input_output_aliases=aliases or {},
        name=name,
    )


def struct(*shape, far=False):
    return pltpu.HBM(shape, jnp.bfloat16) if far else jax.ShapeDtypeStruct(shape, jnp.bfloat16)


def stay(*arrays):
    return [pltpu.with_memory_space_constraint(array, pltpu.HBM) for array in arrays]


def project_kernel(
    slots, h0, h1, h2, h3, weight_ref, bias_ref, norm_ref, cos_ref, lead_ref, trail_ref,
    out_ref, first_ref, second_ref, flip_ref, weight, h_ref
):
    settle(slots, weight_ref, weight)
    choose((h0, h1, h2, h3), h_ref)
    normal, _ = normal_of(h_ref[...].astype(jnp.float32))
    flip_ref[...] = normal.astype(jnp.bfloat16).T
    first = (normal * norm_ref[0:1, :] + norm_ref[2:3, :]).astype(jnp.bfloat16)
    first_ref[...] = first
    second_ref[...] = (normal * norm_ref[1:2, :] + norm_ref[3:4, :]).astype(jnp.bfloat16)
    heads_of(first, weight[...], bias_ref[0:1, 0 : weight.shape[1]], (cos_ref[...], lead_ref[...], trail_ref[...]), out_ref)


def project(slots, pieces, weight, cols, bias, norms, turns, far=False):
    rows, width = pieces[0].shape
    seq = rows * len(pieces)
    block = pl.BlockSpec((rows, width), lambda i, s: (i, 0))
    return call(
        project_kernel,
        "project",
        (seq // rows,),
        [whole_of(x) for x in (*pieces, weight, bias, norms)] + [pl.BlockSpec((rows, 128), lambda i, s: (i, 0))] * 3,
        [pl.BlockSpec((rows, cols), lambda i, s: (i, 0)), block, block, pl.BlockSpec((width, rows), lambda i, s: (0, i))],
        [struct(seq, cols)] + [struct(*shape, far=far) for shape in ((seq, width), (seq, width), (width, seq))],
        [weight_scratch(width, weight, cols), pltpu.VMEM((rows, width), jnp.bfloat16)],
        4e9,
        18e6,
    )(slots, *pieces, weight, bias, norms, *turns)


def project_more_kernel(slots, first_ref, weight_ref, bias_ref, cos_ref, lead_ref, trail_ref, out_ref, weight):
    settle(slots, weight_ref, weight)
    heads_of(
        first_ref[...], weight[...], bias_ref[1:2, 0 : weight.shape[1]], (cos_ref[...], lead_ref[...], trail_ref[...]), out_ref
    )


def project_more(slots, first, weight, cols, bias, turns):
    seq, width = first.shape
    rows = 512
    return call(
        project_more_kernel,
        "project_more",
        (seq // rows,),
        [pl.BlockSpec((rows, width), lambda i, s: (i, 0)), whole_of(weight), whole_of(bias)]
        + [pl.BlockSpec((rows, 128), lambda i, s: (i, 0))] * 3,
        pl.BlockSpec((rows, cols), lambda i, s: (i, 0)),
        struct(seq, cols),
        [weight_scratch(width, weight, cols)],
        3e9,
        8e6,
    )(slots, first, weight, bias, *turns)


def gelu_kernel(part, slots, a_ref, weight_ref, bias_ref, out_ref, slope_ref, weight):
    settle(slots, weight_ref, weight, weight_ref.shape[2] - weight.shape[1])
    inner = mm(a_ref[...], weight[...]) + bias_ref[part : part + 1, bias_ref.shape[1] - weight.shape[1] :]
    size = jnp.abs(inner)
    t = 1.0 / (1.0 + (0.3275911 * math.sqrt(0.5)) * size)
    bell = jnp.exp2((-0.5 * LOG2E) * inner * inner)
    poly = 0.5 * 1.061405429 * t + 0.5 * -1.453152027
    poly = poly * t + 0.5 * 1.421413741
    poly = poly * t + 0.5 * -0.284496736
    poly = poly * t + 0.5 * 0.254829592
    tail = poly * t * bell
    below = jnp.where(inner >= 0, 1.0 - tail, tail)
    out_ref[...] = (inner * below).astype(jnp.bfloat16)
    slope_ref[...] = (below + inner * bell * (1.0 / math.sqrt(2 * math.pi))).astype(jnp.bfloat16)


def gelu_up(slots, second, weight, cols, bias, part, far=False):
    seq, width = second.shape
    rows = 256
    block = pl.BlockSpec((rows, cols), lambda i, s: (i, 0))
    return call(
        functools.partial(gelu_kernel, part),
        "gelu_up",
        (seq // rows,),
        [pl.BlockSpec((rows, width), lambda i, s: (i, 0)), whole_of(weight), whole_of(bias)],
        [block, block],
        [struct(seq, cols), struct(seq, cols, far=far)],
        [weight_scratch(width, weight, cols)],
        5e9,
        10e6,
        2e6,
    )(slots, second, weight, bias)


def deal(value, *targets):
    for step, target in enumerate(targets):

        @pl.when(pl.program_id(0) == step)
        def _():
            target[...] = value


def down_kernel(slots, mixed_mine, mixed_other, act_mine, act_other, mine_ref, other_ref, near_ref, beside_ref, mine, other):
    settle(slots, mine_ref, mine)
    settle(slots, other_ref, other)
    heads = mixed_mine.shape[1]
    total = mm(mixed_mine[...], mine[:, 0:heads], NT) + mm(act_mine[...], mine[:, heads:], NT)
    total += mm(mixed_other[...], other[:, 0:heads], NT) + mm(act_other[...], other[:, heads:], NT)
    deal(total.astype(jnp.bfloat16), near_ref, beside_ref)


def down(slots, mixed, act, weights, half):
    seq = mixed[0].shape[0]
    width = weights[0].shape[0] * weights[0].shape[1]
    rows = 512
    steps = seq // rows // 2
    return call(
        down_kernel,
        "down",
        (steps,),
        [pl.BlockSpec((rows, x.shape[1]), lambda i, s: (i + half * steps, 0)) for x in (*mixed, *act)]
        + [whole_of(w) for w in weights],
        [pl.BlockSpec((rows, width), lambda i, s: (0, 0))] * 2,
        [struct(rows, width)] * 2,
        [weight_scratch(width, w) for w in weights],
        4e9,
        8e6,
    )(slots, *mixed, *act, *weights)


def down_back_kernel(
    slots, g0, g1, g2, g3, slope_mine, slope_other, mine_ref, other_ref,
    mixed_mine, mixed_other, inner_mine, inner_other, flip_ref, mine, other, grad_ref
):
    choose((g0, g1, g2, g3), grad_ref)
    settle(slots, mine_ref, mine)
    settle(slots, other_ref, other)
    heads = mixed_mine.shape[1]
    flip_ref[...] = grad_ref[...].T
    for slope, weight, mixed, inner in (
        (slope_mine, mine, mixed_mine, inner_mine),
        (slope_other, other, mixed_other, inner_other),
    ):
        mixed[...] = mm(grad_ref[...], weight[:, 0:heads]).astype(jnp.bfloat16)
        inner[...] = (mm(grad_ref[...], weight[:, heads:]) * slope[...].astype(jnp.float32)).astype(jnp.bfloat16)


def down_back(slots, pieces, slopes, weights, heads, far=False):
    rows, width = pieces[0].shape
    seq = rows * len(pieces)
    hidden = slopes[0].shape[1]
    wide = pl.BlockSpec((rows, hidden), lambda i, s: (i, 0))
    return call(
        down_back_kernel,
        "down_back",
        (seq // rows,),
        [whole_of(x) for x in pieces] + [wide, wide] + [whole_of(w) for w in weights],
        [pl.BlockSpec((rows, heads), lambda i, s: (i, 0))] * 2 + [wide, wide, pl.BlockSpec((width, rows), lambda i, s: (0, i))],
        [struct(seq, heads)] * 2 + [struct(seq, hidden, far=far)] * 2 + [struct(width, seq, far=far)],
        [weight_scratch(width, w) for w in weights] + [pltpu.VMEM((rows, width), jnp.bfloat16)],
        8e9,
        18e6,
    )(slots, *pieces, *slopes, *weights)


def up_back_kernel(
    slots, in_slots, proj_mine, proj_other, inner_mine, inner_other, qkv_mine, qkv_other, in_mine, in_other, gain_ref, near_ref, beside_ref, *weights
):
    for source, target in zip((qkv_mine, qkv_other), weights[:2]):
        settle(slots, source, target)
    for source, target in zip((in_mine, in_other), weights[2:]):
        settle(in_slots, source, target, source.shape[2] - target.shape[1])
    qkv_a, qkv_b, in_a, in_b = weights
    first = mm(proj_mine[...], qkv_a[...], NT) + mm(proj_other[...], qkv_b[...], NT)
    second = mm(inner_mine[...], in_a[...], NT) + mm(inner_other[...], in_b[...], NT)
    deal((first * gain_ref[0:1, :] + second * gain_ref[1:2, :]).astype(jnp.bfloat16), near_ref, beside_ref)


def up_back(slots, proj, inner, qkv_w, in_w, gains, half):
    seq = proj[0].shape[0]
    width = gains.shape[1]
    rows = 512
    steps = seq // rows // 2
    return call(
        up_back_kernel,
        "up_back",
        (steps,),
        [pl.BlockSpec((rows, x.shape[1]), lambda i, *s: (i + half * steps, 0)) for x in (*proj, *inner)]
        + [whole_of(w) for w in (*qkv_w, *in_w, gains)],
        [pl.BlockSpec((rows, width), lambda i, *s: (0, 0))] * 2,
        [struct(rows, width)] * 2,
        [weight_scratch(width, w, x.shape[1]) for w, x in zip((*qkv_w, *in_w), (*proj, *inner))],
        4e9,
        10e6,
        scalars=2,
    )(*slots, *proj, *inner, *qkv_w, *in_w, gains)


def grads_kernel(ups, downs, adds, slots, *refs):
    refs = list(refs)
    normal = refs.pop(0) if ups else None
    flipped = refs.pop(0) if downs else None
    backs = [refs.pop(0) for _ in range(ups)]
    sources = [refs.pop(0) for _ in range(downs)]
    weights = [refs.pop(0) for _ in range(ups)]
    norm_ref = refs.pop(0)
    got_ref = refs.pop(0) if adds else None
    out_ref = refs.pop(0)
    row = 1 if downs else 0
    norm = norm_ref[...].T
    gain_column, bias_column = norm[:, row : row + 1], norm[:, 2 + row : 3 + row]

    def store(first, last, value):
        if adds:
            value += got_ref[0, :, first:last].astype(jnp.float32)
        out_ref[0, :, first:last] = value.astype(jnp.bfloat16)

    at = 0
    for k in range(ups):
        stat_ref, sum_ref = refs[2 * k : 2 * k + 2]
        cols = backs[k].shape[1]
        raw = mm(normal[...], backs[k][...])
        total = mm(jnp.ones((8, backs[k].shape[0]), jnp.bfloat16), backs[k][...])
        sum_ref[...] = total
        total = total[0:1, :]
        store(at, at + cols, raw * gain_column + total * bias_column)
        first = weights[k].shape[2] - cols if downs else 0
        wide = weights[k][0, :, first : first + cols].astype(jnp.float32)
        gain = jnp.sum(raw * wide, 1, keepdims=True)
        shift = jnp.sum(wide * total, 1, keepdims=True)
        lane = lax.broadcasted_iota(jnp.int32, (raw.shape[0], 128), 1)
        stat_ref[...] = jnp.where(lane == 0, gain, jnp.where(lane == 1, shift, 0.0)).T[0:8, :]
        at += cols
    for source in sources:
        cols = source.shape[1]
        store(at, at + cols, mm(flipped[...], source[...]))
        at += cols


def weight_grads(slots, normal, flipped, ups, downs, norms, got=None):
    width, seq = (normal if ups else flipped).shape
    groups = 4
    rows = width // groups
    strip = pl.BlockSpec((rows, seq), lambda i, s: (i, 0))
    args, specs = [], []
    for array, used in ((normal, ups), (flipped, downs)):
        if used:
            args.append(array)
            specs.append(strip)
    for array in [back for back, _ in ups] + list(downs):
        args.append(array)
        specs.append(whole_of(array))
    for _, weight in ups:
        args.append(weight)
        specs.append(pl.BlockSpec((1, rows, weight.shape[2]), lambda i, s: (s[i], 0, 0)))
    args.append(norms)
    specs.append(pl.BlockSpec((norms.shape[0], rows), lambda i, s: (0, i)))
    cols = sum(back.shape[1] for back, _ in ups) + sum(source.shape[1] for source in downs)
    out_specs = [pl.BlockSpec((1, rows, cols), lambda i, s: (i, 0, 0))]
    if got is not None:
        args.append(got)
        specs.append(out_specs[0])
    out_shape = [struct(groups, rows, cols, far=True)]
    for back, _ in ups:
        out_specs += [pl.BlockSpec((8, rows), lambda i, s: (0, i)), pl.BlockSpec((8, back.shape[1]), lambda i, s: (0, 0))]
        out_shape += [pltpu.HBM((8, width), jnp.float32), pltpu.HBM((8, back.shape[1]), jnp.float32)]
    return call(
        functools.partial(grads_kernel, len(ups), len(downs), got is not None),
        "weight_grads",
        (groups,),
        specs,
        out_specs,
        out_shape,
        [],
        2 * seq * width * cols,
        8e6,
    )(slots, *args)


def shards(
    inputs,
    cotangent,
    lengths,
    qkv_weight,
    qkv_bias,
    dense_weight,
    in_weight,
    in_bias,
    out_weight,
    norm_gains,
    norm_biases,
    out_biases,
):
    f32, bf16 = jnp.float32, jnp.bfloat16
    lefthand = lax.axis_index("section") == 0
    me, depth = lax.axis_index("tensor"), lax.axis_index("dp")
    n_tensor, n_dp = lax.axis_size("tensor"), lax.axis_size("dp")
    shard_rows, width = inputs.shape[1:]
    heads = qkv_weight.shape[3]
    hidden = in_weight.shape[2]
    groups = 4
    direct = n_dp == groups

    def pick(first, second):
        return jnp.where(lefthand, first, second)

    def ordered(mine, other):
        return pick(mine, other), pick(other, mine)

    def gather_deep(piece):
        if not direct:
            return lax.all_gather(piece, "dp", axis=0, tiled=True).reshape(groups, -1, piece.shape[1])
        pieces = [piece]
        for hop in range(1, n_dp):
            pieces.append(lax.ppermute(piece, "dp", [(i, (i + hop) % n_dp) for i in range(n_dp)]))
        return jnp.stack(pieces)

    def scatter_late(total):
        return lax.psum_scatter(total.reshape(-1, total.shape[2]), "dp", scatter_dimension=0, tiled=True)

    def pin(*values):
        return lax.optimization_barrier(values)

    h_own = pick(inputs[0], inputs[1])
    cot = pick(cotangent[0], cotangent[1])
    row = pick(lengths[0], lengths[1])

    def halves(group):
        return pick(group[0], group[1]), pick(group[1], group[0])

    def cut(array, axis, k):
        size = array.shape[axis] // 2
        return lax.slice_in_dim(array, k * size, k * size + size, axis=axis)

    small = jnp.concatenate([piece[0].reshape(-1) for piece in (qkv_bias, norm_gains, norm_biases, out_biases, in_bias)])
    part = qkv_bias.shape[2]
    n_small = small.shape[0]
    qkv_cols, in_cols = 3 * heads // 2, hidden // 2
    qkv_half = halves([cut(qkv_weight[0], 2, k).reshape(-1, qkv_cols) for k in range(2)])
    qkv_got = flip(qkv_half[1], "section")
    pair = jnp.stack([small, flip(small, "tensor", 2)])
    h_own, pair = pin(h_own, pair)
    h_far = flip(h_own, "tensor", 2)
    pair = jnp.stack([pair, flip(pair, "tensor", 1)], 1)
    pair = jnp.stack(ordered(pair, flip(pair, "section"))).reshape(-1)
    extra = -(-pair.shape[0] // (16 * qkv_cols)) * 16
    pair = jnp.zeros((extra * qkv_cols,), bf16).at[: pair.shape[0]].set(pair).reshape(extra, qkv_cols)
    deep = qkv_half[0].shape[0]
    qkv_shard = ordered(qkv_half[0], qkv_got)
    first = jnp.concatenate([qkv_shard[0], pair], 0)
    zero = jnp.zeros((), jnp.int32)
    first, row, zero, cot, in_weight, dense_weight, out_weight = pin(
        first, row, zero, cot, in_weight, dense_weight, out_weight
    )
    rest_half = halves(
        [
            jnp.concatenate([cut(in_weight[0], 1, k), cut(dense_weight[0], 0, k).T, cut(out_weight[0], 0, k).T], 1)
            for k in range(2)
        ]
    )
    first = gather_deep(first) if direct else lax.all_gather(first, "dp", axis=0)

    steps = zero + jnp.arange(groups, dtype=jnp.int32)
    slots = (depth - steps) % groups if direct else steps
    rest_mine, rest_got = rest_half[0], flip(rest_half[1], "section")
    qkv0 = first if direct else first[:, :deep].reshape(groups, -1, qkv_cols)
    pair = first[:, deep:].reshape(n_dp, -1)[:, : 2 * n_tensor * n_small].reshape(n_dp, 2, n_tensor, n_small)
    order = (zero + jnp.arange(n_tensor)) ^ me
    small_all = pair.astype(f32).transpose(1, 2, 0, 3)

    def chosen(array, index, axis):
        size = index.shape[0]
        shape = [1] * array.ndim
        shape[axis] = size
        return sum(
            jnp.where(index.reshape(shape) == place, lax.slice_in_dim(array, place, place + 1, axis=axis), 0.0)
            for place in range(size)
        )

    if direct:
        small_all = chosen(small_all, slots, 2)
    here = small_all[:, 0]
    small_all = chosen(small_all, order, 1)

    def gather_early(piece):
        return lax.all_gather(piece, "dp", axis=0, tiled=True).reshape(groups, -1, piece.shape[1])

    def shares(rest):
        return rest[:, :in_cols], rest[:, in_cols:]

    table = jnp.arange(n_tensor, dtype=jnp.int32) ^ me
    positions = jnp.concatenate(
        [slot * shard_rows + zero + jnp.arange(shard_rows, dtype=jnp.int32) for slot in (me, me ^ 1, me ^ 2, me ^ 3)]
    )
    ends = jnp.cumsum(row)
    passed = positions[:, None] >= ends[None, :]
    doc = jnp.sum(passed.astype(jnp.int32), -1)
    offset = positions - jnp.sum(jnp.where(passed, row[None, :], 0), -1)
    valid_own = (positions < ends[-1])[:shard_rows]
    lane = jnp.arange(128, dtype=jnp.int32) + zero
    same = doc[:, None] == lane[None, :]
    feats_q = jnp.where(same, -FAR, 0.0).astype(bf16)
    feats_k = jnp.where(same | (lane[None, :] > row.shape[0]), 0.0, FAR).astype(bf16)
    place = lane % HDIM
    rotary = HDIM // 4
    counter = (place % (rotary // 2)).astype(f32)
    inverse = jnp.exp(counter * (-2.0 * math.log(10000.0) / rotary))
    angles = offset.astype(f32)[:, None] * inverse[None, :]
    turned = (place < rotary)[None, :]
    sine = jnp.sin(angles)
    rotary_turns = (
        jnp.where(turned, jnp.cos(angles), 1.0),
        jnp.where((place < rotary // 2)[None, :], -sine, 0.0),
        jnp.where(turned & (place >= rotary // 2)[None, :], sine, 0.0),
    )

    rows_all = small_all[..., 3 * part : 9 * part].reshape(2, n_tensor, n_dp, 6, part).transpose(0, 3, 1, 2, 4)
    rows_all = jnp.pad(rows_all.reshape(2, 6, width), ((0, 0), (0, 2), (0, 0)))
    qkv_parts = here[..., : 3 * part].reshape(2, n_dp, 3, part).transpose(0, 2, 1, 3).reshape(2, 3, 2, heads // 2)
    qkv_parts = qkv_parts.transpose(0, 2, 1, 3).reshape(2, 2, qkv_cols)
    bias_all = jnp.concatenate([qkv_parts, here[..., 9 * part : n_small].reshape(2, 2, in_cols)], 2)
    bias_all = jnp.stack(ordered(bias_all[:, 0], bias_all[:, 1]), 1)

    def chip_sum(terms):
        return terms[0].astype(f32) + flip(terms[1], "tensor", 1).astype(f32)

    def branch_sum(make):
        far = chip_sum(make(1)).astype(bf16)
        return chip_sum(make(0)), far

    def result_of(own, near, far, rows):
        return (own.astype(f32) + near + far.astype(f32) + rows[4:5] + rows[5:6]).astype(bf16)

    def input_back(own, grad_own, partial):
        n, inverse = normal_of(own.astype(f32))
        return grad_own.astype(f32) + inverse * (
            partial - jnp.mean(partial, -1, keepdims=True) - n * jnp.mean(partial * n, -1, keepdims=True)
        )

    def attend_one(qkv):
        return attend(table, qkv, feats_q, feats_k)

    def attend_back_one(qkv, attended, grad_mixed):
        mixed, lse = attended
        return attend_back(table, qkv, grad_mixed, mixed, lse, feats_q, feats_k, stay(*rotary_turns))

    def rows_of(own, far):
        return own, flip(own, "tensor", 1), far, flip(far, "tensor", 1)

    in_shard0 = pick(rest_mine[:, :in_cols], rest_got[:, :in_cols])
    qkv0, rows_all, bias_all, in_shard0, *h_all = pin(qkv0, rows_all, bias_all, in_shard0, *rows_of(h_own, h_far))
    in0 = gather_deep(in_shard0)
    (norms0, norms1), (bias0, bias1) = rows_all, bias_all
    qkv0_other = flip(qkv0, "section")
    qkv_a0, normed, second, normal0 = project(slots, h_all, qkv0, qkv_cols, bias0, norms0, rotary_turns, True)
    qkv_a0, cot, rest_mine, rest_got = pin(qkv_a0, cot, rest_mine, rest_got)
    rest0, rest1 = ordered(rest_mine, rest_got)
    (_, out_shard0), (in_shard1, out_shard1) = shares(rest0), shares(rest1)
    grad2 = cot * valid_own[:, None].astype(bf16)
    grad2_far = flip(grad2, "tensor", 2)
    mixed_a0 = attend_one(qkv_a0)
    in0, qkv0_other, normed, out_shard0, *mixed_a0 = pin(in0, qkv0_other, normed, out_shard0, *mixed_a0)
    out0 = gather_early(out_shard0)
    in0_other = flip(in0, "section")
    qkv0 = stay(qkv0, qkv0_other)
    qkv_b0 = project_more(slots, *stay(normed), qkv0[1], qkv_cols, bias0, rotary_turns)
    mixed_b0 = attend_one(qkv_b0)
    second, grad2_far, in0_other, *mixed_b0 = pin(second, grad2_far, in0_other, *mixed_b0)
    in0 = stay(in0, in0_other)
    hid_a0 = gelu_up(slots, *stay(second), in0[0], in_cols, bias0, 0, True)
    grad_all1 = rows_of(grad2, grad2_far)
    second, out0, hid_a0, qkv_shard1 = pin(second, out0, hid_a0, qkv_shard[1])
    qkv1 = gather_deep(qkv_shard1)
    out0 = stay(out0, flip(out0, "section"))
    hid_b0 = gelu_up(slots, *stay(second), in0[1], in_cols, bias0, 1, True)
    mixed0 = (mixed_a0[0], mixed_b0[0])
    hid_b0, qkv1, in_shard1 = pin(hid_b0, qkv1, in_shard1)
    in1 = gather_early(in_shard1)
    far = chip_sum(down(steps, stay(*mixed0), stay(hid_a0[0], hid_b0[0]), out0, 1)).astype(bf16)
    far, mixed0, qkv1, *grad_all1 = pin(far, mixed0, qkv1, *grad_all1)
    qkv1_other = flip(qkv1, "section")
    near = chip_sum(down(steps, stay(*mixed0), stay(hid_a0[0], hid_b0[0]), out0, 0))
    middle = result_of(h_own, near, flip(far, "tensor", 2), norms0)
    middle, qkv1_other, out_shard1 = pin(middle, qkv1_other, out_shard1)
    out1 = gather_early(out_shard1)

    h_all = rows_of(middle, flip(middle, "tensor", 2))
    in1, *h_all = pin(in1, *h_all)
    in1_other = flip(in1, "section")
    qkv1 = (qkv1, qkv1_other)
    qkv_a1, normed, second, normal1 = project(slots, h_all, qkv1[0], qkv_cols, bias1, norms1, rotary_turns)
    mixed_a1 = attend_one(qkv_a1)
    normed, out1, in1_other, *mixed_a1 = pin(normed, out1, in1_other, *mixed_a1)
    in1 = (in1, in1_other)
    out1_other = flip(out1, "section")
    qkv_b1 = project_more(slots, normed, qkv1[1], qkv_cols, bias1, rotary_turns)
    mixed_b1 = attend_one(qkv_b1)
    second, *mixed_b1 = pin(second, *mixed_b1)
    hid_a1 = gelu_up(steps, second, in1[0], in_cols, bias1, 0)
    hid_b1 = gelu_up(steps, second, in1[1], in_cols, bias1, 1)
    mixed1 = (mixed_a1[0], mixed_b1[0])
    out1_other, hid_a1, hid_b1 = pin(out1_other, hid_a1, hid_b1)
    out1 = (out1, out1_other)

    gm_a, gm_b, gi_a1, gi_b1, flipped1 = down_back(steps, grad_all1, (hid_a1[1], hid_b1[1]), out1, heads // 2)

    def rest_grads(blocks, normal, flipped, gi, in_w, mixed, hid, norms, got=None):
        return weight_grads(blocks, normal, flipped, ((gi, in_w),), (mixed, hid[0]), norms, got)

    def qkv_grads(blocks, normal, gp, qkv_w, norms, got=None):
        return weight_grads(blocks, normal, None, ((*stay(gp), qkv_w),), (), norms, got)

    rest_b1 = rest_grads(steps, normal1, flipped1, gi_b1, in1[1], mixed1[1], hid_b1, norms1)
    gm_a, gm_b, rest_b1_grad = pin(gm_a, gm_b, rest_b1[0])
    rest_got1 = flip(rest_b1_grad, "section")
    gp_b1 = attend_back_one(qkv_b1, mixed_b1, gm_b)
    gm_a, gp_b1, normal1 = pin(gm_a, gp_b1, normal1)
    qkv_g_b1 = qkv_grads(slots, normal1, gp_b1, qkv1[1], norms1)
    gm_a, gp_b1, qkv_b1_grad = pin(gm_a, gp_b1, qkv_g_b1[0])
    gp_a1 = attend_back_one(qkv_a1, mixed_a1, gm_a)
    gp_a1, rest_got1 = pin(gp_a1, rest_got1)
    near, far = branch_sum(lambda half: up_back((slots, steps), stay(gp_a1, gp_b1), stay(gi_a1, gi_b1), qkv1, in1, norms1, half))
    far, normal1, flipped1, rest_got1 = pin(far, normal1, flipped1, rest_got1)
    far = flip(far, "tensor", 2)
    rest_a1 = rest_grads(steps, normal1, flipped1, gi_a1, in1[0], mixed1[0], hid_a1, norms1, rest_got1)
    normal1, rest_a1_grad, qkv_b1_grad, mixed1_a, mixed1_b = pin(normal1, rest_a1[0], qkv_b1_grad, *mixed1)
    qkv_got1 = flip(qkv_b1_grad, "section")
    final_far = chip_sum(down(steps, stay(mixed1_a, mixed1_b), stay(hid_a1[0], hid_b1[0]), stay(*out1), 1)).astype(bf16)
    far, normal1, rest_a1_grad = pin(far, normal1, rest_a1_grad)
    grad1 = input_back(middle, grad2, near + far.astype(f32))
    grad1_low = grad1.astype(bf16)
    grad1_low, rest_a1_grad, normal1, final_far, mixed1_a, mixed1_b = pin(
        grad1_low, rest_a1_grad, normal1, final_far, mixed1_a, mixed1_b
    )
    grad1_far = flip(grad1_low, "tensor", 2)
    reduced_rest1 = scatter_late(rest_a1_grad)
    near_terms = down(steps, stay(mixed1_a, mixed1_b), stay(hid_a1[0], hid_b1[0]), stay(*out1), 0)
    qkv_got1, normal1, *near_terms = pin(qkv_got1, normal1, *near_terms)
    qkv_g_a1 = qkv_grads(slots, normal1, gp_a1, qkv1[0], norms1, qkv_got1)
    grad1_far, qkv_a1_grad = pin(grad1_far, qkv_g_a1[0])
    grad_all0 = rows_of(grad1_low, grad1_far)
    final_far, *grad_all0 = pin(final_far, *grad_all0)
    final_far = flip(final_far, "tensor", 2)

    (normal0,) = stay(normal0)
    gm_a, gm_b, gi_a0, gi_b0, flipped0 = down_back(steps, grad_all0, stay(hid_a0[1], hid_b0[1]), out0, heads // 2, True)
    rest_b0 = rest_grads(slots, normal0, flipped0, gi_b0, in0[1], mixed0[1], hid_b0, norms0)
    gm_a, gm_b, rest_b0_grad, qkv_a1_grad, reduced_rest1 = pin(gm_a, gm_b, rest_b0[0], qkv_a1_grad, reduced_rest1)
    rest_got0 = flip(rest_b0_grad, "section")
    reduced_qkv1 = scatter_late(qkv_a1_grad)
    gp_b0 = attend_back_one(*stay(qkv_b0), stay(*mixed_b0), gm_b)
    gp_b0, gm_a, normal0, final_far = pin(gp_b0, gm_a, normal0, final_far)
    final = result_of(middle, chip_sum(near_terms), final_far, norms1)
    qkv_g_b0 = qkv_grads(slots, normal0, gp_b0, qkv0[1], norms0)
    normal0, qkv_b0_grad = pin(normal0, qkv_g_b0[0])
    rest_a0 = rest_grads(slots, normal0, flipped0, gi_a0, in0[0], mixed0[0], hid_a0, norms0)
    gm_a, qkv_b0_grad, rest_a0_grad, rest_got0, final, reduced_qkv1 = pin(
        gm_a, qkv_b0_grad, rest_a0[0], rest_got0, final, reduced_qkv1
    )
    qkv_got0 = flip(qkv_b0_grad, "section")
    rest_total0 = (rest_a0_grad.astype(f32) + rest_got0.astype(f32)).astype(bf16)
    gm_a, rest_total0 = pin(gm_a, rest_total0)
    reduced_in0 = scatter_late(rest_total0[:, :, :in_cols])
    gp_a0 = attend_back_one(*stay(qkv_a0), stay(*mixed_a0), gm_a)
    gp_a0, normal0, qkv_got0 = pin(gp_a0, normal0, qkv_got0)
    qkv_g_a0 = qkv_grads(slots, normal0, gp_a0, qkv0[0], norms0, qkv_got0)
    gp_a0, last, final, reduced_in0, rest_total0 = pin(gp_a0, qkv_g_a0[0], final, reduced_in0, rest_total0)
    act_got = flip(pick(final, middle), "section")
    reduced_out0 = scatter_late(rest_total0[:, :, in_cols:])
    reduced_qkv0 = scatter_late(last)
    stats = [
        [[pieces[0][1], pieces[1][1], pieces[0][2], pieces[1][2]] for pieces in pair]
        for pair in (((qkv_g_a0, qkv_g_b0), (rest_a0, rest_b0)), ((qkv_g_a1, qkv_g_b1), (rest_a1, rest_b1)))
    ]
    packed = []
    for grad_own, (qkv_t, in_t) in zip((grad1_low, grad2), stats):
        qkv_sum, in_sum = qkv_t[0] + qkv_t[1], in_t[0] + in_t[1]
        bias_sum = jnp.sum(grad_own.astype(f32), 0, keepdims=True)
        vectors = jnp.concatenate([qkv_sum[0:1], in_sum[0:1], qkv_sum[1:2], in_sum[1:2], bias_sum], 0)
        everywhere = vectors.reshape(5, n_tensor, n_dp, part).transpose(1, 2, 0, 3).reshape(n_tensor, n_dp, -1)
        halves_q = ordered(qkv_t[2][0].reshape(3, heads // 2), qkv_t[3][0].reshape(3, heads // 2))
        bias_q = jnp.concatenate(halves_q, 1).reshape(3, n_dp, part).transpose(1, 0, 2).reshape(n_dp, -1)
        bias_i = jnp.concatenate(ordered(in_t[2][0], in_t[3][0])).reshape(n_dp, -1)
        mine = jnp.concatenate([bias_q, bias_i], 1)
        only = (jnp.arange(n_tensor) == me)[:, None, None]
        packed.append(jnp.concatenate([everywhere, jnp.where(only, mine[None], 0.0)], 2))
    gp_a0, gp_b0, *packed = pin(gp_a0, gp_b0, *packed)

    def last_terms(half):
        return up_back((slots, slots), stay(gp_a0, gp_b0), stay(gi_a0, gi_b0), qkv0, in0, norms0, half)

    far = chip_sum(last_terms(1)).astype(bf16)
    far, gp_a0, gp_b0 = pin(far, gp_a0, gp_b0)
    near, beside = last_terms(0)
    near = (near, flip(beside, "tensor", 1))
    far = flip(far, "tensor", 2)
    total = pick(packed[0], packed[1]) + flip(pick(packed[1], packed[0]), "section")
    total = chosen(total, order, 0)
    small_sum = total[0::2] + flip(total[1::2], "tensor", 1)
    far, small_sum, reduced_qkv0, reduced_out0, act_got = pin(far, small_sum, reduced_qkv0, reduced_out0, act_got)
    near = near[0].astype(f32) + near[1].astype(f32)
    grad0 = input_back(h_own, grad1_low, near + far.astype(f32))
    grad_got = flip(pick(grad1_low, grad0.astype(bf16)), "section")

    total = small_sum
    total = total[0] + flip(total[1], "tensor", 2)
    sums = lax.psum_scatter(total, "dp", scatter_dimension=0) if not direct else None
    if direct:
        total = chosen(total, slots, 0)
        got = [lax.ppermute(total[hop], "dp", [(i, (i - hop) % n_dp) for i in range(n_dp)]) for hop in range(1, n_dp)]
        sums = sum(got, total[0])
    grad_got, sums = pin(grad_got, sums)

    activations = jnp.stack(ordered(pick(middle, final), act_got))
    input_grads = jnp.stack(ordered(pick(grad0, grad1_low.astype(f32)), grad_got.astype(f32)))

    def settled(one, two):
        got = flip(pick(two, one), "section")
        return [piece.astype(f32) for piece in ordered(pick(one, two), got)]

    rest_g = settled(jnp.concatenate([reduced_in0, reduced_out0], 1), reduced_rest1)
    qkv_g = settled(reduced_qkv0, reduced_qkv1)
    qkv_grad = jnp.concatenate([piece.reshape(-1, 3, heads // 2) for piece in qkv_g], 2)
    in_grad = jnp.concatenate([piece[:, :in_cols] for piece in rest_g], 1)
    dense_grad = jnp.concatenate([piece[:, in_cols : in_cols + heads // 2].T for piece in rest_g], 0)
    out_grad = jnp.concatenate([piece[:, in_cols + heads // 2 :].T for piece in rest_g], 0)

    return (
        activations[None],
        input_grads[None],
        qkv_grad[None],
        sums[5 * part : 8 * part].reshape(1, 3, part),
        dense_grad[None],
        in_grad[None],
        sums[8 * part :].reshape(1, -1),
        out_grad[None],
        sums[: 2 * part].reshape(1, 2, part),
        sums[2 * part : 4 * part].reshape(1, 2, part),
        jnp.stack([sums[4 * part : 5 * part]] * 2)[None],
    )


def solution(mesh):
    placed = (
        P("dp", "tensor", None),
        P("dp", "tensor", None),
        P("dp", None),
        P("section", "dp", None, "tensor"),
        P("section", None, ("tensor", "dp")),
        P("section", "tensor", "dp"),
        P("section", "dp", "tensor"),
        P("section", ("tensor", "dp")),
        P("section", "tensor", "dp"),
        P("section", None, ("tensor", "dp")),
        P("section", None, ("tensor", "dp")),
        P("section", None, ("tensor", "dp")),
    )
    return jax.shard_map(
        shards,
        mesh=mesh,
        in_specs=placed,
        out_specs=(
            P("section", "dp", "tensor", None),
            P("section", "dp", "tensor", None),
            P("section", "dp", None, "tensor"),
            P("section", None, ("tensor", "dp")),
            P("section", "tensor", "dp"),
            P("section", "dp", "tensor"),
            P("section", ("tensor", "dp")),
            P("section", "tensor", "dp"),
            P("section", None, ("tensor", "dp")),
            P("section", None, ("tensor", "dp")),
            P("section", None, ("tensor", "dp")),
        ),
        check_vma=False,
    )
```
